32 devices in a mesh: sub: 8 (over z, core), tile: 4 (over y, x).
Axes of the slice: x: 2, y: 2, z: 4, core: 2. Of those that a mesh axis runs over, the one named last changes fastest.
Arguments:
- load_current: float32 [8, 2, 256, 4096], P('sub', None, 'tile'), may hold values from -6 to 6
- diagonal: float32 [8, 2, 256, 4096], P('sub', None, 'tile')
- start_field: float32 [8, 2, 256, 4096], P('sub', None, 'tile'), may hold values from -4 to 4
- block_inverse: float32 [8, 16, 2, 256, 2, 256], P('sub')
- multipliers: float32 [8, 2, 256, 128], P('sub', None, 'tile'), may hold values from -6 to 6
- active_rows: int32 [8], replicated, may hold values from 64 to 256, as said below
- contact_peer: int32 [8, 8], replicated, may hold values from 0 to 7, as said below
- contact_len: int32 [8, 8], replicated, may hold values from 1 to 128, 256 in all within a row
- port_row: int32 [8, 16], P('sub'), may hold values from 0 to 255
- port_col: int32 [8, 16], P('sub'), may hold values from 0 to 3968
- port_current: float32 [8, 2, 16], P('sub'), may hold values from -16 to 16
Outputs:
- solution: float32 [8, 2, 256, 4096], P('sub', None, 'tile')
- next_multipliers: float32 [8, 2, 256, 128], P('sub', None, 'tile')
The draws below stay inside these ranges and needn't reach their ends.
Inputs may be any that keep to these rules, and one draw needn't show every extreme that they name: `active_rows`: at least one subdomain has all 256 lines active. `contact_peer`: a contact never names its own subdomain.
All inputs are finite; a program needn't handle non-finite values.
Results may differ from the reference program's by a relative error of at most 0.0003.
Values sent between devices are 32-bit elements; how exact they have to be, the bound alone decides.
No kernel may reach another device: no remote copies, remote signals or barrier semaphores. Data moves between devices by JAX's collectives and lax.ppermute only.
A program may use at most 128 MiB of HBM per device.

```python
import math
import jax
import jax.numpy as jnp
import numpy as np
from jax import lax

W = 4096
B = 256
IB = 128
NC = 8
NP = 16
PB = 128
SWEEPS = 3
ROWS = 256
SUBS = 8
NB = 16


def draw_active_rows(key, part):
    values = jax.random.randint(key, (SUBS,), ROWS // 4, ROWS + 1)
    chosen = jax.random.randint(jax.random.fold_in(key, 7), (), 0, SUBS)
    return jnp.where(jnp.arange(SUBS) == chosen, ROWS, values).astype(jnp.int32)


def draw_contact_peer(key, part):
    offset = jax.random.randint(key, (SUBS, NC), 1, SUBS)
    return ((jnp.arange(SUBS, dtype=jnp.int32)[:, None] + offset) % SUBS).astype(jnp.int32)


def draw_diagonal(key, part):
    first = jax.random.uniform(jax.random.fold_in(key, 1), (SUBS, 1, ROWS, W), jnp.float32, 4.5, 6.0)
    second = jnp.exp(jax.random.uniform(jax.random.fold_in(key, 2), (SUBS, 1, ROWS, W), jnp.float32, jnp.log(0.3), jnp.log(3.0)))
    return jnp.concatenate([first, second], axis=1)


def draw_block_inverse(key, part):
    shape = (SUBS, NB, 2, B, 2, B)
    comp_out = jnp.arange(2)[None, None, :, None, None, None]
    comp_in = jnp.arange(2)[None, None, None, None, :, None]
    node_out = jnp.arange(B)[None, None, None, :, None, None]
    node_in = jnp.arange(B)[None, None, None, None, None, :]
    unit = ((comp_out == comp_in) & (node_out == node_in)).astype(jnp.float32)
    noise = jax.random.normal(key, shape, jnp.float32)
    scale = 0.15
    return scale * (unit + 0.25 * noise / jnp.sqrt(2.0 * B))


def set_ends(result, stream_key, smallest, top_value):
    dims = result.shape
    index_at = [jax.random.randint(jax.random.fold_in(stream_key, axis), (), 0, dims[axis]) for axis in range(len(dims))]
    result = result.at[tuple(index_at)].set(smallest)
    longest = dims.index(max(dims))
    index_at[longest] = (index_at[longest] + 1) % dims[longest]
    return result.at[tuple(index_at)].set(top_value)


def block_scale(own_key, dims, split, smallest, high):
    def one(dim, blocks):
        heights = jax.random.uniform(jax.random.fold_in(jax.random.fold_in(own_key, 6), dim), (blocks,), jnp.float32, smallest / len(split), high / len(split))
        return jnp.repeat(jnp.exp(heights), dims[dim] // blocks).reshape((-1,) + (1,) * (len(dims) - dim - 1))

    factor_of = one(*split[0])
    for cut in split[1:]:
        factor_of = factor_of * one(*cut)
    return factor_of


def split_up(amount, total, reach, skew):
    loads = [(1 << 20) // math.isqrt(standing ** skew) + 1 for standing in range(2, amount + 1)]
    surplus, given = total - reach - (amount - 1), [1] * (amount - 1)
    while surplus > 0:
        candidates = [i for i in range(amount - 1) if given[i] < reach]
        whole, budget = sum([loads[i] for i in candidates]), surplus
        for i in candidates:
            more = min(reach - given[i], max(1, budget * loads[i] // whole), surplus)
            given[i] = given[i] + more
            surplus = surplus - more
    return np.array([reach] + given)


def ragged(stream_key, count, total, bound, skew):
    if count == 2:
        one = jax.random.randint(stream_key, (), max(1, total - bound), min(bound, total - 1) + 1)
        return jnp.stack([one, total - one])
    lengths = jnp.asarray(split_up(count, total, bound, skew), jnp.int32)
    twos = (count - 1) // 2
    donor, sink = lengths[1:1 + 2 * twos:2], lengths[2:2 + 2 * twos:2]
    room = jnp.minimum(donor - 1, bound - sink)
    passed = jax.random.randint(jax.random.fold_in(stream_key, 1), (twos,), 0, 1 << 20) % (room + 1)
    lengths = lengths.at[1:1 + 2 * twos:2].set(donor - passed).at[2:2 + 2 * twos:2].set(sink + passed)
    return lengths[jax.random.permutation(jax.random.fold_in(stream_key, 2), count)]


def bell_draw(rng, shape, deviation, reach, split=(), held_as=jnp.bfloat16):
    gain = block_scale(rng, shape, split, -0.22, 0.18) if split else 1.0
    array = jax.random.normal(rng, shape, jnp.float32) * deviation * gain
    return jnp.minimum(jnp.maximum(array, -reach), reach).astype(held_as)


def setup_inputs(seed: int = 0) -> dict:
    splits = jax.random.split(jax.random.key(seed), 12)
    return {
        "load_current": bell_draw(splits[0], (SUBS, 2, ROWS, W), 1.0, 6.0, ((0, 8), (2, 4)), jnp.float32),
        "diagonal": draw_diagonal(jax.random.fold_in(splits[11], 71), 0),
        "start_field": bell_draw(splits[2], (SUBS, 2, ROWS, W), 0.3, 4.0, ((0, 8), (2, 4)), jnp.float32),
        "block_inverse": draw_block_inverse(jax.random.fold_in(splits[11], 71), 0),
        "multipliers": bell_draw(splits[4], (SUBS, 2, ROWS, IB), 0.5, 6.0, ((0, 8), (2, 4)), jnp.float32),
        "active_rows": draw_active_rows(jax.random.fold_in(splits[11], 71), 0),
        "contact_peer": draw_contact_peer(jax.random.fold_in(splits[11], 71), 0),
        "contact_len": jax.vmap(lambda own: ragged(own, NC, ROWS, ROWS // 2, 2))(jax.random.split(splits[7], SUBS)).reshape((SUBS, NC)).astype(jnp.int32),
        "port_row": set_ends(jax.random.randint(splits[8], (SUBS, NP), 0, ROWS), jax.random.fold_in(splits[8], 1), 0, ROWS - 1).astype(jnp.int32),
        "port_col": set_ends(jax.random.randint(splits[9], (SUBS, NP), 0, W - PB + 1), jax.random.fold_in(splits[9], 1), 0, W - PB).astype(jnp.int32),
        "port_current": bell_draw(splits[10], (SUBS, 2, NP), 3.0, 16.0, ((0, 8),), jnp.float32),
    }


def contract(form, left, right):
    return jnp.einsum(form, left, right, precision=lax.Precision.HIGHEST)


def row_peers(contact_peer, contact_len, first_row, count):
    ends = jnp.cumsum(contact_len, axis=1).astype(jnp.int32)
    starts = ends - contact_len
    lines = first_row + jnp.arange(count, dtype=jnp.int32)
    inside = (lines[None, None, :] >= starts[:, :, None]) & (lines[None, None, :] < ends[:, :, None])
    return jnp.sum(jnp.where(inside, contact_peer[:, :, None], 0), axis=1).astype(jnp.int32)


def ports_source(load, prow, pcol, pcur, lines):
    width = load.shape[2]
    rows_hot = (prow[:, None] == lines[None, :]).astype(jnp.float32)
    columns = jnp.arange(width, dtype=jnp.int32)
    cols_hot = ((columns[None, :] >= pcol[:, None]) & (columns[None, :] < pcol[:, None] + PB)).astype(jnp.float32)
    weighted = pcur[:, :, None] * rows_hot[None]
    return load + contract('cpg,pj->cgj', weighted, cols_hot)


def operate_rows(extended, diag):
    middle = extended[:, 1:-1]
    sides = jnp.pad(middle, ((0, 0), (0, 0), (1, 1)))
    beside = extended[:, :-2] + extended[:, 2:] + sides[:, :, :-2] + sides[:, :, 2:]
    real = diag[0] * middle[0] - diag[1] * middle[1]
    imag = diag[0] * middle[1] + diag[1] * middle[0]
    return jnp.stack([real, imag]) - beside


def relax_lines(extended, source, diag, blocks, mask):
    middle = extended[:, 1:-1]
    resid = source - operate_rows(extended, diag)
    count, width = resid.shape[1], resid.shape[2]
    nblock, bsize = blocks.shape[0], blocks.shape[2]
    update = contract('ncidj,drnj->crni', blocks, resid.reshape(2, count, nblock, bsize)).reshape(2, count, width)
    return mask[None, :, None] * (middle + update)


def reference(load_current, diagonal, start_field, block_inverse, multipliers, active_rows, contact_peer, contact_len, port_row, port_col, port_current):
    peers = row_peers(contact_peer, contact_len, 0, ROWS)
    owners = jnp.arange(SUBS, dtype=jnp.int32)
    hot = (peers[:, None, :] == owners[None, :, None]).astype(jnp.float32)
    incoming = contract('sng,scgj->ncgj', hot, multipliers)
    lines = jnp.arange(ROWS, dtype=jnp.int32)

    def one_domain(items):
        load, diag, start, blocks, mult, inflow, active, prow, pcol, pcur = items
        source = ports_source(load, prow, pcol, pcur, lines)
        source = source.at[:, :, :IB].add(-mult)
        source = source.at[:, :, W - IB:].add(inflow)
        mask = ((lines >= 0) & (lines < active)).astype(jnp.float32)
        field = mask[None, :, None] * start
        for sweep in range(SWEEPS):
            extended = jnp.pad(field, ((0, 0), (1, 1), (0, 0)))
            field = relax_lines(extended, source, diag, blocks, mask)
        return field

    fields = lax.map(one_domain, (load_current, diagonal, start_field, block_inverse, multipliers, incoming, active_rows, port_row, port_col, port_current))
    far = fields[:, :, :, W - IB:]
    peer_end = contract('sng,ncgj->scgj', hot, far)
    return fields, multipliers + (fields[:, :, :, :IB] - peer_end)
```

```python
import functools

import jax
import jax.numpy as jnp
from jax import lax
from jax.experimental import pallas as pl
from jax.experimental.pallas import tpu as pltpu
from jax.sharding import PartitionSpec as P

IB = 128
PB = 128
SWEEPS = 3
LANES = 128
PAD = 8
SLOTS = 4
MIB = 1 << 20

VMEM_SPEC = pl.BlockSpec(memory_space=pltpu.VMEM)
SMEM_SPEC = pl.BlockSpec(memory_space=pltpu.SMEM)
ANY_SPEC = pl.BlockSpec(memory_space=pl.ANY)


def call(kernel, args, specs, outs, limit, scratch=(), flops=0, moved=0):
    return pl.pallas_call(
        kernel,
        out_shape=outs,
        in_specs=specs,
        out_specs=jax.tree.map(lambda _: VMEM_SPEC, outs),
        scratch_shapes=scratch,
        compiler_params=pltpu.CompilerParams(vmem_limit_bytes=limit),
        cost_estimate=pl.CostEstimate(flops=flops, bytes_accessed=moved, transcendentals=0),
    )(*args)


def held(shape, dtype=jnp.float32):
    return pltpu.VMEM(shape, dtype)


def line_peers(peer_ref, len_ref, s, lines):
    found = jnp.zeros(lines.shape, jnp.int32)
    start = jnp.int32(0)
    for c in range(peer_ref.shape[1]):
        end = start + len_ref[s, c]
        found = jnp.where((lines >= start) & (lines < end), peer_ref[s, c], found)
        start = end
    return found


def pick(hit, cells):
    return jnp.where(hit[None], cells, 0.0)


def split_halves(x):
    high = x.astype(jnp.bfloat16)
    return high, (x - high.astype(jnp.float32)).astype(jnp.bfloat16)


def weights_kernel(size, b_ref, hi_ref, lo_ref, buf, sem):
    nb = b_ref.shape[0]
    both = 2 * size
    parts = both // LANES

    def copy(k):
        return pltpu.make_async_copy(b_ref.at[k], buf.at[k % SLOTS], sem.at[k % SLOTS])

    for k in range(min(SLOTS - 1, nb)):
        copy(k).start()
    for k in range(nb):
        if k + SLOTS - 1 < nb:
            copy(k + SLOTS - 1).start()
        copy(k).wait()
        for q in range(parts):
            piece, comp = divmod(q, 2)
            rows = pl.ds(comp * size + piece * LANES, LANES)
            high, low = split_halves(buf[k % SLOTS, pl.ds(q, both, parts), :].T)
            hi_ref[k, rows, :] = high
            lo_ref[k, rows, :] = low


def split_weights(blocks):
    nb, _, size, _, _ = blocks.shape
    both = 2 * size
    parts = both // LANES
    flat = blocks.reshape(nb, 2, size, 2, size // LANES, LANES).transpose(0, 1, 2, 4, 3, 5)
    flat = flat.reshape(nb, both * parts, LANES)
    shape = (nb, both, both)
    return call(
        functools.partial(weights_kernel, size),
        (flat,),
        [ANY_SPEC],
        [held(shape, jnp.bfloat16)] * 2,
        10 * MIB,
        [pltpu.VMEM((SLOTS, both * parts, LANES), jnp.float32), pltpu.SemaphoreType.DMA((SLOTS,))],
        moved=nb * both * both * 8,
    )


def edges_kernel(start_ref, load_ref, diag_ref, one_ref, two_ref):
    rows = start_ref.shape[1]
    even = lax.rem(lax.axis_index("tile"), 2) == 0
    top, bottom = pl.ds(0, PAD), pl.ds(rows - PAD, PAD)
    row = lax.broadcasted_iota(jnp.int32, (PAD, start_ref.shape[2]), 0)
    for c in range(2):
        first = jnp.where(
            row < 3,
            start_ref[c, top, :],
            jnp.where(
                row < 5, pltpu.roll(load_ref[c, top, :], 3, 0), pltpu.roll(diag_ref[c, top, :], 5, 0)
            ),
        )
        last = jnp.where(
            row < 3,
            pltpu.roll(start_ref[c, bottom, :], 3, 0),
            jnp.where(
                row < 5,
                pltpu.roll(load_ref[c, bottom, :], 5, 0),
                pltpu.roll(diag_ref[c, bottom, :], 7, 0),
            ),
        )
        one_ref[c] = jnp.where(even, last, first)
        two_ref[c] = jnp.where(even, first, last)


def swaps(count):
    one = [(i, i ^ 1) for i in range(count)]
    two = [(i, ((i - 1) if i % 2 == 0 else (i + 1)) % count) for i in range(count)]
    return one, two


def swap_edges(one, two):
    first, second = swaps(lax.axis_size("tile"))
    return lax.ppermute(one, "tile", first), lax.ppermute(two, "tile", second)


def to_subs_kernel(tail, far, own_ref, other_ref, peer_ref, len_ref, *outs):
    count = peer_ref.shape[0]
    me = lax.axis_index("sub")
    partner = me + 1 - 2 * lax.rem(me, 2)
    shape = own_ref.shape[1:]
    rows = shape[0] - tail
    at = lax.broadcasted_iota(jnp.int32, shape, 0)
    at = jnp.where(at < rows + tail // 2, at, at - rows - tail)
    lines = at + lax.axis_index("tile") * rows
    own, other = own_ref[...], other_ref[...]
    if far:
        outs[-1][...] = pick(line_peers(peer_ref, len_ref, me, lines) == partner, other)
    else:
        of_own = line_peers(peer_ref, len_ref, me, lines)
        of_other = line_peers(peer_ref, len_ref, partner, lines)
        outs[-1][...] = pick(of_other == me, other)
    for step in range(1, count // 2):
        to = lax.rem(me + 2 * step, count)
        if far:
            wanted = line_peers(peer_ref, len_ref, to, lines)
            sent = pick(wanted == me, own) + pick(wanted == partner, other)
        else:
            sent = pick(of_own == to, own) + pick(of_other == to, other)
        outs[step - 1][...] = sent


def to_subs(cells, contact_peer, contact_len, tail, far):
    count = lax.axis_size("sub")
    other = lax.ppermute(cells, "sub", [(i, i ^ 1) for i in range(count)])
    outs = call(
        functools.partial(to_subs_kernel, tail, far),
        (cells, other, contact_peer, contact_len),
        [VMEM_SPEC, VMEM_SPEC, SMEM_SPEC, SMEM_SPEC],
        [held(cells.shape)] * (count // 2),
        4 * MIB,
    )
    got = [
        lax.ppermute(outs[step - 1], "sub", [(i, (i + 2 * step) % count) for i in range(count)])
        for step in range(1, count // 2)
    ]
    return got + [outs[-1]]


def line_mask(active_ref, shape, rows):
    at = lax.broadcasted_iota(jnp.int32, shape, 0) - PAD + lax.axis_index("tile") * rows
    return (at >= 0) & (at < active_ref[lax.axis_index("sub")])


def tiles_of(parts, c, k, size, last):
    def ref_of(b):
        for first, ref in parts:
            if first <= b < first + ref.shape[2] // size:
                return ref, (b - first) * size

    ref, at = ref_of(k)
    mid = ref[c, :, at : at + size]
    none = jnp.zeros((mid.shape[0], LANES), jnp.float32)
    left, right = none, none
    if k > 0:
        ref, at = ref_of(k - 1)
        left = ref[c, :, at + size - LANES : at + size]
    if k < last:
        ref, at = ref_of(k + 1)
        right = ref[c, :, at : at + LANES]
    return mid, jnp.concatenate([left, mid, right], axis=1)


def relax_block(parts, source, diag_ref, hi_ref, lo_ref, k, mask):
    size = hi_ref.shape[1] // 2
    last = hi_ref.shape[0] - 1
    mids, sums = [], []
    for c in range(2):
        mid, wide = tiles_of(parts, c, k, size, last)
        rows, width = wide.shape
        beside = (
            pltpu.roll(wide, 1, 1)[:, LANES : LANES + size]
            + pltpu.roll(wide, width - 1, 1)[:, LANES : LANES + size]
        )
        beside = beside + (pltpu.roll(mid, 1, 0) + pltpu.roll(mid, rows - 1, 0))
        mids.append(mid)
        sums.append(source(c) + beside)
    cols = slice(k * size, (k + 1) * size)
    d0, d1 = diag_ref[0, :, cols], diag_ref[1, :, cols]
    r0 = sums[0] - (d0 * mids[0] - d1 * mids[1])
    r1 = sums[1] - (d0 * mids[1] + d1 * mids[0])
    high, low = split_halves(jnp.concatenate([r0, r1], axis=1))
    rows = high.shape[0]
    z = jnp.dot(
        jnp.concatenate([high, low], axis=0), hi_ref[k], preferred_element_type=jnp.float32
    )
    z = (z[:rows] + z[rows:]) + jnp.dot(high, lo_ref[k], preferred_element_type=jnp.float32)
    return [
        jnp.where(mask, mids[c] + z[:, c * size : (c + 1) * size], 0.0) for c in range(2)
    ]


def stored_source(source_ref, k, size):
    return lambda c: source_ref[c, :, k * size : (k + 1) * size]


def first_kernel(
    upto, start_ref, load_ref, diag_ref, one_ref, two_ref, mult_ref, hi_ref, lo_ref,
    active_ref, prow_ref, pcol_ref, pcur_ref, src_ref, dg_ref, f1_ref, f0_ref,
):
    _, rows, width = load_ref.shape
    size = hi_ref.shape[1] // 2
    own = slice(PAD, PAD + rows)
    above, below = slice(0, PAD), slice(PAD + rows, 2 * PAD + rows)
    tile = lax.axis_index("tile")
    even = lax.rem(tile, 2) == 0
    active = active_ref[lax.axis_index("sub")]

    def masked(cells, first):
        line = lax.broadcasted_iota(jnp.int32, cells.shape, 0) + (first + tile * rows)
        return jnp.where((line >= 0) & (line < active), cells, 0.0)

    for c in range(2):
        one, two = one_ref[c], two_ref[c]
        up = jnp.where(even, two, one)
        down = jnp.where(even, one, two)
        f0_ref[c, own, :] = masked(start_ref[c], 0)
        f0_ref[c, above, :] = masked(pltpu.roll(up, 5, 0), -PAD)
        f0_ref[c, below, :] = masked(down, rows)
        src_ref[c, own, :] = load_ref[c]
        src_ref[c, above, :] = pltpu.roll(up, 3, 0)
        src_ref[c, below, :] = pltpu.roll(down, 5, 0)
        dg_ref[c, own, :] = diag_ref[c]
        dg_ref[c, above, :] = pltpu.roll(up, 1, 0)
        dg_ref[c, below, :] = pltpu.roll(down, 3, 0)
        src_ref[c, own, 0:IB] -= mult_ref[c, 0:rows, :]
        src_ref[c, above, 0:IB] -= mult_ref[c, rows:, :]
        src_ref[c, below, 0:IB] -= mult_ref[c, rows:, :]
    span = PB + LANES
    at_row = lax.broadcasted_iota(jnp.int32, (PAD, span), 0)
    at_col = lax.broadcasted_iota(jnp.int32, (PAD, span), 1)
    for p in range(prow_ref.shape[1]):
        row = prow_ref[0, p] - tile * rows + PAD
        col = pcol_ref[0, p]
        base = pl.multiple_of(jnp.minimum(col // LANES * LANES, width - span), LANES)

        @pl.when((row >= 0) & (row < rows + 2 * PAD))
        def _(p=p, row=row, col=col, base=base):
            first = pl.multiple_of(row // PAD * PAD, PAD)
            hit = (at_row == row - first) & (at_col >= col - base) & (at_col < col - base + PB)
            for c in range(2):
                where = (c, pl.ds(first, PAD), pl.ds(base, span))
                src_ref[where] = src_ref[where] + jnp.where(hit, pcur_ref[0, c, p], 0.0)

    mask = line_mask(active_ref, (rows + 2 * PAD, size), rows)
    for k in range(upto):
        new = relax_block(
            [(0, f0_ref)], stored_source(src_ref, k, size), dg_ref, hi_ref, lo_ref, k, mask
        )
        for c in range(2):
            f1_ref[c, :, k * size : (k + 1) * size] = new[c]


def far_kernel(
    count, f0_ref, f1_ref, src_ref, dg_ref, hi_ref, lo_ref, active_ref, *refs
):
    pieces, (f1e_ref, f2e_ref, f3e_ref, far_ref) = refs[:count], refs[count:]
    last = hi_ref.shape[0] - 1
    size = hi_ref.shape[1] // 2
    rows = far_ref.shape[1]
    mask = line_mask(active_ref, (rows + 2 * PAD, size), rows)
    into = []
    for c in range(2):
        piece = pieces[0][c]
        for other in pieces[1:]:
            piece = piece + other[c]
        edge = piece[rows:]
        ends = jnp.concatenate([edge, piece[:rows], edge], axis=0)
        into.append(jnp.concatenate([jnp.zeros((rows + 2 * PAD, size - IB), jnp.float32), ends], axis=1))
    end = stored_source(src_ref, last, size)

    def with_incoming(c):
        return end(c) + into[c]

    new = relax_block([(0, f0_ref)], with_incoming, dg_ref, hi_ref, lo_ref, last, mask)
    for c in range(2):
        f1e_ref[c] = new[c]
    f1 = [(last, f1e_ref), (0, f1_ref)]
    for k, source in ((last, with_incoming), (last - 1, stored_source(src_ref, last - 1, size))):
        new = relax_block(f1, source, dg_ref, hi_ref, lo_ref, k, mask)
        for c in range(2):
            f2e_ref[c, :, (k - last + 1) * size : (k - last + 2) * size] = new[c]
    new = relax_block([(last - 1, f2e_ref)], with_incoming, dg_ref, hi_ref, lo_ref, last, mask)
    for c in range(2):
        f3e_ref[c] = new[c][PAD : PAD + rows]
        far_ref[c] = new[c][PAD : PAD + rows, size - IB :]


def middle_kernel(f1_ref, src_ref, dg_ref, hi_ref, lo_ref, active_ref, f2_ref):
    size = hi_ref.shape[1] // 2
    mask = line_mask(active_ref, (f2_ref.shape[1], size), f2_ref.shape[1] - 2 * PAD)
    for k in range(f2_ref.shape[2] // size):
        new = relax_block(
            [(0, f1_ref)], stored_source(src_ref, k, size), dg_ref, hi_ref, lo_ref, k, mask
        )
        for c in range(2):
            f2_ref[c, :, k * size : (k + 1) * size] = new[c]


def last_kernel(f2_ref, f2e_ref, f3e_ref, src_ref, dg_ref, hi_ref, lo_ref, active_ref, out_ref, near_ref):
    size = hi_ref.shape[1] // 2
    last = hi_ref.shape[0] - 1
    rows = out_ref.shape[1]
    mask = line_mask(active_ref, (rows + 2 * PAD, size), rows)
    f2 = [(last - 1, f2e_ref), (0, f2_ref)]
    for k in range(last):
        new = relax_block(f2, stored_source(src_ref, k, size), dg_ref, hi_ref, lo_ref, k, mask)
        for c in range(2):
            out_ref[c, :, k * size : (k + 1) * size] = new[c][PAD : PAD + rows]
            if k == 0:
                near_ref[c] = new[c][PAD : PAD + rows, :IB]
    for c in range(2):
        out_ref[c, :, last * size :] = f3e_ref[c]


def per_device(
    load_current,
    diagonal,
    start_field,
    block_inverse,
    multipliers,
    active_rows,
    contact_peer,
    contact_len,
    port_row,
    port_col,
    port_current,
):
    load, diag, start, mult = load_current[0], diagonal[0], start_field[0], multipliers[0]
    _, rows, width = load.shape
    nb, _, size, _, _ = block_inverse.shape[1:]
    high = rows + 2 * PAD
    step = 6 * high * (2 * size) ** 2
    even = lax.axis_index("tile") % 2 == 0

    top, bottom = mult[:, :PAD], mult[:, rows - PAD :]
    one, two = swap_edges(jnp.where(even, bottom, top), jnp.where(even, top, bottom))
    up, down = jnp.where(even, two, one), jnp.where(even, one, two)
    tail = jnp.concatenate([down[:, : PAD // 2], up[:, PAD // 2 :]], axis=1)
    lines_mult = jnp.concatenate([mult, tail], axis=1)

    edge = jax.ShapeDtypeStruct((2, PAD, width), jnp.float32)
    one, two = swap_edges(
        *call(edges_kernel, (start, load, diag), [VMEM_SPEC] * 3, [edge] * 2, 16 * MIB)
    )
    incoming = to_subs(lines_mult, contact_peer, contact_len, PAD, False)
    hi, lo = split_weights(block_inverse[0])

    whole = held((2, high, width))
    src, dg, f1, f0 = call(
        functools.partial(first_kernel, nb - 1),
        (start, load, diag, one, two, lines_mult, hi, lo, active_rows, port_row, port_col, port_current),
        [VMEM_SPEC] * 8 + [SMEM_SPEC] * 4,
        [whole, whole, held((2, high, (nb - 1) * size)), whole],
        16 * MIB,
        flops=step * (nb - 1),
    )
    f1e, f2e, f3e, far = call(
        functools.partial(far_kernel, len(incoming)),
        (f0, f1, src, dg, hi, lo, active_rows, *incoming),
        [VMEM_SPEC] * 6 + [SMEM_SPEC] + [VMEM_SPEC] * len(incoming),
        [held((2, high, size)), held((2, high, 2 * size)), held((2, rows, size)), held((2, rows, IB))],
        8 * MIB,
        flops=step * 4,
    )
    ends = to_subs(far, contact_peer, contact_len, 0, True)
    f2 = call(
        middle_kernel,
        (f1, src, dg, hi, lo, active_rows),
        [VMEM_SPEC] * 5 + [SMEM_SPEC],
        held((2, high, (nb - 2) * size)),
        8 * MIB,
        flops=step * (nb - 2),
    )
    solved, near = call(
        last_kernel,
        (f2, f2e, f3e, src, dg, hi, lo, active_rows),
        [VMEM_SPEC] * 7 + [SMEM_SPEC],
        [jax.ShapeDtypeStruct((2, rows, width), jnp.float32), held((2, rows, IB))],
        8 * MIB,
        flops=step * (nb - 1),
    )
    updated = mult + (near - sum(ends))
    return (solved[None], updated[None])


def solution(mesh):
    lines = P("sub", None, "tile", None)
    in_specs = (
        lines,
        lines,
        lines,
        P("sub", None, None, None, None, None),
        lines,
        P(),
        P(),
        P(),
        P("sub", None),
        P("sub", None),
        P("sub", None, None),
    )
    return jax.shard_map(
        per_device, mesh=mesh, in_specs=in_specs, out_specs=(lines, lines), check_vma=False
    )
```

```python
import functools

import jax
import jax.numpy as jnp
from jax import lax
from jax.experimental import pallas as pl
from jax.experimental.pallas import tpu as pltpu
from jax.sharding import PartitionSpec as P

IB = 128
PB = 128
SWEEPS = 3
LANES = 128
PAD = 8
FILL = 6
MIB = 1 << 20

VMEM_SPEC = pl.BlockSpec(memory_space=pltpu.VMEM)
SMEM_SPEC = pl.BlockSpec(memory_space=pltpu.SMEM)
ANY_SPEC = pl.BlockSpec(memory_space=pl.ANY)


def call(kernel, args, specs, outs, limit, scratch=(), flops=0, moved=0, out_specs=None):
    return pl.pallas_call(
        kernel,
        out_shape=outs,
        in_specs=specs,
        out_specs=out_specs or jax.tree.map(lambda _: VMEM_SPEC, outs),
        scratch_shapes=scratch,
        compiler_params=pltpu.CompilerParams(vmem_limit_bytes=limit),
        cost_estimate=pl.CostEstimate(flops=flops, bytes_accessed=moved, transcendentals=0),
    )(*args)


def held(shape, dtype=jnp.float32):
    return pltpu.VMEM(shape, dtype)


def line_peers(peer_ref, len_ref, s, lines):
    found = jnp.zeros(lines.shape, jnp.int32)
    start = jnp.int32(0)
    for c in range(peer_ref.shape[1]):
        end = start + len_ref[s, c]
        found = jnp.where((lines >= start) & (lines < end), peer_ref[s, c], found)
        start = end
    return found


def pick(hit, cells):
    return jnp.where(hit[None], cells, 0.0)


def split_halves(x):
    high = x.astype(jnp.bfloat16)
    return high, (x - high.astype(jnp.float32)).astype(jnp.bfloat16)


def weights_kernel(size, b_ref, hi_ref, lo_ref):
    both = 2 * size
    parts = both // LANES
    for k in range(b_ref.shape[0]):
        for q in range(parts):
            piece, comp = divmod(q, 2)
            rows = pl.ds(comp * size + piece * LANES, LANES)
            high, low = split_halves(b_ref[k, pl.ds(q, both, parts), :].T)
            hi_ref[k, rows, :] = high
            lo_ref[k, rows, :] = low


def split_weights(blocks):
    nb, _, size, _, _ = blocks.shape
    both = 2 * size
    parts = both // LANES
    flat = blocks.reshape(nb, 2, size, 2, size // LANES, LANES).transpose(0, 1, 2, 4, 3, 5)
    flat = flat.reshape(nb, both * parts, LANES)
    shape = (nb, both, both)
    return call(
        functools.partial(weights_kernel, size),
        (pltpu.with_memory_space_constraint(flat, pltpu.VMEM),),
        [VMEM_SPEC],
        [held(shape, jnp.bfloat16)] * 2,
        2 * MIB,
        moved=nb * both * both * 8,
    )


def edge_lines(start, load, diag, top):
    rows = load.shape[1]
    field = slice(0, 3) if top else slice(rows - 3, rows)
    other = slice(0, 2) if top else slice(rows - 2, rows)
    parts = [start[:, field], load[:, other], diag[:, other], diag[:, :1]]
    return jnp.concatenate(parts, axis=1)


def lines_kernel(mult_ref, one_ref, two_ref, out_ref):
    rows = mult_ref.shape[1]
    even = lax.rem(lax.axis_index("tile"), 2) == 0
    low = lax.broadcasted_iota(jnp.int32, (PAD, IB), 0) < PAD // 2
    for c in range(2):
        out_ref[c, :rows] = mult_ref[c]
        out_ref[c, rows:] = jnp.where(low == even, one_ref[c], two_ref[c])


def swaps(count):
    one = [(i, i ^ 1) for i in range(count)]
    two = [(i, ((i - 1) if i % 2 == 0 else (i + 1)) % count) for i in range(count)]
    return one, two


def swap_edges(one, two):
    first, second = swaps(lax.axis_size("tile"))
    return lax.ppermute(one, "tile", first), lax.ppermute(two, "tile", second)


def to_subs_kernel(tail, far, own_ref, other_ref, peer_ref, len_ref, *outs):
    count = peer_ref.shape[0]
    me = lax.axis_index("sub")
    partner = me + 1 - 2 * lax.rem(me, 2)
    shape = own_ref.shape[1:]
    rows = shape[0] - tail
    at = lax.broadcasted_iota(jnp.int32, shape, 0)
    at = jnp.where(at < rows + tail // 2, at, at - rows - tail)
    lines = at + lax.axis_index("tile") * rows
    own, other = own_ref[...], other_ref[...]
    if far:
        outs[-1][...] = pick(line_peers(peer_ref, len_ref, me, lines) == partner, other)
    else:
        of_own = line_peers(peer_ref, len_ref, me, lines)
        of_other = line_peers(peer_ref, len_ref, partner, lines)
        outs[-1][...] = pick(of_other == me, other)
    for step in range(1, count // 2):
        to = lax.rem(me + 2 * step, count)
        if far:
            wanted = line_peers(peer_ref, len_ref, to, lines)
            sent = pick(wanted == me, own) + pick(wanted == partner, other)
        else:
            sent = pick(of_own == to, own) + pick(of_other == to, other)
        outs[step - 1][...] = sent


def to_subs(cells, contact_peer, contact_len, tail, far):
    count = lax.axis_size("sub")
    other = lax.ppermute(cells, "sub", [(i, i ^ 1) for i in range(count)])
    outs = call(
        functools.partial(to_subs_kernel, tail, far),
        (cells, other, contact_peer, contact_len),
        [VMEM_SPEC, VMEM_SPEC, SMEM_SPEC, SMEM_SPEC],
        [held(cells.shape)] * (count // 2),
        4 * MIB,
    )
    got = [
        lax.ppermute(outs[step - 1], "sub", [(i, (i + 2 * step) % count) for i in range(count)])
        for step in range(1, count // 2)
    ]
    return got + [outs[-1]]


def line_mask(active_ref, shape, rows):
    at = lax.broadcasted_iota(jnp.int32, shape, 0) - PAD + lax.axis_index("tile") * rows
    return (at >= 0) & (at < active_ref[lax.axis_index("sub")])


def tiles_of(parts, c, k, size, last):
    def ref_of(b):
        for first, ref in parts:
            if first <= b < first + ref.shape[2] // size:
                return ref, (b - first) * size

    ref, at = ref_of(k)
    mid = ref[c, :, at : at + size]
    none = jnp.zeros((mid.shape[0], LANES), jnp.float32)
    left, right = none, none
    if k > 0:
        ref, at = ref_of(k - 1)
        left = ref[c, :, at + size - LANES : at + size]
    if k < last:
        ref, at = ref_of(k + 1)
        right = ref[c, :, at : at + LANES]
    return mid, jnp.concatenate([left, mid, right], axis=1)


def relax_block(parts, source, diag_ref, hi_ref, lo_ref, k, mask):
    size = hi_ref.shape[1] // 2
    last = hi_ref.shape[0] - 1
    mids, sums = [], []
    for c in range(2):
        mid, wide = tiles_of(parts, c, k, size, last)
        rows, width = wide.shape
        beside = (
            pltpu.roll(wide, 1, 1)[:, LANES : LANES + size]
            + pltpu.roll(wide, width - 1, 1)[:, LANES : LANES + size]
        )
        beside = beside + (pltpu.roll(mid, 1, 0) + pltpu.roll(mid, rows - 1, 0))
        mids.append(mid)
        sums.append(source(c) + beside)
    cols = slice(k * size, (k + 1) * size)
    d0, d1 = diag_ref[0, :, cols], diag_ref[1, :, cols]
    r0 = sums[0] - (d0 * mids[0] - d1 * mids[1])
    r1 = sums[1] - (d0 * mids[1] + d1 * mids[0])
    high, low = split_halves(jnp.concatenate([r0, r1], axis=1))
    rows = high.shape[0]
    z = jnp.dot(
        jnp.concatenate([high, low], axis=0), hi_ref[k], preferred_element_type=jnp.float32
    )
    z = (z[:rows] + z[rows:]) + jnp.dot(high, lo_ref[k], preferred_element_type=jnp.float32)
    return [
        jnp.where(mask, mids[c] + z[:, c * size : (c + 1) * size], 0.0) for c in range(2)
    ]


def stored_source(source_ref, k, size):
    return lambda c: source_ref[c, :, k * size : (k + 1) * size]


def first_kernel(
    upto, start_ref, load_ref, diag_ref, one_ref, two_ref, mult_ref, hi_ref, lo_ref,
    active_ref, prow_ref, pcol_ref, pcur_ref, src_ref, dg_ref, f1_ref, f0_ref,
):
    _, rows, width = load_ref.shape
    size = hi_ref.shape[1] // 2
    own = slice(PAD, PAD + rows)
    above, below = slice(0, PAD), slice(PAD + rows, 2 * PAD + rows)
    tile = lax.axis_index("tile")
    even = lax.rem(tile, 2) == 0
    active = active_ref[lax.axis_index("sub")]

    def masked(cells, first):
        line = lax.broadcasted_iota(jnp.int32, cells.shape, 0) + (first + tile * rows)
        return jnp.where((line >= 0) & (line < active), cells, 0.0)

    for c in range(2):
        one, two = one_ref[c], two_ref[c]
        up = jnp.where(even, two, one)
        down = jnp.where(even, one, two)
        f0_ref[c, own, :] = masked(start_ref[c], 0)
        f0_ref[c, above, :] = masked(pltpu.roll(up, 5, 0), -PAD)
        f0_ref[c, below, :] = masked(down, rows)
        src_ref[c, own, :] = load_ref[c]
        src_ref[c, above, :] = pltpu.roll(up, 3, 0)
        src_ref[c, below, :] = pltpu.roll(down, 5, 0)
        dg_ref[c, own, :] = diag_ref[c]
        dg_ref[c, above, :] = pltpu.roll(up, 1, 0)
        dg_ref[c, below, :] = pltpu.roll(down, 3, 0)
        src_ref[c, own, 0:IB] -= mult_ref[c, 0:rows, :]
        src_ref[c, above, 0:IB] -= mult_ref[c, rows:, :]
        src_ref[c, below, 0:IB] -= mult_ref[c, rows:, :]
    span = PB + LANES
    at_row = lax.broadcasted_iota(jnp.int32, (PAD, span), 0)
    at_col = lax.broadcasted_iota(jnp.int32, (PAD, span), 1)
    for p in range(prow_ref.shape[1]):
        row = prow_ref[0, p] - tile * rows + PAD
        col = pcol_ref[0, p]
        base = pl.multiple_of(jnp.minimum(col // LANES * LANES, width - span), LANES)

        @pl.when((row >= 0) & (row < rows + 2 * PAD))
        def _(p=p, row=row, col=col, base=base):
            first = pl.multiple_of(row // PAD * PAD, PAD)
            hit = (at_row == row - first) & (at_col >= col - base) & (at_col < col - base + PB)
            for c in range(2):
                where = (c, pl.ds(first, PAD), pl.ds(base, span))
                src_ref[where] = src_ref[where] + jnp.where(hit, pcur_ref[0, c, p], 0.0)

    mask = line_mask(active_ref, (rows + 2 * PAD, size), rows)
    for k in range(upto):
        new = relax_block(
            [(0, f0_ref)], stored_source(src_ref, k, size), dg_ref, hi_ref, lo_ref, k, mask
        )
        for c in range(2):
            f1_ref[c, :, k * size : (k + 1) * size] = new[c]


def far_kernel(
    count, f0_ref, f1_ref, src_ref, dg_ref, hi_ref, lo_ref, active_ref, *refs
):
    pieces, (f1e_ref, f2s_ref, f2e_ref, f3e_ref, far_ref) = refs[:count], refs[count:]
    last = hi_ref.shape[0] - 1
    size = hi_ref.shape[1] // 2
    rows = far_ref.shape[1]
    mask = line_mask(active_ref, (rows + 2 * PAD, size), rows)
    into = []
    for c in range(2):
        piece = pieces[0][c]
        for other in pieces[1:]:
            piece = piece + other[c]
        edge = piece[rows:]
        ends = jnp.concatenate([edge, piece[:rows], edge], axis=0)
        into.append(jnp.concatenate([jnp.zeros((rows + 2 * PAD, size - IB), jnp.float32), ends], axis=1))
    end = stored_source(src_ref, last, size)

    def with_incoming(c):
        return end(c) + into[c]

    new = relax_block([(0, f0_ref)], with_incoming, dg_ref, hi_ref, lo_ref, last, mask)
    for c in range(2):
        f1e_ref[c] = new[c]
    f1 = [(last, f1e_ref), (0, f1_ref)]
    fill = f2s_ref.shape[2] // size

    def beside(k):
        new = relax_block([(0, f1_ref)], stored_source(src_ref, k, size), dg_ref, hi_ref, lo_ref, k, mask)
        for c in range(2):
            f2s_ref[c, :, k * size : (k + 1) * size] = new[c]

    for k in range(fill // 2):
        beside(k)
    for k, source in ((last, with_incoming), (last - 1, stored_source(src_ref, last - 1, size))):
        new = relax_block(f1, source, dg_ref, hi_ref, lo_ref, k, mask)
        for c in range(2):
            f2e_ref[c, :, (k - last + 1) * size : (k - last + 2) * size] = new[c]
    for k in range(fill // 2, fill):
        beside(k)
    new = relax_block([(last - 1, f2e_ref)], with_incoming, dg_ref, hi_ref, lo_ref, last, mask)
    for c in range(2):
        f3e_ref[c] = new[c][PAD : PAD + rows]
        far_ref[c] = new[c][PAD : PAD + rows, size - IB :]


def middle_kernel(f1_ref, src_ref, dg_ref, hi_ref, lo_ref, active_ref, f2_ref):
    size = hi_ref.shape[1] // 2
    mask = line_mask(active_ref, (f2_ref.shape[1], size), f2_ref.shape[1] - 2 * PAD)
    for i in range(f2_ref.shape[2] // size):
        k = i + FILL
        new = relax_block(
            [(0, f1_ref)], stored_source(src_ref, k, size), dg_ref, hi_ref, lo_ref, k, mask
        )
        for c in range(2):
            f2_ref[c, :, i * size : (i + 1) * size] = new[c]


def last_kernel(
    f2s_ref, f2_ref, f2e_ref, f3e_ref, src_ref, dg_ref, hi_ref, lo_ref, active_ref, out_ref, near_ref,
    held_ref, sem,
):
    size = hi_ref.shape[1] // 2

    def copy(k):
        cols = pl.ds(k * size, size)
        return pltpu.make_async_copy(held_ref.at[:, :, cols], out_ref.at[:, :, cols], sem.at[k])

    last = hi_ref.shape[0] - 1
    rows = out_ref.shape[1]
    mask = line_mask(active_ref, (rows + 2 * PAD, size), rows)
    f2 = [(last - 1, f2e_ref), (FILL, f2_ref), (0, f2s_ref)]
    for c in range(2):
        held_ref[c, :, last * size :] = f3e_ref[c]
    copy(last).start()
    for k in range(last):
        new = relax_block(f2, stored_source(src_ref, k, size), dg_ref, hi_ref, lo_ref, k, mask)
        for c in range(2):
            held_ref[c, :, k * size : (k + 1) * size] = new[c][PAD : PAD + rows]
            if k == 0:
                near_ref[c] = new[c][PAD : PAD + rows, :IB]
        copy(k).start()
    for k in range(last + 1):
        copy(k).wait()


def per_device(
    load_current,
    diagonal,
    start_field,
    block_inverse,
    multipliers,
    active_rows,
    contact_peer,
    contact_len,
    port_row,
    port_col,
    port_current,
):
    load, diag, start, mult = load_current[0], diagonal[0], start_field[0], multipliers[0]
    _, rows, width = load.shape
    nb, _, size, _, _ = block_inverse.shape[1:]
    high = rows + 2 * PAD
    step = 6 * high * (2 * size) ** 2
    even = lax.axis_index("tile") % 2 == 0

    top, bottom = mult[:, :PAD], mult[:, rows - PAD :]
    ends = swap_edges(jnp.where(even, bottom, top), jnp.where(even, top, bottom))
    first = edge_lines(start, load, diag, True)
    last = edge_lines(start, load, diag, False)
    one, two = swap_edges(jnp.where(even, last, first), jnp.where(even, first, last))
    lines_mult = call(
        lines_kernel,
        (mult, *ends),
        [VMEM_SPEC] * 3,
        held((2, rows + PAD, IB)),
        2 * MIB,
        flops=4 * 10**10,
        moved=10**8,
    )
    incoming = to_subs(lines_mult, contact_peer, contact_len, PAD, False)
    hi, lo = split_weights(block_inverse[0])

    whole = held((2, high, width))
    src, dg, f1, f0 = call(
        functools.partial(first_kernel, nb - 1),
        (start, load, diag, one, two, lines_mult, hi, lo, active_rows, port_row, port_col, port_current),
        [VMEM_SPEC] * 8 + [SMEM_SPEC] * 4,
        [whole, whole, held((2, high, (nb - 1) * size)), whole],
        4 * MIB,
        flops=step * (nb - 1),
    )
    f1e, f2s, f2e, f3e, far = call(
        functools.partial(far_kernel, len(incoming)),
        (f0, f1, src, dg, hi, lo, active_rows, *incoming),
        [VMEM_SPEC] * 6 + [SMEM_SPEC] + [VMEM_SPEC] * len(incoming),
        [held((2, high, size)), held((2, high, FILL * size)), held((2, high, 2 * size)), held((2, rows, size)), held((2, rows, IB))],
        4 * MIB,
        flops=step * (4 + FILL),
    )
    ends = to_subs(far, contact_peer, contact_len, 0, True)
    f2 = call(
        middle_kernel,
        (f1, src, dg, hi, lo, active_rows),
        [VMEM_SPEC] * 5 + [SMEM_SPEC],
        held((2, high, (nb - 2 - FILL) * size)),
        4 * MIB,
        flops=step * (nb - 2 - FILL),
    )
    solved, near = call(
        last_kernel,
        (f2s, f2, f2e, f3e, src, dg, hi, lo, active_rows),
        [VMEM_SPEC] * 8 + [SMEM_SPEC],
        [jax.ShapeDtypeStruct((2, rows, width), jnp.float32), held((2, rows, IB))],
        4 * MIB + 8 * rows * width,
        [pltpu.VMEM((2, rows, width), jnp.float32), pltpu.SemaphoreType.DMA((nb,))],
        flops=step * (nb - 1),
        out_specs=[ANY_SPEC, VMEM_SPEC],
    )
    updated = mult + (near - sum(ends))
    return (solved[None], updated[None])


def solution(mesh):
    lines = P("sub", None, "tile", None)
    in_specs = (
        lines,
        lines,
        lines,
        P("sub", None, None, None, None, None),
        lines,
        P(),
        P(),
        P(),
        P("sub", None),
        P("sub", None),
        P("sub", None, None),
    )
    return jax.shard_map(
        per_device, mesh=mesh, in_specs=in_specs, out_specs=(lines, lines), check_vma=False
    )
```

```python
import functools

import jax
import jax.numpy as jnp
from jax import lax
from jax.experimental import pallas as pl
from jax.experimental.pallas import tpu as pltpu
from jax.sharding import PartitionSpec as P

IB = 128
PB = 128
SWEEPS = 3
LANES = 128
PAD = 8
FILL = 6
MIB = 1 << 20

VMEM_SPEC = pl.BlockSpec(memory_space=pltpu.VMEM)
SMEM_SPEC = pl.BlockSpec(memory_space=pltpu.SMEM)
ANY_SPEC = pl.BlockSpec(memory_space=pl.ANY)


def call(kernel, args, specs, outs, limit, scratch=(), flops=0, moved=0, out_specs=None):
    return pl.pallas_call(
        kernel,
        out_shape=outs,
        in_specs=specs,
        out_specs=out_specs or jax.tree.map(lambda _: VMEM_SPEC, outs),
        scratch_shapes=scratch,
        compiler_params=pltpu.CompilerParams(vmem_limit_bytes=limit),
        cost_estimate=pl.CostEstimate(flops=flops, bytes_accessed=moved, transcendentals=0),
    )(*args)


def held(shape, dtype=jnp.float32):
    return pltpu.VMEM(shape, dtype)


def line_peers(peer_ref, len_ref, s, lines):
    found = jnp.zeros(lines.shape, jnp.int32)
    start = jnp.int32(0)
    for c in range(peer_ref.shape[1]):
        end = start + len_ref[s, c]
        found = jnp.where((lines >= start) & (lines < end), peer_ref[s, c], found)
        start = end
    return found


def pick(hit, cells):
    return jnp.where(hit[None], cells, 0.0)


def split_halves(x):
    high = x.astype(jnp.bfloat16)
    return high, (x - high.astype(jnp.float32)).astype(jnp.bfloat16)


def weights_kernel(size, b_ref, hi_ref, lo_ref):
    both = 2 * size
    parts = both // LANES
    for k in range(b_ref.shape[0]):
        for q in range(parts):
            piece, comp = divmod(q, 2)
            rows = pl.ds(comp * size + piece * LANES, LANES)
            high, low = split_halves(b_ref[k, pl.ds(q, both, parts), :].T)
            hi_ref[k, rows, :] = high
            lo_ref[k, rows, :] = low


def split_weights(blocks):
    nb, _, size, _, _ = blocks.shape
    both = 2 * size
    parts = both // LANES
    flat = blocks.reshape(nb, 2, size, 2, size // LANES, LANES).transpose(0, 1, 2, 4, 3, 5)
    flat = flat.reshape(nb, both * parts, LANES)
    shape = (nb, both, both)
    return call(
        functools.partial(weights_kernel, size),
        (pltpu.with_memory_space_constraint(flat, pltpu.VMEM),),
        [VMEM_SPEC],
        [held(shape, jnp.bfloat16)] * 2,
        2 * MIB,
        moved=nb * both * both * 8,
    )


def edges_kernel(start_hbm, load_hbm, diag_hbm, mult_ref, m1_ref, m2_ref, one_ref, two_ref, buf, sem):
    rows = start_hbm.shape[1]
    even = lax.rem(lax.axis_index("tile"), 2) == 0
    ends = (pl.ds(0, PAD), pl.ds(rows - PAD, PAD))
    copies = [
        pltpu.make_async_copy(ref.at[:, ends[e]], buf.at[i, e], sem.at[i, e])
        for i, ref in enumerate((start_hbm, load_hbm, diag_hbm))
        for e in range(2)
    ]
    for copy in copies:
        copy.start()
    for c in range(2):
        first, last = mult_ref[c, ends[0]], mult_ref[c, ends[1]]
        m1_ref[c] = jnp.where(even, last, first)
        m2_ref[c] = jnp.where(even, first, last)
    for copy in copies:
        copy.wait()
    row = lax.broadcasted_iota(jnp.int32, one_ref.shape[1:], 0)

    def lines(c, e, turns):
        field, load, diag = (pltpu.roll(buf[i, e, c], t, 0) if t else buf[i, e, c] for i, t in enumerate(turns))
        return jnp.where(row < 3, field, jnp.where(row < 5, load, diag))

    for c in range(2):
        first, last = lines(c, 0, (0, 3, 5)), lines(c, 1, (3, 5, 7))
        one_ref[c] = jnp.where(even, last, first)
        two_ref[c] = jnp.where(even, first, last)


def pass_kernel(a_ref, b_ref, x_ref, y_ref):
    x_ref[...] = a_ref[...]
    y_ref[...] = b_ref[...]


def lines_kernel(mult_ref, one_ref, two_ref, out_ref):
    rows = mult_ref.shape[1]
    even = lax.rem(lax.axis_index("tile"), 2) == 0
    low = lax.broadcasted_iota(jnp.int32, (PAD, IB), 0) < PAD // 2
    for c in range(2):
        out_ref[c, :rows] = mult_ref[c]
        out_ref[c, rows:] = jnp.where(low == even, one_ref[c], two_ref[c])


def swaps(count):
    one = [(i, i ^ 1) for i in range(count)]
    two = [(i, ((i - 1) if i % 2 == 0 else (i + 1)) % count) for i in range(count)]
    return one, two


def swap_edges(one, two):
    first, second = swaps(lax.axis_size("tile"))
    return lax.ppermute(one, "tile", first), lax.ppermute(two, "tile", second)


def to_subs_kernel(tail, far, own_ref, other_ref, peer_ref, len_ref, *outs):
    count = peer_ref.shape[0]
    me = lax.axis_index("sub")
    partner = me + 1 - 2 * lax.rem(me, 2)
    shape = own_ref.shape[1:]
    rows = shape[0] - tail
    at = lax.broadcasted_iota(jnp.int32, shape, 0)
    at = jnp.where(at < rows + tail // 2, at, at - rows - tail)
    lines = at + lax.axis_index("tile") * rows
    own, other = own_ref[...], other_ref[...]
    if far:
        outs[-1][...] = pick(line_peers(peer_ref, len_ref, me, lines) == partner, other)
    else:
        of_own = line_peers(peer_ref, len_ref, me, lines)
        of_other = line_peers(peer_ref, len_ref, partner, lines)
        outs[-1][...] = pick(of_other == me, other)
    for step in range(1, count // 2):
        to = lax.rem(me + 2 * step, count)
        if far:
            wanted = line_peers(peer_ref, len_ref, to, lines)
            sent = pick(wanted == me, own) + pick(wanted == partner, other)
        else:
            sent = pick(of_own == to, own) + pick(of_other == to, other)
        outs[step - 1][...] = sent


def to_subs(cells, contact_peer, contact_len, tail, far):
    count = lax.axis_size("sub")
    other = lax.ppermute(cells, "sub", [(i, i ^ 1) for i in range(count)])
    outs = call(
        functools.partial(to_subs_kernel, tail, far),
        (cells, other, contact_peer, contact_len),
        [VMEM_SPEC, VMEM_SPEC, SMEM_SPEC, SMEM_SPEC],
        [held(cells.shape)] * (count // 2),
        4 * MIB,
    )
    got = [
        lax.ppermute(outs[step - 1], "sub", [(i, (i + 2 * step) % count) for i in range(count)])
        for step in range(1, count // 2)
    ]
    return got + [outs[-1]]


def line_mask(active_ref, shape, rows):
    at = lax.broadcasted_iota(jnp.int32, shape, 0) - PAD + lax.axis_index("tile") * rows
    return (at >= 0) & (at < active_ref[lax.axis_index("sub")])


def tiles_of(parts, c, k, size, last):
    def ref_of(b):
        for first, ref in parts:
            if first <= b < first + ref.shape[2] // size:
                return ref, (b - first) * size

    ref, at = ref_of(k)
    mid = ref[c, :, at : at + size]
    none = jnp.zeros((mid.shape[0], LANES), jnp.float32)
    left, right = none, none
    if k > 0:
        ref, at = ref_of(k - 1)
        left = ref[c, :, at + size - LANES : at + size]
    if k < last:
        ref, at = ref_of(k + 1)
        right = ref[c, :, at : at + LANES]
    return mid, jnp.concatenate([left, mid, right], axis=1)


def relax_block(parts, source, diag_ref, hi_ref, lo_ref, k, mask):
    size = hi_ref.shape[1] // 2
    last = hi_ref.shape[0] - 1
    mids, sums = [], []
    for c in range(2):
        mid, wide = tiles_of(parts, c, k, size, last)
        rows, width = wide.shape
        beside = (
            pltpu.roll(wide, 1, 1)[:, LANES : LANES + size]
            + pltpu.roll(wide, width - 1, 1)[:, LANES : LANES + size]
        )
        beside = beside + (pltpu.roll(mid, 1, 0) + pltpu.roll(mid, rows - 1, 0))
        mids.append(mid)
        sums.append(source(c) + beside)
    cols = slice(k * size, (k + 1) * size)
    d0, d1 = diag_ref[0, :, cols], diag_ref[1, :, cols]
    r0 = sums[0] - (d0 * mids[0] - d1 * mids[1])
    r1 = sums[1] - (d0 * mids[1] + d1 * mids[0])
    high, low = split_halves(jnp.concatenate([r0, r1], axis=1))
    rows = high.shape[0]
    z = jnp.dot(
        jnp.concatenate([high, low], axis=0), hi_ref[k], preferred_element_type=jnp.float32
    )
    z = (z[:rows] + z[rows:]) + jnp.dot(high, lo_ref[k], preferred_element_type=jnp.float32)
    return [
        jnp.where(mask, mids[c] + z[:, c * size : (c + 1) * size], 0.0) for c in range(2)
    ]


def stored_source(source_ref, k, size):
    return lambda c: source_ref[c, :, k * size : (k + 1) * size]


def first_kernel(
    upto, start_ref, load_ref, diag_ref, one_ref, two_ref, mult_ref, hi_ref, lo_ref,
    active_ref, prow_ref, pcol_ref, pcur_ref, src_ref, dg_ref, f1_ref, f0_ref,
):
    _, rows, width = load_ref.shape
    size = hi_ref.shape[1] // 2
    own = slice(PAD, PAD + rows)
    above, below = slice(0, PAD), slice(PAD + rows, 2 * PAD + rows)
    tile = lax.axis_index("tile")
    even = lax.rem(tile, 2) == 0
    active = active_ref[lax.axis_index("sub")]

    def masked(cells, first):
        line = lax.broadcasted_iota(jnp.int32, cells.shape, 0) + (first + tile * rows)
        return jnp.where((line >= 0) & (line < active), cells, 0.0)

    for c in range(2):
        one, two = one_ref[c], two_ref[c]
        up = jnp.where(even, two, one)
        down = jnp.where(even, one, two)
        f0_ref[c, own, :] = masked(start_ref[c], 0)
        f0_ref[c, above, :] = masked(pltpu.roll(up, 5, 0), -PAD)
        f0_ref[c, below, :] = masked(down, rows)
        src_ref[c, own, :] = load_ref[c]
        src_ref[c, above, :] = pltpu.roll(up, 3, 0)
        src_ref[c, below, :] = pltpu.roll(down, 5, 0)
        dg_ref[c, own, :] = diag_ref[c]
        dg_ref[c, above, :] = pltpu.roll(up, 1, 0)
        dg_ref[c, below, :] = pltpu.roll(down, 3, 0)
        src_ref[c, own, 0:IB] -= mult_ref[c, 0:rows, :]
        src_ref[c, above, 0:IB] -= mult_ref[c, rows:, :]
        src_ref[c, below, 0:IB] -= mult_ref[c, rows:, :]
    span = PB + LANES
    at_row = lax.broadcasted_iota(jnp.int32, (PAD, span), 0)
    at_col = lax.broadcasted_iota(jnp.int32, (PAD, span), 1)
    for p in range(prow_ref.shape[1]):
        row = prow_ref[0, p] - tile * rows + PAD
        col = pcol_ref[0, p]
        base = pl.multiple_of(jnp.minimum(col // LANES * LANES, width - span), LANES)

        @pl.when((row >= 0) & (row < rows + 2 * PAD))
        def _(p=p, row=row, col=col, base=base):
            first = pl.multiple_of(row // PAD * PAD, PAD)
            hit = (at_row == row - first) & (at_col >= col - base) & (at_col < col - base + PB)
            for c in range(2):
                where = (c, pl.ds(first, PAD), pl.ds(base, span))
                src_ref[where] = src_ref[where] + jnp.where(hit, pcur_ref[0, c, p], 0.0)

    mask = line_mask(active_ref, (rows + 2 * PAD, size), rows)
    for k in range(upto):
        new = relax_block(
            [(0, f0_ref)], stored_source(src_ref, k, size), dg_ref, hi_ref, lo_ref, k, mask
        )
        for c in range(2):
            f1_ref[c, :, k * size : (k + 1) * size] = new[c]


def far_kernel(
    count, f0_ref, f1_ref, src_ref, dg_ref, hi_ref, lo_ref, active_ref, *refs
):
    pieces, (f1e_ref, f2s_ref, f2e_ref, f3e_ref, far_ref) = refs[:count], refs[count:]
    last = hi_ref.shape[0] - 1
    size = hi_ref.shape[1] // 2
    rows = far_ref.shape[1]
    mask = line_mask(active_ref, (rows + 2 * PAD, size), rows)
    into = []
    for c in range(2):
        piece = pieces[0][c]
        for other in pieces[1:]:
            piece = piece + other[c]
        edge = piece[rows:]
        ends = jnp.concatenate([edge, piece[:rows], edge], axis=0)
        into.append(jnp.concatenate([jnp.zeros((rows + 2 * PAD, size - IB), jnp.float32), ends], axis=1))
    end = stored_source(src_ref, last, size)

    def with_incoming(c):
        return end(c) + into[c]

    new = relax_block([(0, f0_ref)], with_incoming, dg_ref, hi_ref, lo_ref, last, mask)
    for c in range(2):
        f1e_ref[c] = new[c]
    f1 = [(last, f1e_ref), (0, f1_ref)]
    fill = f2s_ref.shape[2] // size

    def beside(k):
        new = relax_block([(0, f1_ref)], stored_source(src_ref, k, size), dg_ref, hi_ref, lo_ref, k, mask)
        for c in range(2):
            f2s_ref[c, :, k * size : (k + 1) * size] = new[c]

    for k in range(fill // 2):
        beside(k)
    for k, source in ((last, with_incoming), (last - 1, stored_source(src_ref, last - 1, size))):
        new = relax_block(f1, source, dg_ref, hi_ref, lo_ref, k, mask)
        for c in range(2):
            f2e_ref[c, :, (k - last + 1) * size : (k - last + 2) * size] = new[c]
    for k in range(fill // 2, fill):
        beside(k)
    new = relax_block([(last - 1, f2e_ref)], with_incoming, dg_ref, hi_ref, lo_ref, last, mask)
    for c in range(2):
        f3e_ref[c] = new[c][PAD : PAD + rows]
        far_ref[c] = new[c][PAD : PAD + rows, size - IB :]


def middle_kernel(f1_ref, src_ref, dg_ref, hi_ref, lo_ref, active_ref, f2_ref):
    size = hi_ref.shape[1] // 2
    mask = line_mask(active_ref, (f2_ref.shape[1], size), f2_ref.shape[1] - 2 * PAD)
    for i in range(f2_ref.shape[2] // size):
        k = i + FILL
        new = relax_block(
            [(0, f1_ref)], stored_source(src_ref, k, size), dg_ref, hi_ref, lo_ref, k, mask
        )
        for c in range(2):
            f2_ref[c, :, i * size : (i + 1) * size] = new[c]


def last_kernel(
    f2s_ref, f2_ref, f2e_ref, f3e_ref, src_ref, dg_ref, hi_ref, lo_ref, active_ref, out_ref, near_ref,
    held_ref, sem,
):
    size = hi_ref.shape[1] // 2

    def copy(k):
        cols = pl.ds(k * size, size)
        return pltpu.make_async_copy(held_ref.at[:, :, cols], out_ref.at[:, :, cols], sem.at[k])

    last = hi_ref.shape[0] - 1
    rows = out_ref.shape[1]
    mask = line_mask(active_ref, (rows + 2 * PAD, size), rows)
    f2 = [(last - 1, f2e_ref), (FILL, f2_ref), (0, f2s_ref)]
    for c in range(2):
        held_ref[c, :, last * size :] = f3e_ref[c]
    copy(last).start()
    for k in range(last):
        new = relax_block(f2, stored_source(src_ref, k, size), dg_ref, hi_ref, lo_ref, k, mask)
        for c in range(2):
            held_ref[c, :, k * size : (k + 1) * size] = new[c][PAD : PAD + rows]
            if k == 0:
                near_ref[c] = new[c][PAD : PAD + rows, :IB]
        copy(k).start()
    for k in range(last + 1):
        copy(k).wait()


def per_device(
    load_current,
    diagonal,
    start_field,
    block_inverse,
    multipliers,
    active_rows,
    contact_peer,
    contact_len,
    port_row,
    port_col,
    port_current,
):
    load, diag, start, mult = load_current[0], diagonal[0], start_field[0], multipliers[0]
    _, rows, width = load.shape
    nb, _, size, _, _ = block_inverse.shape[1:]
    high = rows + 2 * PAD
    step = 6 * high * (2 * size) ** 2

    m1, m2, one, two = call(
        edges_kernel,
        (start, load, diag, mult),
        [ANY_SPEC] * 3 + [VMEM_SPEC],
        [held((2, PAD, IB))] * 2 + [held((2, PAD, width))] * 2,
        56 * MIB,
        [pltpu.VMEM((3, 2, 2, PAD, width), jnp.float32), pltpu.SemaphoreType.DMA((3, 2))],
    )
    m1, m2 = call(
        pass_kernel, (m1, m2), [VMEM_SPEC] * 2, [held(m1.shape)] * 2, MIB, flops=4 * 10**10, moved=10**8
    )
    ends = swap_edges(m1, m2)
    one, two = swap_edges(one, two)
    lines_mult = call(
        lines_kernel,
        (mult, *ends),
        [VMEM_SPEC] * 3,
        held((2, rows + PAD, IB)),
        2 * MIB,
        flops=4 * 10**10,
        moved=10**8,
    )
    incoming = to_subs(lines_mult, contact_peer, contact_len, PAD, False)
    hi, lo = split_weights(block_inverse[0])

    whole = held((2, high, width))
    src, dg, f1, f0 = call(
        functools.partial(first_kernel, nb - 1),
        (start, load, diag, one, two, lines_mult, hi, lo, active_rows, port_row, port_col, port_current),
        [VMEM_SPEC] * 8 + [SMEM_SPEC] * 4,
        [whole, whole, held((2, high, (nb - 1) * size)), whole],
        4 * MIB,
        flops=step * (nb - 1),
    )
    f1e, f2s, f2e, f3e, far = call(
        functools.partial(far_kernel, len(incoming)),
        (f0, f1, src, dg, hi, lo, active_rows, *incoming),
        [VMEM_SPEC] * 6 + [SMEM_SPEC] + [VMEM_SPEC] * len(incoming),
        [held((2, high, size)), held((2, high, FILL * size)), held((2, high, 2 * size)), held((2, rows, size)), held((2, rows, IB))],
        4 * MIB,
        flops=step * (4 + FILL),
    )
    ends = to_subs(far, contact_peer, contact_len, 0, True)
    f2 = call(
        middle_kernel,
        (f1, src, dg, hi, lo, active_rows),
        [VMEM_SPEC] * 5 + [SMEM_SPEC],
        held((2, high, (nb - 2 - FILL) * size)),
        4 * MIB,
        flops=step * (nb - 2 - FILL),
    )
    solved, near = call(
        last_kernel,
        (f2s, f2, f2e, f3e, src, dg, hi, lo, active_rows),
        [VMEM_SPEC] * 8 + [SMEM_SPEC],
        [jax.ShapeDtypeStruct((2, rows, width), jnp.float32), held((2, rows, IB))],
        4 * MIB + 8 * rows * width,
        [pltpu.VMEM((2, rows, width), jnp.float32), pltpu.SemaphoreType.DMA((nb,))],
        flops=step * (nb - 1),
        out_specs=[ANY_SPEC, VMEM_SPEC],
    )
    updated = mult + (near - sum(ends))
    return (solved[None], updated[None])


def solution(mesh):
    lines = P("sub", None, "tile", None)
    in_specs = (
        lines,
        lines,
        lines,
        P("sub", None, None, None, None, None),
        lines,
        P(),
        P(),
        P(),
        P("sub", None),
        P("sub", None),
        P("sub", None, None),
    )
    return jax.shard_map(
        per_device, mesh=mesh, in_specs=in_specs, out_specs=(lines, lines), check_vma=False
    )
```

```python
import functools

import jax
import jax.numpy as jnp
from jax import lax
from jax.experimental import pallas as pl
from jax.experimental.pallas import tpu as pltpu
from jax.sharding import PartitionSpec as P

IB = 128
PB = 128
SWEEPS = 3
LANES = 128
PAD = 8
CARRY = 4 * 10**10, 10**10
MIB = 1 << 20

VMEM_SPEC = pl.BlockSpec(memory_space=pltpu.VMEM)
SMEM_SPEC = pl.BlockSpec(memory_space=pltpu.SMEM)
ANY_SPEC = pl.BlockSpec(memory_space=pl.ANY)


def call(kernel, args, specs, outs, limit, scratch=(), flops=0, moved=0, out_specs=None):
    return pl.pallas_call(
        kernel,
        out_shape=outs,
        in_specs=specs,
        out_specs=out_specs or jax.tree.map(lambda _: VMEM_SPEC, outs),
        scratch_shapes=scratch,
        compiler_params=pltpu.CompilerParams(vmem_limit_bytes=limit),
        cost_estimate=pl.CostEstimate(flops=flops, bytes_accessed=moved, transcendentals=0),
    )(*args)


def held(shape, dtype=jnp.float32):
    return pltpu.VMEM(shape, dtype)


def line_peers(peer_ref, len_ref, s, lines):
    found = jnp.zeros(lines.shape, jnp.int32)
    start = jnp.int32(0)
    for c in range(peer_ref.shape[1]):
        end = start + len_ref[s, c]
        found = jnp.where((lines >= start) & (lines < end), peer_ref[s, c], found)
        start = end
    return found


def pick(hit, cells):
    return jnp.where(hit[None], cells, 0.0)


def split_halves(x):
    high = x.astype(jnp.bfloat16)
    return high, (x - high.astype(jnp.float32)).astype(jnp.bfloat16)


def weights_kernel(size, first, b_ref, _, hi_ref, lo_ref, token_ref):
    token_ref[...] = jnp.zeros_like(token_ref)
    both = 2 * size
    parts = both // LANES
    for k in range(hi_ref.shape[0]):
        for q in range(parts):
            piece, comp = divmod(q, 2)
            rows = pl.ds(comp * size + piece * LANES, LANES)
            high, low = split_halves(b_ref[first + k, pl.ds(q, both, parts), :].T)
            hi_ref[k, rows, :] = high
            lo_ref[k, rows, :] = low


def flat_weights(blocks):
    nb, _, size, _, _ = blocks.shape
    flat = blocks.reshape(nb, 2, size, 2, size // LANES, LANES).transpose(0, 1, 2, 4, 3, 5)
    return pltpu.with_memory_space_constraint(flat.reshape(nb, -1, LANES), pltpu.VMEM)


def split_weights(flat, size, first, count, after):
    shape = (count, 2 * size, 2 * size)
    return call(
        functools.partial(weights_kernel, size, first),
        (flat, after),
        [VMEM_SPEC] * 2,
        [held(shape, jnp.bfloat16)] * 2 + [held((PAD, LANES))],
        2 * MIB,
        moved=count * size * size * 32,
    )


def edges_kernel(
    start_hbm, load_hbm, diag_hbm, mult_ref, peer_ref, len_ref, active_ref,
    m1_ref, m2_ref, one_ref, two_ref, peers_ref, mask_ref, buf, sem,
):
    rows = start_hbm.shape[1]
    even = lax.rem(lax.axis_index("tile"), 2) == 0
    ends = (pl.ds(0, PAD), pl.ds(rows - PAD, PAD))
    copies = [
        pltpu.make_async_copy(ref.at[:, ends[e]], buf.at[i, e], sem.at[i, e])
        for i, ref in enumerate((start_hbm, load_hbm, diag_hbm))
        for e in range(2)
    ]
    for copy in copies:
        copy.start()
    for c in range(2):
        top, bottom = mult_ref[c, ends[0]], mult_ref[c, ends[1]]
        m1_ref[c] = jnp.where(even, bottom, top)
        m2_ref[c] = jnp.where(even, top, bottom)
    me = lax.axis_index("sub")
    first = lax.axis_index("tile") * rows
    at = lax.broadcasted_iota(jnp.int32, peers_ref.shape[1:], 0)
    lines = jnp.where(at < rows + PAD // 2, at, at - rows - PAD) + first
    peers_ref[0] = line_peers(peer_ref, len_ref, me, lines)
    peers_ref[1] = line_peers(peer_ref, len_ref, me + 1 - 2 * lax.rem(me, 2), lines)
    at = lax.broadcasted_iota(jnp.int32, mask_ref.shape, 0) + (first - PAD)
    mask_ref[...] = jnp.where((at >= 0) & (at < active_ref[me]), 1.0, 0.0)
    row = lax.broadcasted_iota(jnp.int32, one_ref.shape[1:], 0)
    for copy in copies:
        copy.wait()

    def lines_of(c, e, turns):
        field, load, diag = (pltpu.roll(buf[i, e, c], t, 0) if t else buf[i, e, c] for i, t in enumerate(turns))
        return jnp.where(row < 3, field, jnp.where(row < 5, load, diag))

    for c in range(2):
        top, bottom = lines_of(c, 0, (0, 3, 5)), lines_of(c, 1, (3, 5, 7))
        one_ref[c] = jnp.where(even, bottom, top)
        two_ref[c] = jnp.where(even, top, bottom)


def pass_kernel(*refs):
    half = len(refs) // 2
    for ref, out in zip(refs[:half], refs[half:]):
        out[...] = ref[...]


def lines_kernel(mult_ref, one_ref, two_ref, _, out_ref):
    rows = mult_ref.shape[1]
    even = lax.rem(lax.axis_index("tile"), 2) == 0
    low = lax.broadcasted_iota(jnp.int32, (PAD, IB), 0) < PAD // 2
    for c in range(2):
        out_ref[c, :rows] = mult_ref[c]
        out_ref[c, rows:] = jnp.where(low == even, one_ref[c], two_ref[c])


def passed(cost, *arrays):
    return call(
        pass_kernel,
        arrays,
        [VMEM_SPEC] * len(arrays),
        [held(x.shape) for x in arrays],
        MIB,
        flops=cost,
        moved=10**6,
    )


def swaps(count):
    one = [(i, i ^ 1) for i in range(count)]
    two = [(i, ((i - 1) if i % 2 == 0 else (i + 1)) % count) for i in range(count)]
    return one, two


def swap_edges(one, two):
    first, second = swaps(lax.axis_size("tile"))
    return lax.ppermute(one, "tile", first), lax.ppermute(two, "tile", second)


def to_chip(cells, step):
    count = lax.axis_size("sub")
    return lax.ppermute(cells, "sub", [(i, (i + 2 * step) % count) for i in range(count)])


def swap_cores(cells):
    return lax.ppermute(cells, "sub", [(i, i ^ 1) for i in range(lax.axis_size("sub"))])


def merge_kernel(peers_ref, own_ref, other_ref, _, *outs):
    me, count = lax.axis_index("sub"), 2 * len(outs)
    own, other = own_ref[...], other_ref[...]
    for step in range(1, len(outs)):
        to = lax.rem(me + 2 * step, count)
        outs[step][...] = pick(peers_ref[0] == to, own) + pick(peers_ref[1] == to, other)
    outs[0][...] = pick(peers_ref[1] == me, other)


def sums_kernel(peers_ref, *refs):
    pieces, (mine_ref, theirs_ref) = refs[:-2], refs[-2:]
    me, count = lax.axis_index("sub"), 2 * len(pieces)
    rows = mine_ref.shape[1]
    mine = theirs = 0.0
    for j, piece in enumerate(pieces):
        cells = piece[...]
        s = lax.rem(me + count - 2 * j, count)
        mine += pick(peers_ref[0, :rows] == s, cells)
        theirs += pick(peers_ref[1, :rows] == s, cells)
    mine_ref[...] = mine
    theirs_ref[...] = theirs


class Weights:
    def __init__(self, *refs):
        self.parts = refs[:2], refs[2:]
        self.size = refs[0].shape[1] // 2
        self.last = refs[0].shape[0] + refs[2].shape[0] - 1

    def part(self, k, low):
        first = self.parts[0][0].shape[0]
        return self.parts[0][low][k] if k < first else self.parts[1][low][k - first]

    def high(self, k):
        return self.part(k, 0)

    def low(self, k):
        return self.part(k, 1)


def line_mask(mask_ref, size):
    active = mask_ref[...] > 0.0
    return jnp.concatenate([active] * (size // LANES), axis=1)


def with_ends(own_ref, ends_ref, c, cols):
    return jnp.concatenate([ends_ref[c, :PAD, cols], own_ref[c, :, cols], ends_ref[c, PAD:, cols]], axis=0)


def reader(parts, size):
    def read(c, start, count):
        for first, ref in parts:
            if first * size <= start and start + count <= first * size + ref.shape[2]:
                return ref[c, :, start - first * size : start - first * size + count]

    return read


def tiles_of(read, c, k, size, last):
    mid = read(c, k * size, size)
    none = jnp.zeros((mid.shape[0], LANES), jnp.float32)
    left = read(c, k * size - LANES, LANES) if k > 0 else none
    right = read(c, (k + 1) * size, LANES) if k < last else none
    return mid, jnp.concatenate([left, mid, right], axis=1)


def relax_block(field, source, diag_ref, w, k, mask):
    size, last = w.size, w.last
    mids, sums = [], []
    for c in range(2):
        mid, wide = tiles_of(field, c, k, size, last)
        rows, width = wide.shape
        beside = (
            pltpu.roll(wide, 1, 1)[:, LANES : LANES + size]
            + pltpu.roll(wide, width - 1, 1)[:, LANES : LANES + size]
        )
        beside = beside + (pltpu.roll(mid, 1, 0) + pltpu.roll(mid, rows - 1, 0))
        mids.append(mid)
        sums.append(source(c) + beside)
    cols = slice(k * size, (k + 1) * size)
    d0, d1 = (with_ends(*diag_ref, c, cols) for c in range(2))
    r0 = sums[0] - (d0 * mids[0] - d1 * mids[1])
    r1 = sums[1] - (d0 * mids[1] + d1 * mids[0])
    high, low = split_halves(jnp.concatenate([r0, r1], axis=1))
    rows = high.shape[0]
    z = jnp.dot(
        jnp.concatenate([high, low], axis=0), w.high(k), preferred_element_type=jnp.float32
    )
    z = (z[:rows] + z[rows:]) + jnp.dot(high, w.low(k), preferred_element_type=jnp.float32)
    return [
        jnp.where(mask, mids[c] + z[:, c * size : (c + 1) * size], 0.0) for c in range(2)
    ]


def start_reader(start_ref, ends_ref, mask_ref):
    def read(c, start, count):
        cells = with_ends(start_ref, ends_ref, c, slice(start, start + count))
        return jnp.where(line_mask(mask_ref, count), cells, 0.0)

    return read


def stored_source(source_ref, k, size):
    return lambda c: source_ref[c, :, k * size : (k + 1) * size]


def first_kernel(
    upto, start_ref, load_ref, diag_ref, one_ref, two_ref, mult_ref, ha_ref, la_ref, hb_ref, lb_ref, mask_ref,
    prow_ref, pcol_ref, pcur_ref, src_ref, dge_ref, f1_ref, f0e_ref,
):
    _, rows, width = load_ref.shape
    w = Weights(ha_ref, la_ref, hb_ref, lb_ref)
    size = w.size
    own = slice(PAD, PAD + rows)
    above, below = slice(0, PAD), slice(PAD + rows, 2 * PAD + rows)
    tile = lax.axis_index("tile")
    even = lax.rem(tile, 2) == 0
    for c in range(2):
        one, two = one_ref[c], two_ref[c]
        up = jnp.where(even, two, one)
        down = jnp.where(even, one, two)
        f0e_ref[c, :PAD] = pltpu.roll(up, 5, 0)
        f0e_ref[c, PAD:] = down
        dge_ref[c, :PAD] = pltpu.roll(up, 1, 0)
        dge_ref[c, PAD:] = pltpu.roll(down, 3, 0)
        src_ref[c, own, :] = load_ref[c]
        src_ref[c, above, :] = pltpu.roll(up, 3, 0)
        src_ref[c, below, :] = pltpu.roll(down, 5, 0)
        src_ref[c, own, 0:IB] -= mult_ref[c, :rows]
        src_ref[c, above, 0:IB] -= mult_ref[c, rows:]
        src_ref[c, below, 0:IB] -= mult_ref[c, rows:]
    span = PB + LANES
    at_row = lax.broadcasted_iota(jnp.int32, (PAD, span), 0)
    at_col = lax.broadcasted_iota(jnp.int32, (PAD, span), 1)
    for p in range(prow_ref.shape[1]):
        row = prow_ref[0, p] - tile * rows + PAD
        col = pcol_ref[0, p]
        base = pl.multiple_of(jnp.minimum(col // LANES * LANES, width - span), LANES)

        @pl.when((row >= 0) & (row < rows + 2 * PAD))
        def _(p=p, row=row, col=col, base=base):
            first = pl.multiple_of(row // PAD * PAD, PAD)
            hit = (at_row == row - first) & (at_col >= col - base) & (at_col < col - base + PB)
            for c in range(2):
                where = (c, pl.ds(first, PAD), pl.ds(base, span))
                src_ref[where] = src_ref[where] + jnp.where(hit, pcur_ref[0, c, p], 0.0)

    mask = line_mask(mask_ref, size)
    f0 = start_reader(start_ref, f0e_ref, mask_ref)
    dg_ref = (diag_ref, dge_ref)
    for k in range(upto):
        new = relax_block(f0, stored_source(src_ref, k, size), dg_ref, w, k, mask)
        for c in range(2):
            f1_ref[c, :, k * size : (k + 1) * size] = new[c]


def far_kernel(
    start_ref, f0e_ref, f1_ref, src_ref, diag_ref, dge_ref, ha_ref, la_ref, hb_ref, lb_ref, mask_ref, *refs,
):
    w = Weights(ha_ref, la_ref, hb_ref, lb_ref)
    size, last = w.size, w.last
    pieces, (f1e_ref, f2s_ref, f2e_ref, f3e_ref, far_ref) = refs[:-5], refs[-5:]
    rows = far_ref.shape[1]
    mask = line_mask(mask_ref, size)
    into = []
    for c in range(2):
        cells = pieces[0][c]
        for piece in pieces[1:]:
            cells += piece[c]
        ends = jnp.concatenate([cells[rows:], cells[:rows], cells[rows:]], axis=0)
        into.append(jnp.concatenate([jnp.zeros((rows + 2 * PAD, size - IB), jnp.float32), ends], axis=1))
    end = stored_source(src_ref, last, size)

    def with_incoming(c):
        return end(c) + into[c]

    dg_ref = (diag_ref, dge_ref)
    new = relax_block(start_reader(start_ref, f0e_ref, mask_ref), with_incoming, dg_ref, w, last, mask)
    for c in range(2):
        f1e_ref[c] = new[c]
    f1 = reader([(last, f1e_ref), (0, f1_ref)], size)
    old = reader([(0, f1_ref)], size)
    fill = f2s_ref.shape[2] // size

    def beside(k):
        new = relax_block(old, stored_source(src_ref, k, size), dg_ref, w, k, mask)
        for c in range(2):
            f2s_ref[c, :, k * size : (k + 1) * size] = new[c]

    for k in range(fill // 2):
        beside(k)
    for k, source in ((last, with_incoming), (last - 1, stored_source(src_ref, last - 1, size))):
        new = relax_block(f1, source, dg_ref, w, k, mask)
        for c in range(2):
            f2e_ref[c, :, (k - last + 1) * size : (k - last + 2) * size] = new[c]
    for k in range(fill // 2, fill):
        beside(k)
    new = relax_block(reader([(last - 1, f2e_ref)], size), with_incoming, dg_ref, w, last, mask)
    for c in range(2):
        f3e_ref[c] = new[c][PAD : PAD + rows]
        far_ref[c] = new[c][PAD : PAD + rows, size - IB :]


def middle_kernel(
    f1_ref, f2s_ref, src_ref, diag_ref, dge_ref, ha_ref, la_ref, hb_ref, lb_ref, mask_ref, f2_ref, f3_ref
):
    w = Weights(ha_ref, la_ref, hb_ref, lb_ref)
    size = w.size
    rows = f3_ref.shape[1]
    first = f2s_ref.shape[2] // size
    mask = line_mask(mask_ref, size)
    dg_ref = (diag_ref, dge_ref)
    f1 = reader([(0, f1_ref)], size)
    for i in range(f2_ref.shape[2] // size):
        k = first + i
        new = relax_block(f1, stored_source(src_ref, k, size), dg_ref, w, k, mask)
        for c in range(2):
            f2_ref[c, :, i * size : (i + 1) * size] = new[c]
    f2 = reader([(0, f2s_ref), (first, f2_ref)], size)
    for k in range(f3_ref.shape[2] // size):
        new = relax_block(f2, stored_source(src_ref, k, size), dg_ref, w, k, mask)
        for c in range(2):
            f3_ref[c, :, k * size : (k + 1) * size] = new[c][PAD : PAD + rows]


def last_kernel(
    f2s_ref, f2_ref, f2e_ref, f3_ref, f3e_ref, src_ref, diag_ref, dge_ref, ha_ref, la_ref, hb_ref, lb_ref, mask_ref,
    out_ref, held_ref, sem,
):
    w = Weights(ha_ref, la_ref, hb_ref, lb_ref)
    size, last = w.size, w.last
    rows = out_ref.shape[1]
    done = f3_ref.shape[2] // size
    mask = line_mask(mask_ref, size)

    def copy(ref, first, blocks, slot):
        cols = pl.ds(first * size, blocks * size)
        return pltpu.make_async_copy(ref, out_ref.at[:, :, cols], sem.at[slot])

    copies = [copy(f3_ref, 0, done, 0), copy(f3e_ref, last, 1, 1)]
    for one in copies:
        one.start()
    dg_ref = (diag_ref, dge_ref)
    f2 = reader([(last - 1, f2e_ref), (f2s_ref.shape[2] // size, f2_ref), (0, f2s_ref)], size)
    for i in range(last - done):
        k = done + i
        new = relax_block(f2, stored_source(src_ref, k, size), dg_ref, w, k, mask)
        for c in range(2):
            held_ref[i, c] = new[c][PAD : PAD + rows]
        copies.append(copy(held_ref.at[i], k, 1, 2 + i))
        copies[-1].start()
    for one in copies:
        one.wait()


def per_device(
    load_current,
    diagonal,
    start_field,
    block_inverse,
    multipliers,
    active_rows,
    contact_peer,
    contact_len,
    port_row,
    port_col,
    port_current,
):
    load, diag, start, mult = load_current[0], diagonal[0], start_field[0], multipliers[0]
    _, rows, width = load.shape
    nb, _, size, _, _ = block_inverse.shape[1:]
    high = rows + 2 * PAD
    step = 6 * high * (2 * size) ** 2

    fill, done = nb * 3 // 8, nb // 2
    count = lax.axis_size("sub")

    m1, m2, one, two, peers, mask = call(
        edges_kernel,
        (start, load, diag, mult, contact_peer, contact_len, active_rows),
        [ANY_SPEC] * 3 + [VMEM_SPEC] + [SMEM_SPEC] * 3,
        [held((2, PAD, IB))] * 2
        + [held((2, PAD, width))] * 2
        + [held((2, rows + PAD, LANES), jnp.int32), held((high, LANES))],
        56 * MIB,
        [pltpu.VMEM((3, 2, 2, PAD, width), jnp.float32), pltpu.SemaphoreType.DMA((3, 2))],
    )
    m1, m2 = passed(CARRY[0], m1, m2)
    m1, m2 = swap_edges(m1, m2)
    one, two = swap_edges(one, two)
    (mask,) = passed(CARRY[1], mask)
    flat = flat_weights(block_inverse[0])
    half = nb // 2
    ha, la, token = split_weights(flat, size, 0, half, mask)
    lines_mult = call(
        lines_kernel,
        (mult, m1, m2, token),
        [VMEM_SPEC] * 4,
        held((2, rows + PAD, IB)),
        MIB,
    )
    other = swap_cores(lines_mult)
    hb, lb, token = split_weights(flat, size, half, nb - half, token)
    merged = call(
        merge_kernel,
        (peers, lines_mult, other, token),
        [VMEM_SPEC] * 4,
        [held(lines_mult.shape)] * (count // 2),
        2 * MIB,
    )
    incoming = [to_chip(cells, step) if step else cells for step, cells in enumerate(merged)]
    weights = (ha, la, hb, lb)

    whole, some = held((2, high, width)), held((2, 2 * PAD, width))
    src, dge, f1, f0e = call(
        functools.partial(first_kernel, nb - 1),
        (start, load, diag, one, two, lines_mult, *weights, mask, port_row, port_col, port_current),
        [VMEM_SPEC] * 11 + [SMEM_SPEC] * 3,
        [whole, some, held((2, high, (nb - 1) * size)), some],
        4 * MIB,
        flops=step * (nb - 1),
    )
    f1e, f2s, f2e, f3e, far = call(
        far_kernel,
        (start, f0e, f1, src, diag, dge, *weights, mask, *incoming),
        [VMEM_SPEC] * (11 + len(incoming)),
        [
            held((2, high, size)),
            held((2, high, fill * size)),
            held((2, high, 2 * size)),
            held((2, rows, size)),
            held((2, rows, IB)),
        ],
        4 * MIB,
        flops=step * (4 + fill),
    )
    ends = [to_chip(far, step) if step else far for step in range(count // 2)]
    f2, f3 = call(
        middle_kernel,
        (f1, f2s, src, diag, dge, *weights, mask),
        [VMEM_SPEC] * 10,
        [held((2, high, (nb - 2 - fill) * size)), held((2, rows, done * size))],
        4 * MIB,
        flops=step * (nb - 2 - fill + done),
    )
    mine, theirs = call(
        sums_kernel, (peers, *ends), [VMEM_SPEC] * (1 + len(ends)), [held(far.shape)] * 2, MIB
    )
    theirs = swap_cores(theirs)
    solved = call(
        last_kernel,
        (f2s, f2, f2e, f3, f3e, src, diag, dge, *weights, mask),
        [VMEM_SPEC] * 13,
        jax.ShapeDtypeStruct((2, rows, width), jnp.float32),
        4 * MIB + 8 * rows * width,
        [pltpu.VMEM((nb - 1 - done, 2, rows, size), jnp.float32), pltpu.SemaphoreType.DMA((nb + 1 - done,))],
        flops=step * (nb - 1 - done),
        out_specs=ANY_SPEC,
    )
    updated = mult + (f3[:, :, :IB] - (mine + theirs))
    return (solved[None], updated[None])


def solution(mesh):
    lines = P("sub", None, "tile", None)
    in_specs = (
        lines,
        lines,
        lines,
        P("sub", None, None, None, None, None),
        lines,
        P(),
        P(),
        P(),
        P("sub", None),
        P("sub", None),
        P("sub", None, None),
    )
    return jax.shard_map(
        per_device, mesh=mesh, in_specs=in_specs, out_specs=(lines, lines), check_vma=False
    )
```

```python
import functools

import jax
import jax.numpy as jnp
from jax import lax
from jax.experimental import pallas as pl
from jax.experimental.pallas import tpu as pltpu
from jax.sharding import PartitionSpec as P

IB = 128
PB = 128
SWEEPS = 3
LANES = 128
PAD = 8
CARRY = 4 * 10**10, 10**10
MIB = 1 << 20

VMEM_SPEC = pl.BlockSpec(memory_space=pltpu.VMEM)
SMEM_SPEC = pl.BlockSpec(memory_space=pltpu.SMEM)
ANY_SPEC = pl.BlockSpec(memory_space=pl.ANY)


def call(kernel, args, specs, outs, limit, scratch=(), flops=0, moved=0, out_specs=None):
    return pl.pallas_call(
        kernel,
        out_shape=outs,
        in_specs=specs,
        out_specs=out_specs or jax.tree.map(lambda _: VMEM_SPEC, outs),
        scratch_shapes=scratch,
        compiler_params=pltpu.CompilerParams(vmem_limit_bytes=limit),
        cost_estimate=pl.CostEstimate(flops=flops, bytes_accessed=moved, transcendentals=0),
    )(*args)


def held(shape, dtype=jnp.float32):
    return pltpu.VMEM(shape, dtype)


def line_peers(peer_ref, len_ref, s, lines):
    found = jnp.zeros(lines.shape, jnp.int32)
    start = jnp.int32(0)
    for c in range(peer_ref.shape[1]):
        end = start + len_ref[s, c]
        found = jnp.where((lines >= start) & (lines < end), peer_ref[s, c], found)
        start = end
    return found


def pick(hit, cells):
    return jnp.where(hit[None], cells, 0.0)


def split_halves(x):
    high = x.astype(jnp.bfloat16)
    return high, (x - high.astype(jnp.float32)).astype(jnp.bfloat16)


def weights_kernel(size, first, b_ref, _, hi_ref, lo_ref, token_ref):
    token_ref[...] = jnp.zeros_like(token_ref)
    both = 2 * size
    parts = both // LANES
    for k in range(hi_ref.shape[0]):
        for q in range(parts):
            piece, comp = divmod(q, 2)
            rows = pl.ds(comp * size + piece * LANES, LANES)
            high, low = split_halves(b_ref[first + k, pl.ds(q, both, parts), :].T)
            hi_ref[k, rows, :] = high
            lo_ref[k, rows, :] = low


def flat_weights(blocks):
    nb, _, size, _, _ = blocks.shape
    flat = blocks.reshape(nb, 2, size, 2, size // LANES, LANES).transpose(0, 1, 2, 4, 3, 5)
    return pltpu.with_memory_space_constraint(flat.reshape(nb, -1, LANES), pltpu.VMEM)


def split_weights(flat, size, first, count, after):
    shape = (count, 2 * size, 2 * size)
    high, low, token = call(
        functools.partial(weights_kernel, size, first),
        (flat, after),
        [VMEM_SPEC] * 2,
        [held(shape, jnp.bfloat16)] * 2 + [held((PAD, LANES))],
        2 * MIB,
        moved=count * size * size * 32,
    )
    return (high, low), token


def edges_kernel(
    start_hbm, load_hbm, diag_hbm, mult_ref, peer_ref, len_ref, active_ref,
    m1_ref, m2_ref, one_ref, two_ref, peers_ref, mask_ref, buf, sem,
):
    rows = start_hbm.shape[1]
    even = lax.rem(lax.axis_index("tile"), 2) == 0
    ends = (pl.ds(0, PAD), pl.ds(rows - PAD, PAD))
    copies = [
        pltpu.make_async_copy(ref.at[:, ends[e]], buf.at[i, e], sem.at[i, e])
        for i, ref in enumerate((start_hbm, load_hbm, diag_hbm))
        for e in range(2)
    ]
    for copy in copies:
        copy.start()
    for c in range(2):
        top, bottom = mult_ref[c, ends[0]], mult_ref[c, ends[1]]
        m1_ref[c] = jnp.where(even, bottom, top)
        m2_ref[c] = jnp.where(even, top, bottom)
    me = lax.axis_index("sub")
    first = lax.axis_index("tile") * rows
    at = lax.broadcasted_iota(jnp.int32, peers_ref.shape[1:], 0)
    lines = jnp.where(at < rows + PAD // 2, at, at - rows - PAD) + first
    peers_ref[0] = line_peers(peer_ref, len_ref, me, lines)
    peers_ref[1] = line_peers(peer_ref, len_ref, me + 1 - 2 * lax.rem(me, 2), lines)
    at = lax.broadcasted_iota(jnp.int32, mask_ref.shape, 0) + (first - PAD)
    mask_ref[...] = jnp.where((at >= 0) & (at < active_ref[me]), 1.0, 0.0)
    row = lax.broadcasted_iota(jnp.int32, (PAD, start_hbm.shape[2]), 0)
    for copy in copies:
        copy.wait()

    def lines_of(c, e, turns):
        field, load, diag = (pltpu.roll(buf[i, e, c], t, 0) if t else buf[i, e, c] for i, t in enumerate(turns))
        return jnp.where(row < 3, field, jnp.where(row < 5, load, diag))

    for c in range(2):
        top, bottom = pack_rows(lines_of(c, 0, (0, 3, 5))), pack_rows(lines_of(c, 1, (3, 5, 7)))
        one_ref[c] = jnp.where(even, bottom, top)
        two_ref[c] = jnp.where(even, top, bottom)


def pack_rows(cells):
    width = cells.shape[1] // PAD * (PAD - 1)
    ends = cells[:, width:]
    tail = jnp.concatenate([pltpu.roll(ends, PAD - 1 - r, 0) for r in range(PAD - 1)], axis=1)
    row = lax.broadcasted_iota(jnp.int32, tail.shape, 0)
    return jnp.where(row == PAD - 1, tail, cells[:, :width])


def unpack_rows(cells):
    step = cells.shape[1] // (PAD - 1)
    row = lax.broadcasted_iota(jnp.int32, (PAD, step), 0)
    ends = pltpu.roll(cells[:, :step], 1, 0)
    for r in range(1, PAD - 1):
        ends = jnp.where(row == r, pltpu.roll(cells[:, r * step : (r + 1) * step], r + 1, 0), ends)
    return jnp.concatenate([cells, ends], axis=1)


def pass_kernel(*refs):
    half = len(refs) // 2
    for ref, out in zip(refs[:half], refs[half:]):
        out[...] = ref[...]


def lines_kernel(mult_ref, one_ref, two_ref, _, out_ref):
    rows = mult_ref.shape[1]
    even = lax.rem(lax.axis_index("tile"), 2) == 0
    low = lax.broadcasted_iota(jnp.int32, (PAD, IB), 0) < PAD // 2
    for c in range(2):
        out_ref[c, :rows] = mult_ref[c]
        out_ref[c, rows:] = jnp.where(low == even, one_ref[c], two_ref[c])


def passed(cost, *arrays):
    return call(
        pass_kernel,
        arrays,
        [VMEM_SPEC] * len(arrays),
        [held(x.shape) for x in arrays],
        MIB,
        flops=cost,
        moved=10**6,
    )


def swaps(count):
    one = [(i, i ^ 1) for i in range(count)]
    two = [(i, ((i - 1) if i % 2 == 0 else (i + 1)) % count) for i in range(count)]
    return one, two


def swap_edges(one, two):
    first, second = swaps(lax.axis_size("tile"))
    return lax.ppermute(one, "tile", first), lax.ppermute(two, "tile", second)


def to_chip(cells, step):
    count = lax.axis_size("sub")
    return lax.ppermute(cells, "sub", [(i, (i + 2 * step) % count) for i in range(count)])


def swap_cores(cells):
    return lax.ppermute(cells, "sub", [(i, i ^ 1) for i in range(lax.axis_size("sub"))])


def merge_kernel(peers_ref, own_ref, other_ref, _, keep_ref, send_ref):
    me = lax.axis_index("sub")
    own, other = own_ref[...], other_ref[...]
    for x in range(2 * keep_ref.shape[0]):
        to = me ^ (2 * x)
        out = send_ref if x % 2 else keep_ref
        out[x // 2] = pick(peers_ref[0] == to, own) + pick(peers_ref[1] == to, other)


def fold_kernel(keep_ref, got_ref, _, next_ref, send_ref):
    for x in range(keep_ref.shape[0]):
        out = send_ref if x % 2 else next_ref
        out[x // 2] = keep_ref[x] + got_ref[x]


def halved(cells):
    shape = (cells.shape[0] // 2, *cells.shape[1:])
    return [held(shape), held(shape)]


def over_bit(cells, bit):
    return lax.ppermute(cells, "sub", [(i, i ^ (2 * bit)) for i in range(lax.axis_size("sub"))])


def sums_kernel(peers_ref, *refs):
    pieces, (mine_ref, theirs_ref) = refs[:-2], refs[-2:]
    me, count = lax.axis_index("sub"), 2 * len(pieces)
    rows = mine_ref.shape[1]
    mine = theirs = 0.0
    for j, piece in enumerate(pieces):
        cells = piece[...]
        s = lax.rem(me + count - 2 * j, count)
        mine += pick(peers_ref[0, :rows] == s, cells)
        theirs += pick(peers_ref[1, :rows] == s, cells)
    mine_ref[...] = mine
    theirs_ref[...] = theirs


class Weights:
    def __init__(self, refs):
        self.runs = list(zip(refs[::2], refs[1::2]))
        self.size = refs[0].shape[1] // 2
        self.last = sum(ref.shape[0] for ref in refs[::2]) - 1

    def part(self, k, low):
        for run in self.runs:
            if k < run[0].shape[0]:
                return run[low][k]
            k -= run[0].shape[0]

    def high(self, k):
        return self.part(k, 0)

    def low(self, k):
        return self.part(k, 1)


def line_mask(mask_ref, size):
    active = mask_ref[...] > 0.0
    return jnp.concatenate([active] * (size // LANES), axis=1)


def with_ends(own_ref, ends_ref, c, cols):
    return jnp.concatenate([ends_ref[c, :PAD, cols], own_ref[c, :, cols], ends_ref[c, PAD:, cols]], axis=0)


def reader(parts, size):
    def read(c, start, count):
        for first, ref in parts:
            if first * size <= start and start + count <= first * size + ref.shape[2]:
                return ref[c, :, start - first * size : start - first * size + count]

    return read


def tiles_of(read, c, k, size, last):
    mid = read(c, k * size, size)
    none = jnp.zeros((mid.shape[0], LANES), jnp.float32)
    left = read(c, k * size - LANES, LANES) if k > 0 else none
    right = read(c, (k + 1) * size, LANES) if k < last else none
    return mid, jnp.concatenate([left, mid, right], axis=1)


def relax_block(field, source, diag_ref, w, k, mask):
    size, last = w.size, w.last
    mids, sums = [], []
    for c in range(2):
        mid, wide = tiles_of(field, c, k, size, last)
        rows, width = wide.shape
        beside = (
            pltpu.roll(wide, 1, 1)[:, LANES : LANES + size]
            + pltpu.roll(wide, width - 1, 1)[:, LANES : LANES + size]
        )
        beside = beside + (pltpu.roll(mid, 1, 0) + pltpu.roll(mid, rows - 1, 0))
        mids.append(mid)
        sums.append(source(c) + beside)
    cols = slice(k * size, (k + 1) * size)
    d0, d1 = (with_ends(*diag_ref, c, cols) for c in range(2))
    r0 = sums[0] - (d0 * mids[0] - d1 * mids[1])
    r1 = sums[1] - (d0 * mids[1] + d1 * mids[0])
    high, low = split_halves(jnp.concatenate([r0, r1], axis=1))
    rows = high.shape[0]
    z = jnp.dot(
        jnp.concatenate([high, low], axis=0), w.high(k), preferred_element_type=jnp.float32
    )
    z = (z[:rows] + z[rows:]) + jnp.dot(high, w.low(k), preferred_element_type=jnp.float32)
    return [
        jnp.where(mask, mids[c] + z[:, c * size : (c + 1) * size], 0.0) for c in range(2)
    ]


def start_reader(start_ref, ends_ref, mask_ref):
    def read(c, start, count):
        cells = with_ends(start_ref, ends_ref, c, slice(start, start + count))
        return jnp.where(line_mask(mask_ref, count), cells, 0.0)

    return read


def stored_source(source_ref, k, size):
    return lambda c: source_ref[c, :, k * size : (k + 1) * size]


def first_kernel(
    upto, start_ref, load_ref, diag_ref, one_ref, two_ref, mult_ref, mask_ref,
    prow_ref, pcol_ref, pcur_ref, *refs,
):
    w_refs, (src_ref, dge_ref, f1_ref, f0e_ref) = refs[:-4], refs[-4:]
    _, rows, width = load_ref.shape
    w = Weights(w_refs)
    size = w.size
    own = slice(PAD, PAD + rows)
    above, below = slice(0, PAD), slice(PAD + rows, 2 * PAD + rows)
    tile = lax.axis_index("tile")
    even = lax.rem(tile, 2) == 0
    for c in range(2):
        one, two = one_ref[c], two_ref[c]
        up = unpack_rows(jnp.where(even, two, one))
        down = unpack_rows(jnp.where(even, one, two))
        f0e_ref[c, :PAD] = pltpu.roll(up, 5, 0)
        f0e_ref[c, PAD:] = down
        dge_ref[c, :PAD] = pltpu.roll(up, 1, 0)
        dge_ref[c, PAD:] = pltpu.roll(down, 3, 0)
        src_ref[c, own, :] = load_ref[c]
        src_ref[c, above, :] = pltpu.roll(up, 3, 0)
        src_ref[c, below, :] = pltpu.roll(down, 5, 0)
        src_ref[c, own, 0:IB] -= mult_ref[c, :rows]
        src_ref[c, above, 0:IB] -= mult_ref[c, rows:]
        src_ref[c, below, 0:IB] -= mult_ref[c, rows:]
    span = PB + LANES
    at_row = lax.broadcasted_iota(jnp.int32, (PAD, span), 0)
    at_col = lax.broadcasted_iota(jnp.int32, (PAD, span), 1)
    for p in range(prow_ref.shape[1]):
        row = prow_ref[0, p] - tile * rows + PAD
        col = pcol_ref[0, p]
        base = pl.multiple_of(jnp.minimum(col // LANES * LANES, width - span), LANES)

        @pl.when((row >= 0) & (row < rows + 2 * PAD))
        def _(p=p, row=row, col=col, base=base):
            first = pl.multiple_of(row // PAD * PAD, PAD)
            hit = (at_row == row - first) & (at_col >= col - base) & (at_col < col - base + PB)
            for c in range(2):
                where = (c, pl.ds(first, PAD), pl.ds(base, span))
                src_ref[where] = src_ref[where] + jnp.where(hit, pcur_ref[0, c, p], 0.0)

    mask = line_mask(mask_ref, size)
    f0 = start_reader(start_ref, f0e_ref, mask_ref)
    dg_ref = (diag_ref, dge_ref)
    for k in range(upto):
        new = relax_block(f0, stored_source(src_ref, k, size), dg_ref, w, k, mask)
        for c in range(2):
            f1_ref[c, :, k * size : (k + 1) * size] = new[c]


def far_kernel(
    count, start_ref, f0e_ref, f1_ref, src_ref, diag_ref, dge_ref, mask_ref, *refs
):
    pieces, w_refs, (f1e_ref, f2s_ref, f2e_ref, f3e_ref, far_ref) = refs[:count], refs[count:-5], refs[-5:]
    w = Weights(w_refs)
    size, last = w.size, w.last
    rows = far_ref.shape[1]
    mask = line_mask(mask_ref, size)
    into = []
    for c in range(2):
        cells = pieces[0][c]
        for piece in pieces[1:]:
            cells += piece[c]
        ends = jnp.concatenate([cells[rows:], cells[:rows], cells[rows:]], axis=0)
        into.append(jnp.concatenate([jnp.zeros((rows + 2 * PAD, size - IB), jnp.float32), ends], axis=1))
    end = stored_source(src_ref, last, size)

    def with_incoming(c):
        return end(c) + into[c]

    dg_ref = (diag_ref, dge_ref)
    new = relax_block(start_reader(start_ref, f0e_ref, mask_ref), with_incoming, dg_ref, w, last, mask)
    for c in range(2):
        f1e_ref[c] = new[c]
    f1 = reader([(last, f1e_ref), (0, f1_ref)], size)
    old = reader([(0, f1_ref)], size)
    fill = f2s_ref.shape[2] // size

    def beside(k):
        new = relax_block(old, stored_source(src_ref, k, size), dg_ref, w, k, mask)
        for c in range(2):
            f2s_ref[c, :, k * size : (k + 1) * size] = new[c]

    for k in range(fill // 2):
        beside(k)
    for k, source in ((last, with_incoming), (last - 1, stored_source(src_ref, last - 1, size))):
        new = relax_block(f1, source, dg_ref, w, k, mask)
        for c in range(2):
            f2e_ref[c, :, (k - last + 1) * size : (k - last + 2) * size] = new[c]
    for k in range(fill // 2, fill):
        beside(k)
    new = relax_block(reader([(last - 1, f2e_ref)], size), with_incoming, dg_ref, w, last, mask)
    for c in range(2):
        f3e_ref[c] = new[c][PAD : PAD + rows]
        far_ref[c] = new[c][PAD : PAD + rows, size - IB :]


def middle_kernel(
    f1_ref, f2s_ref, src_ref, diag_ref, dge_ref, mask_ref, *refs
):
    w_refs, (f2_ref, f3_ref) = refs[:-2], refs[-2:]
    w = Weights(w_refs)
    size = w.size
    rows = f3_ref.shape[1]
    first = f2s_ref.shape[2] // size
    mask = line_mask(mask_ref, size)
    dg_ref = (diag_ref, dge_ref)
    f1 = reader([(0, f1_ref)], size)
    for i in range(f2_ref.shape[2] // size):
        k = first + i
        new = relax_block(f1, stored_source(src_ref, k, size), dg_ref, w, k, mask)
        for c in range(2):
            f2_ref[c, :, i * size : (i + 1) * size] = new[c]
    f2 = reader([(0, f2s_ref), (first, f2_ref)], size)
    for k in range(f3_ref.shape[2] // size):
        new = relax_block(f2, stored_source(src_ref, k, size), dg_ref, w, k, mask)
        for c in range(2):
            f3_ref[c, :, k * size : (k + 1) * size] = new[c][PAD : PAD + rows]


def last_kernel(
    f2s_ref, f2_ref, f2e_ref, f3_ref, f3e_ref, src_ref, diag_ref, dge_ref, mask_ref, *refs
):
    w_refs, (out_ref, held_ref, sem) = refs[:-3], refs[-3:]
    w = Weights(w_refs)
    size, last = w.size, w.last
    rows = out_ref.shape[1]
    done = f3_ref.shape[2] // size
    mask = line_mask(mask_ref, size)

    def copy(ref, first, blocks, slot):
        cols = pl.ds(first * size, blocks * size)
        return pltpu.make_async_copy(ref, out_ref.at[:, :, cols], sem.at[slot])

    copies = [copy(f3_ref, 0, done, 0), copy(f3e_ref, last, 1, 1)]
    for one in copies:
        one.start()
    dg_ref = (diag_ref, dge_ref)
    f2 = reader([(last - 1, f2e_ref), (f2s_ref.shape[2] // size, f2_ref), (0, f2s_ref)], size)
    for i in range(last - done):
        k = done + i
        new = relax_block(f2, stored_source(src_ref, k, size), dg_ref, w, k, mask)
        for c in range(2):
            held_ref[i, c] = new[c][PAD : PAD + rows]
        copies.append(copy(held_ref.at[i], k, 1, 2 + i))
        copies[-1].start()
    for one in copies:
        one.wait()


def per_device(
    load_current,
    diagonal,
    start_field,
    block_inverse,
    multipliers,
    active_rows,
    contact_peer,
    contact_len,
    port_row,
    port_col,
    port_current,
):
    load, diag, start, mult = load_current[0], diagonal[0], start_field[0], multipliers[0]
    _, rows, width = load.shape
    nb, _, size, _, _ = block_inverse.shape[1:]
    high = rows + 2 * PAD
    step = 6 * high * (2 * size) ** 2

    fill, done = nb * 3 // 8, nb // 2
    count = lax.axis_size("sub")

    m1, m2, one, two, peers, mask = call(
        edges_kernel,
        (start, load, diag, mult, contact_peer, contact_len, active_rows),
        [ANY_SPEC] * 3 + [VMEM_SPEC] + [SMEM_SPEC] * 3,
        [held((2, PAD, IB))] * 2
        + [held((2, PAD, width // PAD * (PAD - 1)))] * 2
        + [held((2, rows + PAD, LANES), jnp.int32), held((high, LANES))],
        56 * MIB,
        [pltpu.VMEM((3, 2, 2, PAD, width), jnp.float32), pltpu.SemaphoreType.DMA((3, 2))],
    )
    m1, m2 = passed(CARRY[0], m1, m2)
    m1, m2 = swap_edges(m1, m2)
    one, two = swap_edges(one, two)
    (mask,) = passed(CARRY[1], mask)
    flat = flat_weights(block_inverse[0])
    chips = count // 2
    quarter = nb // 4
    w1, token = split_weights(flat, size, 0, quarter, mask)
    lines_mult = call(
        lines_kernel,
        (mult, m1, m2, token),
        [VMEM_SPEC] * 4,
        held((2, rows + PAD, IB)),
        MIB,
    )
    other = swap_cores(lines_mult)
    w2, token = split_weights(flat, size, quarter, quarter, token)
    half = held((chips // 2, *lines_mult.shape))
    keep, send = call(
        merge_kernel, (peers, lines_mult, other, token), [VMEM_SPEC] * 4, [half] * 2, 2 * MIB
    )
    got = over_bit(send, 1)
    w3, token = split_weights(flat, size, 2 * quarter, nb - 2 * quarter, keep)
    bit = 1
    while keep.shape[0] > 1:
        keep, send = call(fold_kernel, (keep, got, token), [VMEM_SPEC] * 3, halved(keep), 2 * MIB)
        bit *= 2
        got = over_bit(send, bit)
    incoming = [keep[0], got[0]]
    weights = (*w1, *w2, *w3)

    whole, some = held((2, high, width)), held((2, 2 * PAD, width))
    src, dge, f1, f0e = call(
        functools.partial(first_kernel, nb - 1),
        (start, load, diag, one, two, lines_mult, mask, port_row, port_col, port_current, *weights),
        [VMEM_SPEC] * 7 + [SMEM_SPEC] * 3 + [VMEM_SPEC] * len(weights),
        [whole, some, held((2, high, (nb - 1) * size)), some],
        4 * MIB,
        flops=step * (nb - 1),
    )
    f1e, f2s, f2e, f3e, far = call(
        functools.partial(far_kernel, len(incoming)),
        (start, f0e, f1, src, diag, dge, mask, *incoming, *weights),
        [VMEM_SPEC] * (7 + len(incoming) + len(weights)),
        [
            held((2, high, size)),
            held((2, high, fill * size)),
            held((2, high, 2 * size)),
            held((2, rows, size)),
            held((2, rows, IB)),
        ],
        4 * MIB,
        flops=step * (4 + fill),
    )
    ends = [to_chip(far, step) if step else far for step in range(count // 2)]
    f2, f3 = call(
        middle_kernel,
        (f1, f2s, src, diag, dge, mask, *weights),
        [VMEM_SPEC] * (6 + len(weights)),
        [held((2, high, (nb - 2 - fill) * size)), held((2, rows, done * size))],
        4 * MIB,
        flops=step * (nb - 2 - fill + done),
    )
    mine, theirs = call(
        sums_kernel, (peers, *ends), [VMEM_SPEC] * (1 + len(ends)), [held(far.shape)] * 2, MIB
    )
    theirs = swap_cores(theirs)
    solved = call(
        last_kernel,
        (f2s, f2, f2e, f3, f3e, src, diag, dge, mask, *weights),
        [VMEM_SPEC] * (9 + len(weights)),
        jax.ShapeDtypeStruct((2, rows, width), jnp.float32),
        4 * MIB + 8 * rows * width,
        [pltpu.VMEM((nb - 1 - done, 2, rows, size), jnp.float32), pltpu.SemaphoreType.DMA((nb + 1 - done,))],
        flops=step * (nb - 1 - done),
        out_specs=ANY_SPEC,
    )
    updated = mult + (f3[:, :, :IB] - (mine + theirs))
    return (solved[None], updated[None])


def solution(mesh):
    lines = P("sub", None, "tile", None)
    in_specs = (
        lines,
        lines,
        lines,
        P("sub", None, None, None, None, None),
        lines,
        P(),
        P(),
        P(),
        P("sub", None),
        P("sub", None),
        P("sub", None, None),
    )
    return jax.shard_map(
        per_device, mesh=mesh, in_specs=in_specs, out_specs=(lines, lines), check_vma=False
    )
```

```python
import functools

import jax
import jax.numpy as jnp
from jax import lax
from jax.experimental import pallas as pl
from jax.experimental.pallas import tpu as pltpu
from jax.sharding import PartitionSpec as P

IB = 128
PB = 128
SWEEPS = 3
LANES = 128
PAD = 8
CARRY = 4 * 10**10, 10**10
MIB = 1 << 20

VMEM_SPEC = pl.BlockSpec(memory_space=pltpu.VMEM)
SMEM_SPEC = pl.BlockSpec(memory_space=pltpu.SMEM)
ANY_SPEC = pl.BlockSpec(memory_space=pl.ANY)


def call(kernel, args, specs, outs, limit, scratch=(), flops=0, moved=0, out_specs=None, aliases=None):
    return pl.pallas_call(
        kernel,
        out_shape=outs,
        in_specs=specs,
        out_specs=out_specs or jax.tree.map(lambda _: VMEM_SPEC, outs),
        scratch_shapes=scratch,
        input_output_aliases=aliases or {},
        compiler_params=pltpu.CompilerParams(vmem_limit_bytes=limit),
        cost_estimate=pl.CostEstimate(flops=flops, bytes_accessed=moved, transcendentals=0),
    )(*args)


def held(shape, dtype=jnp.float32):
    return pltpu.VMEM(shape, dtype)


def line_peers(peer_ref, len_ref, s, lines):
    found = jnp.zeros(lines.shape, jnp.int32)
    start = jnp.int32(0)
    for c in range(peer_ref.shape[1]):
        end = start + len_ref[s, c]
        found = jnp.where((lines >= start) & (lines < end), peer_ref[s, c], found)
        start = end
    return found


def pick(hit, cells):
    return jnp.where(hit[None], cells, 0.0)


def split_halves(x):
    high = x.astype(jnp.bfloat16)
    return high, (x - high.astype(jnp.float32)).astype(jnp.bfloat16)


def weights_kernel(size, first, b_ref, _, hi_ref, lo_ref, token_ref):
    token_ref[...] = jnp.zeros_like(token_ref)
    both = 2 * size
    parts = both // LANES
    for k in range(hi_ref.shape[0]):
        for q in range(parts):
            piece, comp = divmod(q, 2)
            rows = pl.ds(comp * size + piece * LANES, LANES)
            high, low = split_halves(b_ref[first + k, pl.ds(q, both, parts), :].T)
            hi_ref[k, rows, :] = high
            lo_ref[k, rows, :] = low


def flat_weights(blocks):
    nb, _, size, _, _ = blocks.shape
    flat = blocks.reshape(nb, 2, size, 2, size // LANES, LANES).transpose(0, 1, 2, 4, 3, 5)
    return pltpu.with_memory_space_constraint(flat.reshape(nb, -1, LANES), pltpu.VMEM)


def split_weights(flat, size, first, count, after):
    shape = (count, 2 * size, 2 * size)
    high, low, token = call(
        functools.partial(weights_kernel, size, first),
        (flat, after),
        [VMEM_SPEC] * 2,
        [held(shape, jnp.bfloat16)] * 2 + [held((PAD, LANES))],
        2 * MIB,
        moved=count * size * size * 32,
    )
    return (high, low), token


def edges_kernel(
    start_hbm, load_hbm, diag_hbm, mult_ref, peer_ref, len_ref, active_ref,
    m1_ref, m2_ref, one_ref, two_ref, peers_ref, mask_ref, buf, sem,
):
    rows = start_hbm.shape[1]
    even = lax.rem(lax.axis_index("tile"), 2) == 0
    ends = (pl.ds(0, PAD), pl.ds(rows - PAD, PAD))
    copies = [
        pltpu.make_async_copy(ref.at[:, ends[e]], buf.at[i, e], sem.at[i, e])
        for i, ref in enumerate((start_hbm, load_hbm, diag_hbm))
        for e in range(2)
    ]
    for copy in copies:
        copy.start()
    for c in range(2):
        top, bottom = mult_ref[c, ends[0]], mult_ref[c, ends[1]]
        m1_ref[c] = jnp.where(even, bottom, top)
        m2_ref[c] = jnp.where(even, top, bottom)
    me = lax.axis_index("sub")
    first = lax.axis_index("tile") * rows
    at = lax.broadcasted_iota(jnp.int32, peers_ref.shape[1:], 0)
    lines = jnp.where(at < rows + PAD // 2, at, at - rows - PAD) + first
    peers_ref[0] = line_peers(peer_ref, len_ref, me, lines)
    peers_ref[1] = line_peers(peer_ref, len_ref, me + 1 - 2 * lax.rem(me, 2), lines)
    at = lax.broadcasted_iota(jnp.int32, mask_ref.shape, 0) + (first - PAD)
    mask_ref[...] = jnp.where((at >= 0) & (at < active_ref[me]), 1.0, 0.0)
    row = lax.broadcasted_iota(jnp.int32, (PAD, start_hbm.shape[2]), 0)
    for copy in copies:
        copy.wait()

    def lines_of(c, e, turns):
        field, load, diag = (pltpu.roll(buf[i, e, c], t, 0) if t else buf[i, e, c] for i, t in enumerate(turns))
        return jnp.where(row < 3, field, jnp.where(row < 5, load, diag))

    for c in range(2):
        top, bottom = pack_rows(lines_of(c, 0, (0, 3, 5))), pack_rows(lines_of(c, 1, (3, 5, 7)))
        one_ref[c] = jnp.where(even, bottom, top)
        two_ref[c] = jnp.where(even, top, bottom)


def pack_rows(cells):
    width = cells.shape[1] // PAD * (PAD - 1)
    ends = cells[:, width:]
    tail = jnp.concatenate([pltpu.roll(ends, PAD - 1 - r, 0) for r in range(PAD - 1)], axis=1)
    row = lax.broadcasted_iota(jnp.int32, tail.shape, 0)
    return jnp.where(row == PAD - 1, tail, cells[:, :width])


def unpack_rows(cells):
    step = cells.shape[1] // (PAD - 1)
    row = lax.broadcasted_iota(jnp.int32, (PAD, step), 0)
    ends = pltpu.roll(cells[:, :step], 1, 0)
    for r in range(1, PAD - 1):
        ends = jnp.where(row == r, pltpu.roll(cells[:, r * step : (r + 1) * step], r + 1, 0), ends)
    return jnp.concatenate([cells, ends], axis=1)


def pass_kernel(*refs):
    half = len(refs) // 2
    for ref, out in zip(refs[:half], refs[half:]):
        out[...] = ref[...]


def lines_kernel(mult_ref, one_ref, two_ref, _, out_ref):
    rows = mult_ref.shape[1]
    even = lax.rem(lax.axis_index("tile"), 2) == 0
    low = lax.broadcasted_iota(jnp.int32, (PAD, IB), 0) < PAD // 2
    for c in range(2):
        out_ref[c, :rows] = mult_ref[c]
        out_ref[c, rows:] = jnp.where(low == even, one_ref[c], two_ref[c])


def passed(cost, *arrays):
    return call(
        pass_kernel,
        arrays,
        [VMEM_SPEC] * len(arrays),
        [held(x.shape) for x in arrays],
        MIB,
        flops=cost,
        moved=10**6,
    )


def swaps(count):
    one = [(i, i ^ 1) for i in range(count)]
    two = [(i, ((i - 1) if i % 2 == 0 else (i + 1)) % count) for i in range(count)]
    return one, two


def swap_edges(one, two):
    first, second = swaps(lax.axis_size("tile"))
    return lax.ppermute(one, "tile", first), lax.ppermute(two, "tile", second)


def to_chip(cells, step):
    count = lax.axis_size("sub")
    return lax.ppermute(cells, "sub", [(i, (i + 2 * step) % count) for i in range(count)])


def swap_cores(cells):
    return lax.ppermute(cells, "sub", [(i, i ^ 1) for i in range(lax.axis_size("sub"))])


def merge_kernel(peers_ref, own_ref, other_ref, _, keep_ref, send_ref):
    me = lax.axis_index("sub")
    own, other = own_ref[...], other_ref[...]
    for x in range(2 * keep_ref.shape[0]):
        to = me ^ (2 * x)
        out = send_ref if x % 2 else keep_ref
        out[x // 2] = pick(peers_ref[0] == to, own) + pick(peers_ref[1] == to, other)


def fold_kernel(keep_ref, got_ref, _, next_ref, send_ref):
    for x in range(keep_ref.shape[0]):
        out = send_ref if x % 2 else next_ref
        out[x // 2] = keep_ref[x] + got_ref[x]


def halved(cells):
    shape = (cells.shape[0] // 2, *cells.shape[1:])
    return [held(shape), held(shape)]


def over_bit(cells, bit):
    return lax.ppermute(cells, "sub", [(i, i ^ (2 * bit)) for i in range(lax.axis_size("sub"))])


def sums_kernel(peers_ref, _, *refs):
    pieces, (mine_ref, theirs_ref) = refs[:-2], refs[-2:]
    me, count = lax.axis_index("sub"), 2 * len(pieces)
    rows = mine_ref.shape[1]
    mine = theirs = 0.0
    for j, piece in enumerate(pieces):
        cells = piece[...]
        s = lax.rem(me + count - 2 * j, count)
        mine += pick(peers_ref[0, :rows] == s, cells)
        theirs += pick(peers_ref[1, :rows] == s, cells)
    mine_ref[...] = mine
    theirs_ref[...] = theirs


class Weights:
    def __init__(self, refs):
        self.runs = list(zip(refs[::2], refs[1::2]))
        self.size = refs[0].shape[1] // 2
        self.last = sum(ref.shape[0] for ref in refs[::2]) - 1

    def part(self, k, low):
        for run in self.runs:
            if k < run[0].shape[0]:
                return run[low][k]
            k -= run[0].shape[0]

    def high(self, k):
        return self.part(k, 0)

    def low(self, k):
        return self.part(k, 1)


def line_mask(mask_ref, size):
    active = mask_ref[...] > 0.0
    return jnp.concatenate([active] * (size // LANES), axis=1)


def with_ends(own_ref, ends_ref, c, cols):
    return jnp.concatenate([ends_ref[c, :PAD, cols], own_ref[c, :, cols], ends_ref[c, PAD:, cols]], axis=0)


def reader(parts, size):
    def read(c, start, count):
        for first, ref in parts:
            if first * size <= start and start + count <= first * size + ref.shape[2]:
                return ref[c, :, start - first * size : start - first * size + count]

    return read


def tiles_of(read, c, k, size, last):
    mid = read(c, k * size, size)
    none = jnp.zeros((mid.shape[0], LANES), jnp.float32)
    left = read(c, k * size - LANES, LANES) if k > 0 else none
    right = read(c, (k + 1) * size, LANES) if k < last else none
    return mid, jnp.concatenate([left, mid, right], axis=1)


def relax_block(field, source, diag_ref, w, k, mask):
    size, last = w.size, w.last
    mids, sums = [], []
    for c in range(2):
        mid, wide = tiles_of(field, c, k, size, last)
        rows, width = wide.shape
        beside = (
            pltpu.roll(wide, 1, 1)[:, LANES : LANES + size]
            + pltpu.roll(wide, width - 1, 1)[:, LANES : LANES + size]
        )
        beside = beside + (pltpu.roll(mid, 1, 0) + pltpu.roll(mid, rows - 1, 0))
        mids.append(mid)
        sums.append(source(c) + beside)
    cols = slice(k * size, (k + 1) * size)
    d0, d1 = (with_ends(*diag_ref, c, cols) for c in range(2))
    r0 = sums[0] - (d0 * mids[0] - d1 * mids[1])
    r1 = sums[1] - (d0 * mids[1] + d1 * mids[0])
    high, low = split_halves(jnp.concatenate([r0, r1], axis=1))
    rows = high.shape[0]
    z = jnp.dot(
        jnp.concatenate([high, low], axis=0), w.high(k), preferred_element_type=jnp.float32
    )
    z = (z[:rows] + z[rows:]) + jnp.dot(high, w.low(k), preferred_element_type=jnp.float32)
    return [
        jnp.where(mask, mids[c] + z[:, c * size : (c + 1) * size], 0.0) for c in range(2)
    ]


def start_reader(start_ref, ends_ref, mask_ref):
    def read(c, start, count):
        cells = with_ends(start_ref, ends_ref, c, slice(start, start + count))
        return jnp.where(line_mask(mask_ref, count), cells, 0.0)

    return read


def stored_source(source, k, size):
    return lambda c: with_ends(*source, c, slice(k * size, (k + 1) * size))


def sweep(w, field, source, diag, mask_ref, first, count, out_ref):
    size = w.size
    mask = line_mask(mask_ref, size)
    rows = out_ref.shape[1]
    lines = slice(PAD, PAD + rows) if rows < mask.shape[0] else slice(0, rows)
    for i in range(count):
        k = first + i
        new = relax_block(field, stored_source(source, k, size), diag, w, k, mask)
        for c in range(2):
            out_ref[c, :, i * size : (i + 1) * size] = new[c][lines]


def source_kernel(load_ref, mult_ref, prow_ref, pcol_ref, pcur_ref, src_ref, srce_ref):
    _, rows, width = load_ref.shape
    tile = lax.axis_index("tile")
    src_ref[...] = load_ref[...]
    srce_ref[...] = jnp.zeros_like(srce_ref)
    for c in range(2):
        src_ref[c, :, :IB] -= mult_ref[c, :rows]
        srce_ref[c, :PAD, :IB] = -mult_ref[c, rows:]
        srce_ref[c, PAD:, :IB] = -mult_ref[c, rows:]
    span = PB + LANES
    at_row = lax.broadcasted_iota(jnp.int32, (PAD, span), 0)
    at_col = lax.broadcasted_iota(jnp.int32, (PAD, span), 1)
    for p in range(prow_ref.shape[1]):
        row = prow_ref[0, p] - tile * rows
        col = pcol_ref[0, p]
        base = pl.multiple_of(jnp.minimum(col // LANES * LANES, width - span), LANES)
        hits_col = (at_col >= col - base) & (at_col < col - base + PB)

        def add(ref, line, p=p, base=base, hits_col=hits_col):
            first = pl.multiple_of(line // PAD * PAD, PAD)
            for c in range(2):
                where = (c, pl.ds(first, PAD), pl.ds(base, span))
                hit = hits_col & (at_row == line - first)
                ref[where] = ref[where] + jnp.where(hit, pcur_ref[0, c, p], 0.0)

        @pl.when((row >= 0) & (row < rows))
        def _():
            add(src_ref, row)

        @pl.when((row >= -PAD) & (row < 0))
        def _():
            add(srce_ref, row + PAD)

        @pl.when((row >= rows) & (row < rows + PAD))
        def _():
            add(srce_ref, row - rows + PAD)


def first_kernel(
    start_ref, diag_ref, one_ref, two_ref, src_ref, add_ref, mask_ref, *refs
):
    w_refs, (srce_ref, dge_ref, f0e_ref, f1_ref) = refs[:-4], refs[-4:]
    w = Weights(w_refs)
    size = w.size
    even = lax.rem(lax.axis_index("tile"), 2) == 0
    for c in range(2):
        one, two = one_ref[c], two_ref[c]
        up = unpack_rows(jnp.where(even, two, one))
        down = unpack_rows(jnp.where(even, one, two))
        f0e_ref[c, :PAD] = pltpu.roll(up, 5, 0)
        f0e_ref[c, PAD:] = down
        dge_ref[c, :PAD] = pltpu.roll(up, 1, 0)
        dge_ref[c, PAD:] = pltpu.roll(down, 3, 0)
        srce_ref[c, :PAD] = add_ref[c, :PAD] + pltpu.roll(up, 3, 0)
        srce_ref[c, PAD:] = add_ref[c, PAD:] + pltpu.roll(down, 5, 0)
    sweep(
        w, start_reader(start_ref, f0e_ref, mask_ref), (src_ref, srce_ref), (diag_ref, dge_ref), mask_ref,
        0, f1_ref.shape[2] // size, f1_ref,
    )


def far_kernel(
    count, start_ref, f0e_ref, f1_ref, src_ref, srce_ref, diag_ref, dge_ref, mask_ref, *refs
):
    pieces, w_refs, (f1e_ref, f2s_ref, f2e_ref, f3e_ref, far_ref) = refs[:count], refs[count:-5], refs[-5:]
    w = Weights(w_refs)
    size, last = w.size, w.last
    rows = far_ref.shape[1]
    mask = line_mask(mask_ref, size)
    into = []
    for c in range(2):
        cells = pieces[0][c]
        for piece in pieces[1:]:
            cells += piece[c]
        ends = jnp.concatenate([cells[rows:], cells[:rows], cells[rows:]], axis=0)
        into.append(jnp.concatenate([jnp.zeros((rows + 2 * PAD, size - IB), jnp.float32), ends], axis=1))
    source, diag = (src_ref, srce_ref), (diag_ref, dge_ref)
    end = stored_source(source, last, size)

    def with_incoming(c):
        return end(c) + into[c]

    new = relax_block(start_reader(start_ref, f0e_ref, mask_ref), with_incoming, diag, w, last, mask)
    for c in range(2):
        f1e_ref[c] = new[c]
    old = reader([(0, f1_ref)], size)
    f1 = reader([(last, f1e_ref), (0, f1_ref)], size)
    fill = f2s_ref.shape[2] // size

    def beside(first, count):
        cols = pl.ds(first * size, count * size)
        sweep(w, old, source, diag, mask_ref, first, count, f2s_ref.at[:, :, cols])

    beside(0, fill // 2)
    for k, at in ((last, with_incoming), (last - 1, stored_source(source, last - 1, size))):
        new = relax_block(f1, at, diag, w, k, mask)
        for c in range(2):
            f2e_ref[c, :, (k - last + 1) * size : (k - last + 2) * size] = new[c]
    beside(fill // 2, fill - fill // 2)
    new = relax_block(reader([(last - 1, f2e_ref)], size), with_incoming, diag, w, last, mask)
    for c in range(2):
        f3e_ref[c] = new[c][PAD : PAD + rows]
        far_ref[c] = new[c][PAD : PAD + rows, size - IB :]


def middle_kernel(f1_ref, f2s_ref, src_ref, srce_ref, diag_ref, dge_ref, mask_ref, *refs):
    w_refs, (out_ref, f2_ref, f3_ref, sem) = refs[:-4], refs[-4:]
    w = Weights(w_refs)
    size = w.size
    first, done = f2s_ref.shape[2] // size, f3_ref.shape[2] // size
    early = first - 1
    source, diag = (src_ref, srce_ref), (diag_ref, dge_ref)
    f1 = reader([(0, f1_ref)], size)
    f2 = reader([(0, f2s_ref), (first, f2_ref)], size)
    sweep(w, f2, source, diag, mask_ref, 0, early, f3_ref.at[:, :, pl.ds(0, early * size)])
    copies = [block_copy(f3_ref, k, out_ref, k, size, sem.at[k]) for k in range(early)]
    for copy in copies:
        copy.start()
    sweep(w, f1, source, diag, mask_ref, first, f2_ref.shape[2] // size, f2_ref)
    rest = pl.ds(early * size, (done - early) * size)
    sweep(w, f2, source, diag, mask_ref, early, done - early, f3_ref.at[:, :, rest])
    for copy in copies:
        copy.wait()


def block_copy(ref, k, out_ref, at, size, sem):
    return pltpu.make_async_copy(
        ref.at[:, :, pl.ds(k * size, size)], out_ref.at[:, :, pl.ds(at * size, size)], sem
    )


def third_kernel(early, _, f2s_ref, f2_ref, f3_ref, src_ref, srce_ref, diag_ref, dge_ref, mask_ref, _after, *refs):
    w_refs, (out_ref, more_ref, sem) = refs[:-3], refs[-3:]
    w = Weights(w_refs)
    size = w.size
    first = f3_ref.shape[2] // size
    source, diag = (src_ref, srce_ref), (diag_ref, dge_ref)
    copies = [block_copy(f3_ref, k, out_ref, k, size, sem.at[k]) for k in range(early, first)]
    for copy in copies:
        copy.start()
    f2 = reader([(f2s_ref.shape[2] // size, f2_ref), (0, f2s_ref)], size)
    sweep(w, f2, source, diag, mask_ref, first, more_ref.shape[2] // size, more_ref)
    for copy in copies:
        copy.wait()


def last_kernel(
    f2_first, _, f2_ref, f2e_ref, near_ref, f3_ref, f3e_ref, src_ref, srce_ref, diag_ref, dge_ref, mask_ref,
    mult_ref, mine_ref, theirs_ref, *refs,
):
    w_refs, (out_ref, next_ref, held_ref, new_ref, sem) = refs[:-5], refs[-5:]
    w = Weights(w_refs)
    size, last = w.size, w.last
    count = held_ref.shape[0]
    first = last - count
    source, diag = (src_ref, srce_ref), (diag_ref, dge_ref)
    more = f3_ref.shape[2] // size
    copies = [block_copy(f3_ref, k, out_ref, first - more + k, size, sem.at[k]) for k in range(more)]
    copies.append(block_copy(f3e_ref, 0, out_ref, last, size, sem.at[more]))
    for copy in copies:
        copy.start()
    new_ref[...] = mult_ref[...] + (near_ref[:, :, :IB] - (mine_ref[...] + theirs_ref[...]))
    copies.append(pltpu.make_async_copy(new_ref, next_ref, sem.at[more + 1]))
    copies[-1].start()
    f2 = reader([(last - 1, f2e_ref), (f2_first, f2_ref)], size)
    for i in range(count):
        sweep(w, f2, source, diag, mask_ref, first + i, 1, held_ref.at[i])
        copies.append(block_copy(held_ref.at[i], 0, out_ref, first + i, size, sem.at[more + 2 + i]))
        copies[-1].start()
    for copy in copies:
        copy.wait()


def per_device(
    load_current,
    diagonal,
    start_field,
    block_inverse,
    multipliers,
    active_rows,
    contact_peer,
    contact_len,
    port_row,
    port_col,
    port_current,
):
    load, diag, start, mult = load_current[0], diagonal[0], start_field[0], multipliers[0]
    _, rows, width = load.shape
    nb, _, size, _, _ = block_inverse.shape[1:]
    high = rows + 2 * PAD

    count = lax.axis_size("sub")

    m1, m2, one, two, peers, mask = call(
        edges_kernel,
        (start, load, diag, mult, contact_peer, contact_len, active_rows),
        [ANY_SPEC] * 3 + [VMEM_SPEC] + [SMEM_SPEC] * 3,
        [held((2, PAD, IB))] * 2
        + [held((2, PAD, width // PAD * (PAD - 1)))] * 2
        + [held((2, rows + PAD, LANES), jnp.int32), held((high, LANES))],
        56 * MIB,
        [pltpu.VMEM((3, 2, 2, PAD, width), jnp.float32), pltpu.SemaphoreType.DMA((3, 2))],
    )
    m1, m2 = passed(CARRY[0], m1, m2)
    m1, m2 = swap_edges(m1, m2)
    one, two = swap_edges(one, two)
    (mask,) = passed(CARRY[1], mask)
    flat = flat_weights(block_inverse[0])
    chips = count // 2
    quarter = nb // 4
    w1, token = split_weights(flat, size, 0, quarter, mask)
    lines_mult = call(
        lines_kernel,
        (mult, m1, m2, token),
        [VMEM_SPEC] * 4,
        held((2, rows + PAD, IB)),
        MIB,
    )
    other = swap_cores(lines_mult)
    w2, token = split_weights(flat, size, quarter, quarter, token)
    half = held((chips // 2, *lines_mult.shape))
    keep, send = call(
        merge_kernel, (peers, lines_mult, other, token), [VMEM_SPEC] * 4, [half] * 2, 2 * MIB
    )
    got = over_bit(send, 1)
    w3, token = split_weights(flat, size, 2 * quarter, nb - 2 * quarter, keep)
    weights = (*w1, *w2, *w3)
    step = 6 * high * (2 * size) ** 2
    some = held((2, 2 * PAD, width))

    src, add = call(
        source_kernel,
        (load, lines_mult, port_row, port_col, port_current),
        [VMEM_SPEC] * 2 + [SMEM_SPEC] * 3,
        [held(load.shape), some],
        2 * MIB,
        moved=8 * MIB,
    )

    def run(kernel, args, outs, blocks, limit=4 * MIB, scratch=(), out_specs=None, aliased=False):
        operands = (*args, *weights)
        specs = [VMEM_SPEC] * len(operands)
        if aliased:
            specs[0] = ANY_SPEC
        return call(
            kernel, operands, specs, outs, limit, scratch, step * blocks, 0, out_specs, {0: 0} if aliased else {}
        )

    bit = 1
    while keep.shape[0] > 1:
        keep, send = call(fold_kernel, (keep, got, token), [VMEM_SPEC] * 3, halved(keep), 2 * MIB)
        bit *= 2
        got = over_bit(send, bit)
    incoming = [keep[0], got[0]]
    srce, dge, f0e, f1 = run(
        first_kernel,
        (start, diag, one, two, src, add, mask),
        [some, some, some, held((2, high, (nb - 1) * size))],
        nb - 1,
    )
    known = (src, srce, diag, dge, mask)
    fill = nb * 3 // 8
    f1e, f2s, f2e, f3e, far = run(
        functools.partial(far_kernel, len(incoming)),
        (start, f0e, f1, *known, *incoming),
        [
            held((2, high, size)),
            held((2, high, fill * size)),
            held((2, high, 2 * size)),
            held((2, rows, size)),
            held((2, rows, IB)),
        ],
        4 + fill,
    )
    ends = [to_chip(far, step) if step else far for step in range(chips)]
    done, tail = nb * 5 // 8, nb // 8
    whole = jax.ShapeDtypeStruct((2, rows, width), jnp.float32)
    partly, f2, f3a = run(
        middle_kernel,
        (f1, f2s, *known),
        [whole, held((2, high, (nb - 2 - fill) * size)), held((2, rows, done * size))],
        nb - 2 - fill + done,
        scratch=[pltpu.SemaphoreType.DMA((fill - 1,))],
        out_specs=[ANY_SPEC, VMEM_SPEC, VMEM_SPEC],
    )
    mine, theirs = call(
        sums_kernel, (peers, f3a, *ends), [VMEM_SPEC] * (2 + len(ends)), [held(far.shape)] * 2, MIB
    )
    theirs = swap_cores(theirs)
    more = nb - 1 - tail - done
    partly, f3b = run(
        functools.partial(third_kernel, fill - 1),
        (partly, f2s, f2, f3a, *known, mine),
        [whole, held((2, rows, more * size))],
        more,
        scratch=[pltpu.SemaphoreType.DMA((done,))],
        out_specs=[ANY_SPEC, VMEM_SPEC],
        aliased=True,
    )
    solved, updated = run(
        functools.partial(last_kernel, fill),
        (partly, f2, f2e, f3a, f3b, f3e, *known, mult, mine, theirs),
        [whole, jax.ShapeDtypeStruct(mult.shape, jnp.float32)],
        tail,
        scratch=[
            pltpu.VMEM((tail, 2, rows, size), jnp.float32),
            pltpu.VMEM(mult.shape, jnp.float32),
            pltpu.SemaphoreType.DMA((2 + more + tail,)),
        ],
        out_specs=[ANY_SPEC] * 2,
        aliased=True,
    )
    return (solved[None], updated[None])


def solution(mesh):
    lines = P("sub", None, "tile", None)
    in_specs = (
        lines,
        lines,
        lines,
        P("sub", None, None, None, None, None),
        lines,
        P(),
        P(),
        P(),
        P("sub", None),
        P("sub", None),
        P("sub", None, None),
    )
    return jax.shard_map(
        per_device, mesh=mesh, in_specs=in_specs, out_specs=(lines, lines), check_vma=False
    )
```

```python
import functools

import jax
import jax.numpy as jnp
from jax import lax
from jax.experimental import pallas as pl
from jax.experimental.pallas import tpu as pltpu
from jax.sharding import PartitionSpec as P

IB = 128
PB = 128
SWEEPS = 3
LANES = 128
PAD = 8
CARRY = 4 * 10**10, 10**10
MIB = 1 << 20

VMEM_SPEC = pl.BlockSpec(memory_space=pltpu.VMEM)
SMEM_SPEC = pl.BlockSpec(memory_space=pltpu.SMEM)
ANY_SPEC = pl.BlockSpec(memory_space=pl.ANY)


def call(kernel, args, specs, outs, limit, scratch=(), flops=0, moved=0, out_specs=None, aliases=None):
    return pl.pallas_call(
        kernel,
        out_shape=outs,
        in_specs=specs,
        out_specs=out_specs or jax.tree.map(lambda _: VMEM_SPEC, outs),
        scratch_shapes=scratch,
        input_output_aliases=aliases or {},
        compiler_params=pltpu.CompilerParams(vmem_limit_bytes=limit),
        cost_estimate=pl.CostEstimate(flops=flops, bytes_accessed=moved, transcendentals=0),
    )(*args)


def held(shape, dtype=jnp.float32):
    return pltpu.VMEM(shape, dtype)


def line_peers(peer_ref, len_ref, s, lines):
    found = jnp.zeros(lines.shape, jnp.int32)
    start = jnp.int32(0)
    for c in range(peer_ref.shape[1]):
        end = start + len_ref[s, c]
        found = jnp.where((lines >= start) & (lines < end), peer_ref[s, c], found)
        start = end
    return found


def pick(hit, cells):
    return jnp.where(hit[None], cells, 0.0)


def split_halves(x):
    high = x.astype(jnp.bfloat16)
    return high, (x - high.astype(jnp.float32)).astype(jnp.bfloat16)


def weights_kernel(size, first, b_ref, _, hi_ref, lo_ref, token_ref):
    token_ref[...] = jnp.zeros_like(token_ref)
    both = 2 * size
    parts = both // LANES
    for k in range(hi_ref.shape[0]):
        for q in range(parts):
            piece, comp = divmod(q, 2)
            rows = pl.ds(comp * size + piece * LANES, LANES)
            high, low = split_halves(b_ref[first + k, pl.ds(q, both, parts), :].T)
            hi_ref[k, rows, :] = high
            lo_ref[k, rows, :] = low


def flat_weights(blocks):
    nb, _, size, _, _ = blocks.shape
    flat = blocks.reshape(nb, 2, size, 2, size // LANES, LANES).transpose(0, 1, 2, 4, 3, 5)
    return pltpu.with_memory_space_constraint(flat.reshape(nb, -1, LANES), pltpu.VMEM)


def split_weights(flat, size, first, count, after):
    shape = (count, 2 * size, 2 * size)
    high, low, token = call(
        functools.partial(weights_kernel, size, first),
        (flat, after),
        [VMEM_SPEC] * 2,
        [held(shape, jnp.bfloat16)] * 2 + [held((PAD, LANES))],
        2 * MIB,
        moved=count * size * size * 32,
    )
    return (high, low), token


def edges_kernel(
    start_hbm, load_hbm, diag_hbm, mult_ref, peer_ref, len_ref, active_ref,
    m1_ref, m2_ref, one_ref, two_ref, peers_ref, mask_ref, buf, sem,
):
    rows = start_hbm.shape[1]
    even = lax.rem(lax.axis_index("tile"), 2) == 0
    ends = (pl.ds(0, PAD), pl.ds(rows - PAD, PAD))
    copies = [
        pltpu.make_async_copy(ref.at[:, ends[e]], buf.at[i, e], sem.at[i, e])
        for i, ref in enumerate((start_hbm, load_hbm, diag_hbm))
        for e in range(2)
    ]
    for copy in copies:
        copy.start()
    for c in range(2):
        top, bottom = mult_ref[c, ends[0]], mult_ref[c, ends[1]]
        m1_ref[c] = jnp.where(even, bottom, top)
        m2_ref[c] = jnp.where(even, top, bottom)
    me = lax.axis_index("sub")
    first = lax.axis_index("tile") * rows
    at = lax.broadcasted_iota(jnp.int32, peers_ref.shape[1:], 0)
    lines = jnp.where(at < rows + PAD // 2, at, at - rows - PAD) + first
    peers_ref[0] = line_peers(peer_ref, len_ref, me, lines)
    peers_ref[1] = line_peers(peer_ref, len_ref, me + 1 - 2 * lax.rem(me, 2), lines)
    at = lax.broadcasted_iota(jnp.int32, mask_ref.shape, 0) + (first - PAD)
    mask_ref[...] = jnp.where((at >= 0) & (at < active_ref[me]), 1.0, 0.0)
    row = lax.broadcasted_iota(jnp.int32, (PAD, start_hbm.shape[2]), 0)
    for copy in copies:
        copy.wait()

    def lines_of(c, e, turns):
        field, load, diag = (pltpu.roll(buf[i, e, c], t, 0) if t else buf[i, e, c] for i, t in enumerate(turns))
        return jnp.where(row < 3, field, jnp.where(row < 5, load, diag))

    for c in range(2):
        top, bottom = pack_rows(lines_of(c, 0, (0, 3, 5))), pack_rows(lines_of(c, 1, (3, 5, 7)))
        one_ref[c] = jnp.where(even, bottom, top)
        two_ref[c] = jnp.where(even, top, bottom)


def pack_rows(cells):
    width = cells.shape[1] // PAD * (PAD - 1)
    ends = cells[:, width:]
    tail = jnp.concatenate([pltpu.roll(ends, PAD - 1 - r, 0) for r in range(PAD - 1)], axis=1)
    row = lax.broadcasted_iota(jnp.int32, tail.shape, 0)
    return jnp.where(row == PAD - 1, tail, cells[:, :width])


def unpack_rows(cells):
    step = cells.shape[1] // (PAD - 1)
    row = lax.broadcasted_iota(jnp.int32, (PAD, step), 0)
    ends = pltpu.roll(cells[:, :step], 1, 0)
    for r in range(1, PAD - 1):
        ends = jnp.where(row == r, pltpu.roll(cells[:, r * step : (r + 1) * step], r + 1, 0), ends)
    return jnp.concatenate([cells, ends], axis=1)


def pass_kernel(*refs):
    half = len(refs) // 2
    for ref, out in zip(refs[:half], refs[half:]):
        out[...] = ref[...]


def lines_kernel(mult_ref, one_ref, two_ref, _, out_ref):
    rows = mult_ref.shape[1]
    even = lax.rem(lax.axis_index("tile"), 2) == 0
    low = lax.broadcasted_iota(jnp.int32, (PAD, IB), 0) < PAD // 2
    for c in range(2):
        out_ref[c, :rows] = mult_ref[c]
        out_ref[c, rows:] = jnp.where(low == even, one_ref[c], two_ref[c])


def passed(cost, *arrays):
    return call(
        pass_kernel,
        arrays,
        [VMEM_SPEC] * len(arrays),
        [held(x.shape) for x in arrays],
        MIB,
        flops=cost,
        moved=10**6,
    )


def swaps(count):
    one = [(i, i ^ 1) for i in range(count)]
    two = [(i, ((i - 1) if i % 2 == 0 else (i + 1)) % count) for i in range(count)]
    return one, two


def swap_edges(one, two):
    first, second = swaps(lax.axis_size("tile"))
    return lax.ppermute(one, "tile", first), lax.ppermute(two, "tile", second)


def to_chip(cells, step):
    count = lax.axis_size("sub")
    return lax.ppermute(cells, "sub", [(i, (i + 2 * step) % count) for i in range(count)])


def swap_cores(cells):
    return lax.ppermute(cells, "sub", [(i, i ^ 1) for i in range(lax.axis_size("sub"))])


def merge_kernel(peers_ref, own_ref, other_ref, _, keep_ref, send_ref):
    me = lax.axis_index("sub")
    own, other = own_ref[...], other_ref[...]
    for x in range(2 * keep_ref.shape[0]):
        to = me ^ (2 * x)
        out = send_ref if x % 2 else keep_ref
        out[x // 2] = pick(peers_ref[0] == to, own) + pick(peers_ref[1] == to, other)


def fold_kernel(keep_ref, got_ref, _, next_ref, send_ref):
    for x in range(keep_ref.shape[0]):
        out = send_ref if x % 2 else next_ref
        out[x // 2] = keep_ref[x] + got_ref[x]


def halved(cells):
    shape = (cells.shape[0] // 2, *cells.shape[1:])
    return [held(shape), held(shape)]


def over_bit(cells, bit):
    return lax.ppermute(cells, "sub", [(i, i ^ (2 * bit)) for i in range(lax.axis_size("sub"))])


def sums_kernel(peers_ref, _, *refs):
    pieces, (mine_ref, theirs_ref) = refs[:-2], refs[-2:]
    me, count = lax.axis_index("sub"), 2 * len(pieces)
    rows = mine_ref.shape[1]
    mine = theirs = 0.0
    for j, piece in enumerate(pieces):
        cells = piece[...]
        s = lax.rem(me + count - 2 * j, count)
        mine += pick(peers_ref[0, :rows] == s, cells)
        theirs += pick(peers_ref[1, :rows] == s, cells)
    mine_ref[...] = mine
    theirs_ref[...] = theirs


class Weights:
    def __init__(self, refs):
        self.runs = list(zip(refs[::2], refs[1::2]))
        self.size = refs[0].shape[1] // 2
        self.last = sum(ref.shape[0] for ref in refs[::2]) - 1

    def part(self, k, low):
        for run in self.runs:
            if k < run[0].shape[0]:
                return run[low][k]
            k -= run[0].shape[0]

    def high(self, k):
        return self.part(k, 0)

    def low(self, k):
        return self.part(k, 1)


def line_mask(mask_ref, size):
    active = mask_ref[...] > 0.0
    return jnp.concatenate([active] * (size // LANES), axis=1)


def with_ends(own_ref, ends_ref, c, cols):
    return jnp.concatenate([ends_ref[c, :PAD, cols], own_ref[c, :, cols], ends_ref[c, PAD:, cols]], axis=0)


def reader(parts, size):
    def read(c, start, count):
        for first, ref in parts:
            if first * size <= start and start + count <= first * size + ref.shape[2]:
                return ref[c, :, start - first * size : start - first * size + count]

    return read


def tiles_of(read, c, k, size, last):
    mid = read(c, k * size, size)
    none = jnp.zeros((mid.shape[0], LANES), jnp.float32)
    left = read(c, k * size - LANES, LANES) if k > 0 else none
    right = read(c, (k + 1) * size, LANES) if k < last else none
    return mid, jnp.concatenate([left, mid, right], axis=1)


def relax_block(field, source, diag_ref, w, k, mask):
    size, last = w.size, w.last
    mids, sums = [], []
    for c in range(2):
        mid, wide = tiles_of(field, c, k, size, last)
        rows, width = wide.shape
        beside = (
            pltpu.roll(wide, 1, 1)[:, LANES : LANES + size]
            + pltpu.roll(wide, width - 1, 1)[:, LANES : LANES + size]
        )
        beside = beside + (pltpu.roll(mid, 1, 0) + pltpu.roll(mid, rows - 1, 0))
        mids.append(mid)
        sums.append(source(c) + beside)
    cols = slice(k * size, (k + 1) * size)
    d0, d1 = (with_ends(*diag_ref, c, cols) for c in range(2))
    r0 = sums[0] - (d0 * mids[0] - d1 * mids[1])
    r1 = sums[1] - (d0 * mids[1] + d1 * mids[0])
    high, low = split_halves(jnp.concatenate([r0, r1], axis=1))
    rows = high.shape[0]
    z = jnp.dot(
        jnp.concatenate([high, low], axis=0), w.high(k), preferred_element_type=jnp.float32
    )
    z = (z[:rows] + z[rows:]) + jnp.dot(high, w.low(k), preferred_element_type=jnp.float32)
    return [
        jnp.where(mask, mids[c] + z[:, c * size : (c + 1) * size], 0.0) for c in range(2)
    ]


def start_reader(start_ref, ends_ref, mask_ref):
    def read(c, start, count):
        cells = with_ends(start_ref, ends_ref, c, slice(start, start + count))
        return jnp.where(line_mask(mask_ref, count), cells, 0.0)

    return read


def stored_source(source, k, size):
    return lambda c: with_ends(*source, c, slice(k * size, (k + 1) * size))


def sweep(w, field, source, diag, mask_ref, first, count, out_ref):
    size = w.size
    mask = line_mask(mask_ref, size)
    rows = out_ref.shape[1]
    lines = slice(PAD, PAD + rows) if rows < mask.shape[0] else slice(0, rows)
    for i in range(count):
        k = first + i
        new = relax_block(field, stored_source(source, k, size), diag, w, k, mask)
        for c in range(2):
            out_ref[c, :, i * size : (i + 1) * size] = new[c][lines]


def source_kernel(load_ref, mult_ref, prow_ref, pcol_ref, pcur_ref, src_ref, srce_ref):
    _, rows, width = load_ref.shape
    tile = lax.axis_index("tile")
    src_ref[...] = load_ref[...]
    srce_ref[...] = jnp.zeros_like(srce_ref)
    for c in range(2):
        src_ref[c, :, :IB] -= mult_ref[c, :rows]
        srce_ref[c, :PAD, :IB] = -mult_ref[c, rows:]
        srce_ref[c, PAD:, :IB] = -mult_ref[c, rows:]
    span = PB + LANES
    at_row = lax.broadcasted_iota(jnp.int32, (PAD, span), 0)
    at_col = lax.broadcasted_iota(jnp.int32, (PAD, span), 1)
    for p in range(prow_ref.shape[1]):
        row = prow_ref[0, p] - tile * rows
        col = pcol_ref[0, p]
        base = pl.multiple_of(jnp.minimum(col // LANES * LANES, width - span), LANES)
        hits_col = (at_col >= col - base) & (at_col < col - base + PB)

        def add(ref, line, p=p, base=base, hits_col=hits_col):
            first = pl.multiple_of(line // PAD * PAD, PAD)
            for c in range(2):
                where = (c, pl.ds(first, PAD), pl.ds(base, span))
                hit = hits_col & (at_row == line - first)
                ref[where] = ref[where] + jnp.where(hit, pcur_ref[0, c, p], 0.0)

        @pl.when((row >= 0) & (row < rows))
        def _():
            add(src_ref, row)

        @pl.when((row >= -PAD) & (row < 0))
        def _():
            add(srce_ref, row + PAD)

        @pl.when((row >= rows) & (row < rows + PAD))
        def _():
            add(srce_ref, row - rows + PAD)


def first_kernel(
    start_ref, diag_ref, one_ref, two_ref, src_ref, add_ref, mask_ref, *refs
):
    w_refs, (srce_ref, dge_ref, f0e_ref, f1_ref) = refs[:-4], refs[-4:]
    w = Weights(w_refs)
    size = w.size
    even = lax.rem(lax.axis_index("tile"), 2) == 0
    for c in range(2):
        one, two = one_ref[c], two_ref[c]
        up = unpack_rows(jnp.where(even, two, one))
        down = unpack_rows(jnp.where(even, one, two))
        f0e_ref[c, :PAD] = pltpu.roll(up, 5, 0)
        f0e_ref[c, PAD:] = down
        dge_ref[c, :PAD] = pltpu.roll(up, 1, 0)
        dge_ref[c, PAD:] = pltpu.roll(down, 3, 0)
        srce_ref[c, :PAD] = add_ref[c, :PAD] + pltpu.roll(up, 3, 0)
        srce_ref[c, PAD:] = add_ref[c, PAD:] + pltpu.roll(down, 5, 0)
    sweep(
        w, start_reader(start_ref, f0e_ref, mask_ref), (src_ref, srce_ref), (diag_ref, dge_ref), mask_ref,
        0, f1_ref.shape[2] // size, f1_ref,
    )


def far_kernel(
    count, start_ref, f0e_ref, f1_ref, src_ref, srce_ref, diag_ref, dge_ref, mask_ref, *refs
):
    pieces, w_refs, (f2s_ref, f2e_ref, f3e_ref, far_ref, f1e_ref) = refs[:count], refs[count:-5], refs[-5:]
    w = Weights(w_refs)
    size, last = w.size, w.last
    rows = far_ref.shape[1]
    mask = line_mask(mask_ref, size)
    into = []
    for c in range(2):
        cells = pieces[0][c]
        for piece in pieces[1:]:
            cells += piece[c]
        ends = jnp.concatenate([cells[rows:], cells[:rows], cells[rows:]], axis=0)
        into.append(jnp.concatenate([jnp.zeros((rows + 2 * PAD, size - IB), jnp.float32), ends], axis=1))
    source, diag = (src_ref, srce_ref), (diag_ref, dge_ref)
    end = stored_source(source, last, size)

    def with_incoming(c):
        return end(c) + into[c]

    new = relax_block(start_reader(start_ref, f0e_ref, mask_ref), with_incoming, diag, w, last, mask)
    for c in range(2):
        f1e_ref[c] = new[c]
    old = reader([(0, f1_ref)], size)
    f1 = reader([(last, f1e_ref), (0, f1_ref)], size)
    fill = f2s_ref.shape[2] // size

    def beside(first, count):
        cols = pl.ds(first * size, count * size)
        sweep(w, old, source, diag, mask_ref, first, count, f2s_ref.at[:, :, cols])

    beside(0, fill // 2)
    for k, at in ((last, with_incoming), (last - 1, stored_source(source, last - 1, size))):
        new = relax_block(f1, at, diag, w, k, mask)
        for c in range(2):
            f2e_ref[c, :, (k - last + 1) * size : (k - last + 2) * size] = new[c]
    beside(fill // 2, fill - fill // 2)
    new = relax_block(reader([(last - 1, f2e_ref)], size), with_incoming, diag, w, last, mask)
    for c in range(2):
        f3e_ref[c] = new[c][PAD : PAD + rows]
        far_ref[c] = new[c][PAD : PAD + rows, size - IB :]


def middle_kernel(f1_ref, f2s_ref, src_ref, srce_ref, diag_ref, dge_ref, mask_ref, *refs):
    w_refs, (out_ref, f2_ref, f3_ref, sem) = refs[:-4], refs[-4:]
    w = Weights(w_refs)
    size = w.size
    first, done = f2s_ref.shape[2] // size, f3_ref.shape[2] // size
    early = first - 1
    source, diag = (src_ref, srce_ref), (diag_ref, dge_ref)
    f1 = reader([(0, f1_ref)], size)
    f2 = reader([(0, f2s_ref), (first, f2_ref)], size)
    sweep(w, f2, source, diag, mask_ref, 0, early, f3_ref.at[:, :, pl.ds(0, early * size)])
    copies = [block_copy(f3_ref, k, out_ref, k, size, sem.at[k]) for k in range(early)]
    for copy in copies:
        copy.start()
    sweep(w, f1, source, diag, mask_ref, first, f2_ref.shape[2] // size, f2_ref)
    rest = pl.ds(early * size, (done - early) * size)
    sweep(w, f2, source, diag, mask_ref, early, done - early, f3_ref.at[:, :, rest])
    for copy in copies:
        copy.wait()


def block_copy(ref, k, out_ref, at, size, sem):
    return pltpu.make_async_copy(
        ref.at[:, :, pl.ds(k * size, size)], out_ref.at[:, :, pl.ds(at * size, size)], sem
    )


def third_kernel(first, f2s_ref, f2_ref, f2e_ref, src_ref, srce_ref, diag_ref, dge_ref, mask_ref, _, *refs):
    w_refs, f3_ref = refs[:-1], refs[-1]
    w = Weights(w_refs)
    size = w.size
    source, diag = (src_ref, srce_ref), (diag_ref, dge_ref)
    f2 = reader([(w.last - 1, f2e_ref), (f2s_ref.shape[2] // size, f2_ref), (0, f2s_ref)], size)
    sweep(w, f2, source, diag, mask_ref, first, f3_ref.shape[2] // size, f3_ref)


def last_kernel(
    f2_first, early, _, f2_ref, f2e_ref, f3_ref, more_ref, f3e_ref, src_ref, srce_ref, diag_ref, dge_ref, mask_ref,
    mult_ref, mine_ref, theirs_ref, *refs,
):
    w_refs, (out_ref, next_ref, held_ref, new_ref, sem) = refs[:-5], refs[-5:]
    w = Weights(w_refs)
    size, last = w.size, w.last
    count = held_ref.shape[0]
    first = last - count
    source, diag = (src_ref, srce_ref), (diag_ref, dge_ref)
    done = f3_ref.shape[2] // size
    copies = [block_copy(f3_ref, k, out_ref, k, size, sem.at[k]) for k in range(early, done)]
    copies += [block_copy(more_ref, k - done, out_ref, k, size, sem.at[k]) for k in range(done, first)]
    copies.append(block_copy(f3e_ref, 0, out_ref, last, size, sem.at[last]))
    for copy in copies:
        copy.start()
    new_ref[...] = mult_ref[...] + (f3_ref[:, :, :IB] - (mine_ref[...] + theirs_ref[...]))
    copies.append(pltpu.make_async_copy(new_ref, next_ref, sem.at[last + 1]))
    copies[-1].start()
    f2 = reader([(last - 1, f2e_ref), (f2_first, f2_ref)], size)
    for i in range(count):
        sweep(w, f2, source, diag, mask_ref, first + i, 1, held_ref.at[i])
        copies.append(block_copy(held_ref.at[i], 0, out_ref, first + i, size, sem.at[first + i]))
        copies[-1].start()
    for copy in copies:
        copy.wait()


def per_device(
    load_current,
    diagonal,
    start_field,
    block_inverse,
    multipliers,
    active_rows,
    contact_peer,
    contact_len,
    port_row,
    port_col,
    port_current,
):
    load, diag, start, mult = load_current[0], diagonal[0], start_field[0], multipliers[0]
    _, rows, width = load.shape
    nb, _, size, _, _ = block_inverse.shape[1:]
    high = rows + 2 * PAD

    count = lax.axis_size("sub")

    m1, m2, one, two, peers, mask = call(
        edges_kernel,
        (start, load, diag, mult, contact_peer, contact_len, active_rows),
        [ANY_SPEC] * 3 + [VMEM_SPEC] + [SMEM_SPEC] * 3,
        [held((2, PAD, IB))] * 2
        + [held((2, PAD, width // PAD * (PAD - 1)))] * 2
        + [held((2, rows + PAD, LANES), jnp.int32), held((high, LANES))],
        56 * MIB,
        [pltpu.VMEM((3, 2, 2, PAD, width), jnp.float32), pltpu.SemaphoreType.DMA((3, 2))],
    )
    m1, m2 = passed(CARRY[0], m1, m2)
    m1, m2 = swap_edges(m1, m2)
    one, two = swap_edges(one, two)
    (mask,) = passed(CARRY[1], mask)
    flat = flat_weights(block_inverse[0])
    chips = count // 2
    quarter = nb // 4
    w1, token = split_weights(flat, size, 0, quarter, mask)
    lines_mult = call(
        lines_kernel,
        (mult, m1, m2, token),
        [VMEM_SPEC] * 4,
        held((2, rows + PAD, IB)),
        MIB,
    )
    other = swap_cores(lines_mult)
    w2, token = split_weights(flat, size, quarter, quarter, token)
    half = held((chips // 2, *lines_mult.shape))
    keep, send = call(
        merge_kernel, (peers, lines_mult, other, token), [VMEM_SPEC] * 4, [half] * 2, 2 * MIB
    )
    got = over_bit(send, 1)
    w3, token = split_weights(flat, size, 2 * quarter, nb - 2 * quarter, keep)
    weights = (*w1, *w2, *w3)
    step = 6 * high * (2 * size) ** 2
    some = held((2, 2 * PAD, width))

    src, add = call(
        source_kernel,
        (load, lines_mult, port_row, port_col, port_current),
        [VMEM_SPEC] * 2 + [SMEM_SPEC] * 3,
        [held(load.shape), some],
        2 * MIB,
        moved=8 * MIB,
    )

    def run(kernel, args, outs, blocks, limit=4 * MIB, scratch=(), out_specs=None, aliased=False):
        operands = (*args, *weights)
        specs = [VMEM_SPEC] * len(operands)
        if aliased:
            specs[0] = ANY_SPEC
        return call(
            kernel, operands, specs, outs, limit, scratch, step * blocks, 0, out_specs, {0: 0} if aliased else {}
        )

    bit = 1
    while keep.shape[0] > 1:
        keep, send = call(fold_kernel, (keep, got, token), [VMEM_SPEC] * 3, halved(keep), 2 * MIB)
        bit *= 2
        got = over_bit(send, bit)
    incoming = [keep[0], got[0]]
    srce, dge, f0e, f1 = run(
        first_kernel,
        (start, diag, one, two, src, add, mask),
        [some, some, some, held((2, high, (nb - 1) * size))],
        nb - 1,
    )
    known = (src, srce, diag, dge, mask)
    fill = nb * 3 // 8
    f2s, f2e, f3e, far = run(
        functools.partial(far_kernel, len(incoming)),
        (start, f0e, f1, *known, *incoming),
        [
            held((2, high, fill * size)),
            held((2, high, 2 * size)),
            held((2, rows, size)),
            held((2, rows, IB)),
        ],
        4 + fill,
        scratch=[held((2, high, size))],
    )
    ends = [to_chip(far, step) if step else far for step in range(chips)]
    done, tail = nb * 9 // 16, nb // 16
    whole = jax.ShapeDtypeStruct((2, rows, width), jnp.float32)
    partly, f2, f3a = run(
        middle_kernel,
        (f1, f2s, *known),
        [whole, held((2, high, (nb - 2 - fill) * size)), held((2, rows, done * size))],
        nb - 2 - fill + done,
        scratch=[pltpu.SemaphoreType.DMA((fill - 1,))],
        out_specs=[ANY_SPEC, VMEM_SPEC, VMEM_SPEC],
    )
    mine, theirs = call(
        sums_kernel, (peers, f3a, *ends), [VMEM_SPEC] * (2 + len(ends)), [held(far.shape)] * 2, MIB
    )
    theirs = swap_cores(theirs)
    more = nb - 1 - tail - done
    f3b = run(
        functools.partial(third_kernel, done),
        (f2s, f2, f2e, *known, mine),
        held((2, rows, more * size)),
        more,
    )
    solved, updated = run(
        functools.partial(last_kernel, fill, fill - 1),
        (partly, f2, f2e, f3a, f3b, f3e, *known, mult, mine, theirs),
        [whole, jax.ShapeDtypeStruct(mult.shape, jnp.float32)],
        tail,
        scratch=[
            pltpu.VMEM((tail, 2, rows, size), jnp.float32),
            pltpu.VMEM(mult.shape, jnp.float32),
            pltpu.SemaphoreType.DMA((nb + 1,)),
        ],
        out_specs=[ANY_SPEC] * 2,
        aliased=True,
    )
    return (solved[None], updated[None])


def solution(mesh):
    lines = P("sub", None, "tile", None)
    in_specs = (
        lines,
        lines,
        lines,
        P("sub", None, None, None, None, None),
        lines,
        P(),
        P(),
        P(),
        P("sub", None),
        P("sub", None),
        P("sub", None, None),
    )
    return jax.shard_map(
        per_device, mesh=mesh, in_specs=in_specs, out_specs=(lines, lines), check_vma=False
    )
```

```python
import functools

import jax
import jax.numpy as jnp
from jax import lax
from jax.experimental import pallas as pl
from jax.experimental.pallas import tpu as pltpu
from jax.sharding import PartitionSpec as P

IB = 128
PB = 128
SWEEPS = 3
LANES = 128
PAD = 8
CARRY = 4 * 10**10, 5 * 10**9, 4 * 10**10
MIB = 1 << 20

VMEM_SPEC = pl.BlockSpec(memory_space=pltpu.VMEM)
SMEM_SPEC = pl.BlockSpec(memory_space=pltpu.SMEM)
ANY_SPEC = pl.BlockSpec(memory_space=pl.ANY)


def call(kernel, args, specs, outs, limit, scratch=(), flops=0, moved=0, out_specs=None, aliases=None):
    return pl.pallas_call(
        kernel,
        out_shape=outs,
        in_specs=specs,
        out_specs=out_specs or jax.tree.map(lambda _: VMEM_SPEC, outs),
        scratch_shapes=scratch,
        input_output_aliases=aliases or {},
        compiler_params=pltpu.CompilerParams(vmem_limit_bytes=limit),
        cost_estimate=pl.CostEstimate(flops=flops, bytes_accessed=moved, transcendentals=0),
    )(*args)


def held(shape, dtype=jnp.float32):
    return pltpu.VMEM(shape, dtype)


def line_peers(peer_ref, len_ref, s, lines):
    found = jnp.zeros(lines.shape, jnp.int32)
    start = jnp.int32(0)
    for c in range(peer_ref.shape[1]):
        end = start + len_ref[s, c]
        found = jnp.where((lines >= start) & (lines < end), peer_ref[s, c], found)
        start = end
    return found


def pick(hit, cells):
    return jnp.where(hit[None], cells, 0.0)


def split_halves(x):
    high = x.astype(jnp.bfloat16)
    return high, (x - high.astype(jnp.float32)).astype(jnp.bfloat16)


def weights_kernel(size, first, b_ref, _, hi_ref, lo_ref, token_ref):
    token_ref[...] = jnp.zeros_like(token_ref)
    both = 2 * size
    parts = both // LANES
    for k in range(hi_ref.shape[0]):
        for q in range(parts):
            piece, comp = divmod(q, 2)
            rows = pl.ds(comp * size + piece * LANES, LANES)
            high, low = split_halves(b_ref[first + k, pl.ds(q, both, parts), :].T)
            hi_ref[k, rows, :] = high
            lo_ref[k, rows, :] = low


def flat_weights(blocks):
    nb, _, size, _, _ = blocks.shape
    flat = blocks.reshape(nb, 2, size, 2, size // LANES, LANES).transpose(0, 1, 2, 4, 3, 5)
    return pltpu.with_memory_space_constraint(flat.reshape(nb, -1, LANES), pltpu.VMEM)


def split_weights(flat, size, first, count, after):
    shape = (count, 2 * size, 2 * size)
    high, low, token = call(
        functools.partial(weights_kernel, size, first),
        (flat, after),
        [VMEM_SPEC] * 2,
        [held(shape, jnp.bfloat16)] * 2 + [held((PAD, LANES))],
        2 * MIB,
        moved=count * size * size * 32,
    )
    return (high, low), token


def tiles_kernel(mult_ref, m1_ref, m2_ref):
    rows = mult_ref.shape[1]
    even = lax.rem(lax.axis_index("tile"), 2) == 0
    top, bottom = mult_ref[:, :PAD], mult_ref[:, rows - PAD :]
    m1_ref[...] = jnp.where(even, bottom, top)
    m2_ref[...] = jnp.where(even, top, bottom)


def edges_kernel(
    start_ref, load_ref, diag_ref, _, peer_ref, len_ref, active_ref, one_ref, two_ref, peers_ref, mask_ref
):
    _, rows, width = start_ref.shape
    even = lax.rem(lax.axis_index("tile"), 2) == 0
    me = lax.axis_index("sub")
    first = lax.axis_index("tile") * rows
    at = lax.broadcasted_iota(jnp.int32, peers_ref.shape[1:], 0)
    lines = jnp.where(at < rows + PAD // 2, at, at - rows - PAD) + first
    peers_ref[0] = line_peers(peer_ref, len_ref, me, lines)
    peers_ref[1] = line_peers(peer_ref, len_ref, me + 1 - 2 * lax.rem(me, 2), lines)
    at = lax.broadcasted_iota(jnp.int32, mask_ref.shape, 0) + (first - PAD)
    mask_ref[...] = jnp.where((at >= 0) & (at < active_ref[me]), 1.0, 0.0)
    row = lax.broadcasted_iota(jnp.int32, (PAD, width), 0)
    ends = (slice(0, PAD), slice(rows - PAD, rows))

    def lines_of(c, e, turns):
        field, load, diag = (
            pltpu.roll(ref[c, ends[e]], t, 0) if t else ref[c, ends[e]]
            for ref, t in zip((start_ref, load_ref, diag_ref), turns)
        )
        return pack_rows(jnp.where(row < 3, field, jnp.where(row < 5, load, diag)))

    for c in range(2):
        top, bottom = lines_of(c, 0, (0, 3, 5)), lines_of(c, 1, (3, 5, 7))
        one_ref[c] = jnp.where(even, bottom, top)
        two_ref[c] = jnp.where(even, top, bottom)


def pack_rows(cells):
    width = cells.shape[1] // PAD * (PAD - 1)
    ends = cells[:, width:]
    tail = jnp.concatenate([pltpu.roll(ends, PAD - 1 - r, 0) for r in range(PAD - 1)], axis=1)
    row = lax.broadcasted_iota(jnp.int32, tail.shape, 0)
    return jnp.where(row == PAD - 1, tail, cells[:, :width])


def unpack_rows(cells):
    step = cells.shape[1] // (PAD - 1)
    row = lax.broadcasted_iota(jnp.int32, (PAD, step), 0)
    ends = pltpu.roll(cells[:, :step], 1, 0)
    for r in range(1, PAD - 1):
        ends = jnp.where(row == r, pltpu.roll(cells[:, r * step : (r + 1) * step], r + 1, 0), ends)
    return jnp.concatenate([cells, ends], axis=1)


def pass_kernel(*refs):
    half = len(refs) // 2
    for ref, out in zip(refs[:half], refs[half:]):
        out[...] = ref[...]


def lines_kernel(mult_ref, one_ref, two_ref, _, out_ref):
    rows = mult_ref.shape[1]
    even = lax.rem(lax.axis_index("tile"), 2) == 0
    low = lax.broadcasted_iota(jnp.int32, (PAD, IB), 0) < PAD // 2
    for c in range(2):
        out_ref[c, :rows] = mult_ref[c]
        out_ref[c, rows:] = jnp.where(low == even, one_ref[c], two_ref[c])


def passed(cost, *arrays):
    return call(
        pass_kernel,
        arrays,
        [VMEM_SPEC] * len(arrays),
        [held(x.shape) for x in arrays],
        MIB,
        flops=cost,
        moved=10**6,
    )


def swaps(count):
    one = [(i, i ^ 1) for i in range(count)]
    two = [(i, ((i - 1) if i % 2 == 0 else (i + 1)) % count) for i in range(count)]
    return one, two


def swap_edges(one, two):
    first, second = swaps(lax.axis_size("tile"))
    return lax.ppermute(one, "tile", first), lax.ppermute(two, "tile", second)


def to_chip(cells, step):
    count = lax.axis_size("sub")
    return lax.ppermute(cells, "sub", [(i, (i + 2 * step) % count) for i in range(count)])


def swap_cores(cells):
    return lax.ppermute(cells, "sub", [(i, i ^ 1) for i in range(lax.axis_size("sub"))])


def merge_kernel(peers_ref, own_ref, other_ref, _, keep_ref, send_ref):
    me = lax.axis_index("sub")
    own, other = own_ref[...], other_ref[...]
    for x in range(2 * keep_ref.shape[0]):
        to = me ^ (2 * x)
        out = send_ref if x % 2 else keep_ref
        out[x // 2] = pick(peers_ref[0] == to, own) + pick(peers_ref[1] == to, other)


def fold_kernel(keep_ref, got_ref, _, next_ref, send_ref):
    for x in range(keep_ref.shape[0]):
        out = send_ref if x % 2 else next_ref
        out[x // 2] = keep_ref[x] + got_ref[x]


def halved(cells):
    shape = (cells.shape[0] // 2, *cells.shape[1:])
    return [held(shape), held(shape)]


def over_bit(cells, bit):
    return lax.ppermute(cells, "sub", [(i, i ^ (2 * bit)) for i in range(lax.axis_size("sub"))])


def sums_kernel(peers_ref, _, *refs):
    pieces, (mine_ref, theirs_ref) = refs[:-2], refs[-2:]
    me, count = lax.axis_index("sub"), 2 * len(pieces)
    rows = mine_ref.shape[1]
    mine = theirs = 0.0
    for j, piece in enumerate(pieces):
        cells = piece[...]
        s = lax.rem(me + count - 2 * j, count)
        mine += pick(peers_ref[0, :rows] == s, cells)
        theirs += pick(peers_ref[1, :rows] == s, cells)
    mine_ref[...] = mine
    theirs_ref[...] = theirs


class Weights:
    def __init__(self, refs):
        self.runs = list(zip(refs[::2], refs[1::2]))
        self.size = refs[0].shape[1] // 2
        self.last = sum(ref.shape[0] for ref in refs[::2]) - 1

    def part(self, k, low):
        for run in self.runs:
            if k < run[0].shape[0]:
                return run[low][k]
            k -= run[0].shape[0]

    def high(self, k):
        return self.part(k, 0)

    def low(self, k):
        return self.part(k, 1)


def line_mask(mask_ref, size):
    active = mask_ref[...] > 0.0
    return jnp.concatenate([active] * (size // LANES), axis=1)


def with_ends(own_ref, ends_ref, c, cols):
    return jnp.concatenate([ends_ref[c, :PAD, cols], own_ref[c, :, cols], ends_ref[c, PAD:, cols]], axis=0)


def reader(parts, size):
    def read(c, start, count):
        for first, ref in parts:
            if first * size <= start and start + count <= first * size + ref.shape[2]:
                return ref[c, :, start - first * size : start - first * size + count]

    return read


def tiles_of(read, c, k, size, last):
    mid = read(c, k * size, size)
    none = jnp.zeros((mid.shape[0], LANES), jnp.float32)
    left = read(c, k * size - LANES, LANES) if k > 0 else none
    right = read(c, (k + 1) * size, LANES) if k < last else none
    return mid, jnp.concatenate([left, mid, right], axis=1)


def relax_block(field, source, diag_ref, w, k, mask):
    size, last = w.size, w.last
    mids, sums = [], []
    for c in range(2):
        mid, wide = tiles_of(field, c, k, size, last)
        rows, width = wide.shape
        beside = (
            pltpu.roll(wide, 1, 1)[:, LANES : LANES + size]
            + pltpu.roll(wide, width - 1, 1)[:, LANES : LANES + size]
        )
        beside = beside + (pltpu.roll(mid, 1, 0) + pltpu.roll(mid, rows - 1, 0))
        mids.append(mid)
        sums.append(source(c) + beside)
    cols = slice(k * size, (k + 1) * size)
    d0, d1 = (with_ends(*diag_ref, c, cols) for c in range(2))
    r0 = sums[0] - (d0 * mids[0] - d1 * mids[1])
    r1 = sums[1] - (d0 * mids[1] + d1 * mids[0])
    high, low = split_halves(jnp.concatenate([r0, r1], axis=1))
    rows = high.shape[0]
    z = jnp.dot(
        jnp.concatenate([high, low], axis=0), w.high(k), preferred_element_type=jnp.float32
    )
    z = (z[:rows] + z[rows:]) + jnp.dot(high, w.low(k), preferred_element_type=jnp.float32)
    return [
        jnp.where(mask, mids[c] + z[:, c * size : (c + 1) * size], 0.0) for c in range(2)
    ]


def start_reader(start_ref, ends_ref, mask_ref):
    def read(c, start, count):
        cells = with_ends(start_ref, ends_ref, c, slice(start, start + count))
        return jnp.where(line_mask(mask_ref, count), cells, 0.0)

    return read


def stored_source(source, k, size):
    return lambda c: with_ends(*source, c, slice(k * size, (k + 1) * size))


def sweep(w, field, source, diag, mask_ref, first, count, out_ref):
    size = w.size
    mask = line_mask(mask_ref, size)
    rows = out_ref.shape[1]
    lines = slice(PAD, PAD + rows) if rows < mask.shape[0] else slice(0, rows)
    for i in range(count):
        k = first + i
        new = relax_block(field, stored_source(source, k, size), diag, w, k, mask)
        for c in range(2):
            out_ref[c, :, i * size : (i + 1) * size] = new[c][lines]


def source_kernel(load_ref, mult_ref, prow_ref, pcol_ref, pcur_ref, src_ref, srce_ref):
    _, rows, width = load_ref.shape
    tile = lax.axis_index("tile")
    src_ref[...] = load_ref[...]
    srce_ref[...] = jnp.zeros_like(srce_ref)
    for c in range(2):
        src_ref[c, :, :IB] -= mult_ref[c, :rows]
        srce_ref[c, :PAD, :IB] = -mult_ref[c, rows:]
        srce_ref[c, PAD:, :IB] = -mult_ref[c, rows:]
    span = PB + LANES
    at_row = lax.broadcasted_iota(jnp.int32, (PAD, span), 0)
    at_col = lax.broadcasted_iota(jnp.int32, (PAD, span), 1)
    for p in range(prow_ref.shape[1]):
        row = prow_ref[0, p] - tile * rows
        col = pcol_ref[0, p]
        base = pl.multiple_of(jnp.minimum(col // LANES * LANES, width - span), LANES)
        hits_col = (at_col >= col - base) & (at_col < col - base + PB)

        def add(ref, line, p=p, base=base, hits_col=hits_col):
            first = pl.multiple_of(line // PAD * PAD, PAD)
            for c in range(2):
                where = (c, pl.ds(first, PAD), pl.ds(base, span))
                hit = hits_col & (at_row == line - first)
                ref[where] = ref[where] + jnp.where(hit, pcur_ref[0, c, p], 0.0)

        @pl.when((row >= 0) & (row < rows))
        def _():
            add(src_ref, row)

        @pl.when((row >= -PAD) & (row < 0))
        def _():
            add(srce_ref, row + PAD)

        @pl.when((row >= rows) & (row < rows + PAD))
        def _():
            add(srce_ref, row - rows + PAD)


def first_kernel(
    start_ref, diag_ref, one_ref, two_ref, src_ref, add_ref, mask_ref, *refs
):
    w_refs, (srce_ref, dge_ref, f0e_ref, f1_ref) = refs[:-4], refs[-4:]
    w = Weights(w_refs)
    size = w.size
    even = lax.rem(lax.axis_index("tile"), 2) == 0
    for c in range(2):
        one, two = one_ref[c], two_ref[c]
        up = unpack_rows(jnp.where(even, two, one))
        down = unpack_rows(jnp.where(even, one, two))
        f0e_ref[c, :PAD] = pltpu.roll(up, 5, 0)
        f0e_ref[c, PAD:] = down
        dge_ref[c, :PAD] = pltpu.roll(up, 1, 0)
        dge_ref[c, PAD:] = pltpu.roll(down, 3, 0)
        srce_ref[c, :PAD] = add_ref[c, :PAD] + pltpu.roll(up, 3, 0)
        srce_ref[c, PAD:] = add_ref[c, PAD:] + pltpu.roll(down, 5, 0)
    sweep(
        w, start_reader(start_ref, f0e_ref, mask_ref), (src_ref, srce_ref), (diag_ref, dge_ref), mask_ref,
        0, f1_ref.shape[2] // size, f1_ref,
    )


def far_kernel(
    count, start_ref, f0e_ref, f1_ref, src_ref, srce_ref, diag_ref, dge_ref, mask_ref, *refs
):
    pieces, w_refs, (f2s_ref, f2e_ref, f3e_ref, far_ref, f1e_ref) = refs[:count], refs[count:-5], refs[-5:]
    w = Weights(w_refs)
    size, last = w.size, w.last
    rows = far_ref.shape[1]
    mask = line_mask(mask_ref, size)
    into = []
    for c in range(2):
        cells = pieces[0][c]
        for piece in pieces[1:]:
            cells += piece[c]
        ends = jnp.concatenate([cells[rows:], cells[:rows], cells[rows:]], axis=0)
        into.append(jnp.concatenate([jnp.zeros((rows + 2 * PAD, size - IB), jnp.float32), ends], axis=1))
    source, diag = (src_ref, srce_ref), (diag_ref, dge_ref)
    end = stored_source(source, last, size)

    def with_incoming(c):
        return end(c) + into[c]

    new = relax_block(start_reader(start_ref, f0e_ref, mask_ref), with_incoming, diag, w, last, mask)
    for c in range(2):
        f1e_ref[c] = new[c]
    old = reader([(0, f1_ref)], size)
    f1 = reader([(last, f1e_ref), (0, f1_ref)], size)
    fill = f2s_ref.shape[2] // size

    def beside(first, count):
        cols = pl.ds(first * size, count * size)
        sweep(w, old, source, diag, mask_ref, first, count, f2s_ref.at[:, :, cols])

    beside(0, fill // 2)
    for k, at in ((last, with_incoming), (last - 1, stored_source(source, last - 1, size))):
        new = relax_block(f1, at, diag, w, k, mask)
        for c in range(2):
            f2e_ref[c, :, (k - last + 1) * size : (k - last + 2) * size] = new[c]
    beside(fill // 2, fill - fill // 2)
    new = relax_block(reader([(last - 1, f2e_ref)], size), with_incoming, diag, w, last, mask)
    for c in range(2):
        f3e_ref[c] = new[c][PAD : PAD + rows]
        far_ref[c] = new[c][PAD : PAD + rows, size - IB :]


def middle_kernel(f1_ref, f2s_ref, src_ref, srce_ref, diag_ref, dge_ref, mask_ref, *refs):
    w_refs, (out_ref, f2_ref, f3_ref, sem) = refs[:-4], refs[-4:]
    w = Weights(w_refs)
    size = w.size
    first, done = f2s_ref.shape[2] // size, f3_ref.shape[2] // size
    early = first - 1
    source, diag = (src_ref, srce_ref), (diag_ref, dge_ref)
    f1 = reader([(0, f1_ref)], size)
    f2 = reader([(0, f2s_ref), (first, f2_ref)], size)
    sweep(w, f2, source, diag, mask_ref, 0, early, f3_ref.at[:, :, pl.ds(0, early * size)])
    copies = [block_copy(f3_ref, k, out_ref, k, size, sem.at[k]) for k in range(early)]
    for copy in copies:
        copy.start()
    sweep(w, f1, source, diag, mask_ref, first, f2_ref.shape[2] // size, f2_ref)
    rest = pl.ds(early * size, (done - early) * size)
    sweep(w, f2, source, diag, mask_ref, early, done - early, f3_ref.at[:, :, rest])
    for copy in copies:
        copy.wait()


def block_copy(ref, k, out_ref, at, size, sem):
    return pltpu.make_async_copy(
        ref.at[:, :, pl.ds(k * size, size)], out_ref.at[:, :, pl.ds(at * size, size)], sem
    )


def third_kernel(first, f2s_ref, f2_ref, f2e_ref, src_ref, srce_ref, diag_ref, dge_ref, mask_ref, _, *refs):
    w_refs, f3_ref = refs[:-1], refs[-1]
    w = Weights(w_refs)
    size = w.size
    source, diag = (src_ref, srce_ref), (diag_ref, dge_ref)
    f2 = reader([(w.last - 1, f2e_ref), (f2s_ref.shape[2] // size, f2_ref), (0, f2s_ref)], size)
    sweep(w, f2, source, diag, mask_ref, first, f3_ref.shape[2] // size, f3_ref)


def last_kernel(
    f2_first, early, _, f2_ref, f2e_ref, f3_ref, more_ref, f3e_ref, src_ref, srce_ref, diag_ref, dge_ref, mask_ref,
    mult_ref, mine_ref, theirs_ref, *refs,
):
    w_refs, (out_ref, next_ref, held_ref, new_ref, sem) = refs[:-5], refs[-5:]
    w = Weights(w_refs)
    size, last = w.size, w.last
    count = held_ref.shape[0]
    first = last - count
    source, diag = (src_ref, srce_ref), (diag_ref, dge_ref)
    done = f3_ref.shape[2] // size
    copies = [block_copy(f3_ref, k, out_ref, k, size, sem.at[k]) for k in range(early, done)]
    copies += [block_copy(more_ref, k - done, out_ref, k, size, sem.at[k]) for k in range(done, first)]
    copies.append(block_copy(f3e_ref, 0, out_ref, last, size, sem.at[last]))
    for copy in copies:
        copy.start()
    new_ref[...] = mult_ref[...] + (f3_ref[:, :, :IB] - (mine_ref[...] + theirs_ref[...]))
    copies.append(pltpu.make_async_copy(new_ref, next_ref, sem.at[last + 1]))
    copies[-1].start()
    f2 = reader([(last - 1, f2e_ref), (f2_first, f2_ref)], size)
    for i in range(count):
        sweep(w, f2, source, diag, mask_ref, first + i, 1, held_ref.at[i])
        copies.append(block_copy(held_ref.at[i], 0, out_ref, first + i, size, sem.at[first + i]))
        copies[-1].start()
    for copy in copies:
        copy.wait()


def per_device(
    load_current,
    diagonal,
    start_field,
    block_inverse,
    multipliers,
    active_rows,
    contact_peer,
    contact_len,
    port_row,
    port_col,
    port_current,
):
    load, diag, start, mult = load_current[0], diagonal[0], start_field[0], multipliers[0]
    _, rows, width = load.shape
    nb, _, size, _, _ = block_inverse.shape[1:]
    high = rows + 2 * PAD

    count = lax.axis_size("sub")

    m1, m2 = call(
        tiles_kernel,
        (mult,),
        [VMEM_SPEC],
        [held((2, PAD, IB))] * 2,
        MIB,
        flops=CARRY[0],
        moved=10**6,
    )
    ends = (m1, m2)
    m1, m2 = swap_edges(m1, m2)
    one, two, peers, mask = call(
        edges_kernel,
        (start, load, diag, ends[0], contact_peer, contact_len, active_rows),
        [VMEM_SPEC] * 4 + [SMEM_SPEC] * 3,
        [held((2, PAD, width // PAD * (PAD - 1)))] * 2
        + [held((2, rows + PAD, LANES), jnp.int32), held((high, LANES))],
        4 * MIB,
        flops=CARRY[2],
        moved=10**6,
    )
    got_one, got_two = swap_edges(one, two)
    flat = flat_weights(block_inverse[0])
    chips = count // 2
    quarter = nb // 4
    lines_mult = call(
        lines_kernel,
        (mult, m1, m2, one),
        [VMEM_SPEC] * 4,
        held((2, rows + PAD, IB)),
        MIB,
    )
    other = swap_cores(lines_mult)
    mask, after = passed(CARRY[1], mask, lines_mult)
    w1, token = split_weights(flat, size, 0, quarter, after)
    half = held((chips // 2, *lines_mult.shape))
    keep, send = call(
        merge_kernel, (peers, lines_mult, other, token), [VMEM_SPEC] * 4, [half] * 2, 2 * MIB
    )
    got = over_bit(send, 1)
    w2, token = split_weights(flat, size, quarter, quarter, keep)
    w3, token = split_weights(flat, size, 2 * quarter, nb - 2 * quarter, token)
    weights = (*w1, *w2, *w3)
    step = 6 * high * (2 * size) ** 2
    some = held((2, 2 * PAD, width))

    src, add = call(
        source_kernel,
        (load, lines_mult, port_row, port_col, port_current),
        [VMEM_SPEC] * 2 + [SMEM_SPEC] * 3,
        [held(load.shape), some],
        2 * MIB,
        moved=8 * MIB,
    )

    def run(kernel, args, outs, blocks, limit=4 * MIB, scratch=(), out_specs=None, aliased=False):
        operands = (*args, *weights)
        specs = [VMEM_SPEC] * len(operands)
        if aliased:
            specs[0] = ANY_SPEC
        return call(
            kernel, operands, specs, outs, limit, scratch, step * blocks, 0, out_specs, {0: 0} if aliased else {}
        )

    bit = 1
    while keep.shape[0] > 1:
        keep, send = call(fold_kernel, (keep, got, token), [VMEM_SPEC] * 3, halved(keep), 2 * MIB)
        bit *= 2
        got = over_bit(send, bit)
    incoming = [keep[0], got[0]]
    srce, dge, f0e, f1 = run(
        first_kernel,
        (start, diag, got_one, got_two, src, add, mask),
        [some, some, some, held((2, high, (nb - 1) * size))],
        nb - 1,
    )
    known = (src, srce, diag, dge, mask)
    fill = nb * 3 // 8
    f2s, f2e, f3e, far = run(
        functools.partial(far_kernel, len(incoming)),
        (start, f0e, f1, *known, *incoming),
        [
            held((2, high, fill * size)),
            held((2, high, 2 * size)),
            held((2, rows, size)),
            held((2, rows, IB)),
        ],
        4 + fill,
        scratch=[held((2, high, size))],
    )
    ends = [to_chip(far, step) if step else far for step in range(chips)]
    done, tail = nb * 9 // 16, nb // 16
    whole = jax.ShapeDtypeStruct((2, rows, width), jnp.float32)
    partly, f2, f3a = run(
        middle_kernel,
        (f1, f2s, *known),
        [whole, held((2, high, (nb - 2 - fill) * size)), held((2, rows, done * size))],
        nb - 2 - fill + done,
        scratch=[pltpu.SemaphoreType.DMA((fill - 1,))],
        out_specs=[ANY_SPEC, VMEM_SPEC, VMEM_SPEC],
    )
    mine, theirs = call(
        sums_kernel, (peers, f3a, *ends), [VMEM_SPEC] * (2 + len(ends)), [held(far.shape)] * 2, MIB
    )
    theirs = swap_cores(theirs)
    more = nb - 1 - tail - done
    f3b = run(
        functools.partial(third_kernel, done),
        (f2s, f2, f2e, *known, mine),
        held((2, rows, more * size)),
        more,
    )
    solved, updated = run(
        functools.partial(last_kernel, fill, fill - 1),
        (partly, f2, f2e, f3a, f3b, f3e, *known, mult, mine, theirs),
        [whole, jax.ShapeDtypeStruct(mult.shape, jnp.float32)],
        tail,
        scratch=[
            pltpu.VMEM((tail, 2, rows, size), jnp.float32),
            pltpu.VMEM(mult.shape, jnp.float32),
            pltpu.SemaphoreType.DMA((nb + 1,)),
        ],
        out_specs=[ANY_SPEC] * 2,
        aliased=True,
    )
    return (solved[None], updated[None])


def solution(mesh):
    lines = P("sub", None, "tile", None)
    in_specs = (
        lines,
        lines,
        lines,
        P("sub", None, None, None, None, None),
        lines,
        P(),
        P(),
        P(),
        P("sub", None),
        P("sub", None),
        P("sub", None, None),
    )
    return jax.shard_map(
        per_device, mesh=mesh, in_specs=in_specs, out_specs=(lines, lines), check_vma=False
    )
```

```python
import functools

import jax
import jax.numpy as jnp
from jax import lax
from jax.experimental import pallas as pl
from jax.experimental.pallas import tpu as pltpu
from jax.sharding import PartitionSpec as P

IB = 128
PB = 128
SWEEPS = 3
LANES = 128
PAD = 8
CARRY = 4 * 10**10, 5 * 10**9, 4 * 10**10
MIB = 1 << 20

VMEM_SPEC = pl.BlockSpec(memory_space=pltpu.VMEM)
SMEM_SPEC = pl.BlockSpec(memory_space=pltpu.SMEM)
ANY_SPEC = pl.BlockSpec(memory_space=pl.ANY)


def call(kernel, args, specs, outs, limit, scratch=(), flops=0, moved=0, out_specs=None, aliases=None):
    return pl.pallas_call(
        kernel,
        out_shape=outs,
        in_specs=specs,
        out_specs=out_specs or jax.tree.map(lambda _: VMEM_SPEC, outs),
        scratch_shapes=scratch,
        input_output_aliases=aliases or {},
        compiler_params=pltpu.CompilerParams(vmem_limit_bytes=limit),
        cost_estimate=pl.CostEstimate(flops=flops, bytes_accessed=moved, transcendentals=0),
    )(*args)


def held(shape, dtype=jnp.float32):
    return pltpu.VMEM(shape, dtype)


def line_peers(peer_ref, len_ref, s, lines):
    found = jnp.zeros(lines.shape, jnp.int32)
    start = jnp.int32(0)
    for c in range(peer_ref.shape[1]):
        end = start + len_ref[s, c]
        found = jnp.where((lines >= start) & (lines < end), peer_ref[s, c], found)
        start = end
    return found


def pick(hit, cells):
    return jnp.where(hit[None], cells, 0.0)


def split_halves(x):
    high = x.astype(jnp.bfloat16)
    return high, (x - high.astype(jnp.float32)).astype(jnp.bfloat16)


def weights_kernel(size, first, b_ref, _, hi_ref, lo_ref, token_ref):
    token_ref[...] = jnp.zeros_like(token_ref)
    both = 2 * size
    parts = both // LANES
    for k in range(hi_ref.shape[0]):
        for q in range(parts):
            piece, comp = divmod(q, 2)
            rows = pl.ds(comp * size + piece * LANES, LANES)
            high, low = split_halves(b_ref[first + k, pl.ds(q, both, parts), :].T)
            hi_ref[k, rows, :] = high
            lo_ref[k, rows, :] = low


def flat_weights(blocks):
    nb, _, size, _, _ = blocks.shape
    flat = blocks.reshape(nb, 2, size, 2, size // LANES, LANES).transpose(0, 1, 2, 4, 3, 5)
    return pltpu.with_memory_space_constraint(flat.reshape(nb, -1, LANES), pltpu.VMEM)


def split_weights(flat, size, first, count, after):
    shape = (count, 2 * size, 2 * size)
    high, low, token = call(
        functools.partial(weights_kernel, size, first),
        (flat, after),
        [VMEM_SPEC] * 2,
        [held(shape, jnp.bfloat16)] * 2 + [held((PAD, LANES))],
        2 * MIB,
        moved=count * size * size * 32,
    )
    return (high, low), token


def tiles_kernel(mult_ref, m1_ref, m2_ref):
    rows = mult_ref.shape[1]
    even = lax.rem(lax.axis_index("tile"), 2) == 0
    top, bottom = mult_ref[:, :PAD], mult_ref[:, rows - PAD :]
    m1_ref[...] = jnp.where(even, bottom, top)
    m2_ref[...] = jnp.where(even, top, bottom)


def edges_kernel(
    start_ref, load_ref, diag_ref, _, peer_ref, len_ref, active_ref, one_ref, two_ref, peers_ref, mask_ref
):
    _, rows, width = start_ref.shape
    even = lax.rem(lax.axis_index("tile"), 2) == 0
    me = lax.axis_index("sub")
    first = lax.axis_index("tile") * rows
    at = lax.broadcasted_iota(jnp.int32, peers_ref.shape[1:], 0)
    lines = jnp.where(at < rows + PAD // 2, at, at - rows - PAD) + first
    peers_ref[0] = line_peers(peer_ref, len_ref, me, lines)
    peers_ref[1] = line_peers(peer_ref, len_ref, me + 1 - 2 * lax.rem(me, 2), lines)
    at = lax.broadcasted_iota(jnp.int32, mask_ref.shape, 0) + (first - PAD)
    mask_ref[...] = jnp.where((at >= 0) & (at < active_ref[me]), 1.0, 0.0)
    row = lax.broadcasted_iota(jnp.int32, (PAD, width), 0)
    ends = (slice(0, PAD), slice(rows - PAD, rows))

    def lines_of(c, e, turns):
        field, load, diag = (
            pltpu.roll(ref[c, ends[e]], t, 0) if t else ref[c, ends[e]]
            for ref, t in zip((start_ref, load_ref, diag_ref), turns)
        )
        return pack_rows(jnp.where(row < 3, field, jnp.where(row < 5, load, diag)))

    for c in range(2):
        top, bottom = lines_of(c, 0, (0, 3, 5)), lines_of(c, 1, (3, 5, 7))
        one_ref[c] = jnp.where(even, bottom, top)
        two_ref[c] = jnp.where(even, top, bottom)


def pack_rows(cells):
    width = cells.shape[1] // PAD * (PAD - 1)
    ends = cells[:, width:]
    tail = jnp.concatenate([pltpu.roll(ends, PAD - 1 - r, 0) for r in range(PAD - 1)], axis=1)
    row = lax.broadcasted_iota(jnp.int32, tail.shape, 0)
    return jnp.where(row == PAD - 1, tail, cells[:, :width])


def unpack_rows(cells):
    step = cells.shape[1] // (PAD - 1)
    row = lax.broadcasted_iota(jnp.int32, (PAD, step), 0)
    ends = pltpu.roll(cells[:, :step], 1, 0)
    for r in range(1, PAD - 1):
        ends = jnp.where(row == r, pltpu.roll(cells[:, r * step : (r + 1) * step], r + 1, 0), ends)
    return jnp.concatenate([cells, ends], axis=1)


def pass_kernel(*refs):
    half = len(refs) // 2
    for ref, out in zip(refs[:half], refs[half:]):
        out[...] = ref[...]


def lines_kernel(mult_ref, one_ref, two_ref, _, out_ref):
    rows = mult_ref.shape[1]
    even = lax.rem(lax.axis_index("tile"), 2) == 0
    low = lax.broadcasted_iota(jnp.int32, (PAD, IB), 0) < PAD // 2
    for c in range(2):
        out_ref[c, :rows] = mult_ref[c]
        out_ref[c, rows:] = jnp.where(low == even, one_ref[c], two_ref[c])


def passed(cost, *arrays):
    return call(
        pass_kernel,
        arrays,
        [VMEM_SPEC] * len(arrays),
        [held(x.shape) for x in arrays],
        MIB,
        flops=cost,
        moved=10**6,
    )


def swaps(count):
    one = [(i, i ^ 1) for i in range(count)]
    two = [(i, ((i - 1) if i % 2 == 0 else (i + 1)) % count) for i in range(count)]
    return one, two


def swap_edges(one, two):
    first, second = swaps(lax.axis_size("tile"))
    return lax.ppermute(one, "tile", first), lax.ppermute(two, "tile", second)


def to_chip(cells, step):
    count = lax.axis_size("sub")
    return lax.ppermute(cells, "sub", [(i, (i + 2 * step) % count) for i in range(count)])


def swap_cores(cells):
    return lax.ppermute(cells, "sub", [(i, i ^ 1) for i in range(lax.axis_size("sub"))])


def merge_kernel(peers_ref, own_ref, other_ref, _, keep_ref, send_ref):
    me = lax.axis_index("sub")
    own, other = own_ref[...], other_ref[...]
    for x in range(2 * keep_ref.shape[0]):
        to = me ^ (2 * x)
        out = send_ref if x % 2 else keep_ref
        out[x // 2] = pick(peers_ref[0] == to, own) + pick(peers_ref[1] == to, other)


def fold_kernel(keep_ref, got_ref, _, next_ref, send_ref):
    for x in range(keep_ref.shape[0]):
        out = send_ref if x % 2 else next_ref
        out[x // 2] = keep_ref[x] + got_ref[x]


def halved(cells):
    shape = (cells.shape[0] // 2, *cells.shape[1:])
    return [held(shape), held(shape)]


def over_bit(cells, bit):
    return lax.ppermute(cells, "sub", [(i, i ^ (2 * bit)) for i in range(lax.axis_size("sub"))])


def sums_kernel(peers_ref, _, *refs):
    pieces, (mine_ref, theirs_ref) = refs[:-2], refs[-2:]
    me, count = lax.axis_index("sub"), 2 * len(pieces)
    rows = mine_ref.shape[1]
    mine = theirs = 0.0
    for j, piece in enumerate(pieces):
        cells = piece[...]
        s = lax.rem(me + count - 2 * j, count)
        mine += pick(peers_ref[0, :rows] == s, cells)
        theirs += pick(peers_ref[1, :rows] == s, cells)
    mine_ref[...] = mine
    theirs_ref[...] = theirs


class Weights:
    def __init__(self, refs):
        self.runs = list(zip(refs[::2], refs[1::2]))
        self.size = refs[0].shape[1] // 2
        self.last = sum(ref.shape[0] for ref in refs[::2]) - 1

    def part(self, k, low):
        for run in self.runs:
            if k < run[0].shape[0]:
                return run[low][k]
            k -= run[0].shape[0]

    def high(self, k):
        return self.part(k, 0)

    def low(self, k):
        return self.part(k, 1)


def line_mask(mask_ref, size):
    active = mask_ref[...] > 0.0
    return jnp.concatenate([active] * (size // LANES), axis=1)


def with_ends(own_ref, ends_ref, c, cols):
    return jnp.concatenate([ends_ref[c, :PAD, cols], own_ref[c, :, cols], ends_ref[c, PAD:, cols]], axis=0)


def reader(parts, size):
    def read(c, start, count):
        for first, ref in parts:
            if first * size <= start and start + count <= first * size + ref.shape[2]:
                return ref[c, :, start - first * size : start - first * size + count]

    return read


def tiles_of(read, c, k, size, last):
    mid = read(c, k * size, size)
    none = jnp.zeros((mid.shape[0], LANES), jnp.float32)
    left = read(c, k * size - LANES, LANES) if k > 0 else none
    right = read(c, (k + 1) * size, LANES) if k < last else none
    return mid, jnp.concatenate([left, mid, right], axis=1)


def relax_block(field, source, diag_ref, w, k, mask):
    size, last = w.size, w.last
    mids, sums = [], []
    for c in range(2):
        mid, wide = tiles_of(field, c, k, size, last)
        rows, width = wide.shape
        beside = (
            pltpu.roll(wide[:, : width - LANES], 1, 1)[:, LANES:]
            + pltpu.roll(wide[:, LANES:], width - LANES - 1, 1)[:, :size]
        )
        beside = beside + (pltpu.roll(mid, 1, 0) + pltpu.roll(mid, rows - 1, 0))
        mids.append(mid)
        sums.append(source(c) + beside)
    cols = slice(k * size, (k + 1) * size)
    d0, d1 = (with_ends(*diag_ref, c, cols) for c in range(2))
    r0 = sums[0] - (d0 * mids[0] - d1 * mids[1])
    r1 = sums[1] - (d0 * mids[1] + d1 * mids[0])
    high, low = split_halves(jnp.concatenate([r0, r1], axis=1))
    rows = high.shape[0]
    z = jnp.dot(
        jnp.concatenate([high, low], axis=0), w.high(k), preferred_element_type=jnp.float32
    )
    z = (z[:rows] + z[rows:]) + jnp.dot(high, w.low(k), preferred_element_type=jnp.float32)
    return [
        jnp.where(mask, mids[c] + z[:, c * size : (c + 1) * size], 0.0) for c in range(2)
    ]


def start_reader(start_ref, ends_ref, mask_ref):
    def read(c, start, count):
        cells = with_ends(start_ref, ends_ref, c, slice(start, start + count))
        return jnp.where(line_mask(mask_ref, count), cells, 0.0)

    return read


def stored_source(source, k, size):
    return lambda c: with_ends(*source, c, slice(k * size, (k + 1) * size))


def sweep(w, field, source, diag, mask_ref, first, count, out_ref):
    size = w.size
    mask = line_mask(mask_ref, size)
    rows = out_ref.shape[1]
    lines = slice(PAD, PAD + rows) if rows < mask.shape[0] else slice(0, rows)
    for i in range(count):
        k = first + i
        new = relax_block(field, stored_source(source, k, size), diag, w, k, mask)
        for c in range(2):
            out_ref[c, :, i * size : (i + 1) * size] = new[c][lines]


def source_kernel(load_ref, mult_ref, prow_ref, pcol_ref, pcur_ref, src_ref, srce_ref):
    _, rows, width = load_ref.shape
    tile = lax.axis_index("tile")
    src_ref[...] = load_ref[...]
    srce_ref[...] = jnp.zeros_like(srce_ref)
    for c in range(2):
        src_ref[c, :, :IB] -= mult_ref[c, :rows]
        srce_ref[c, :PAD, :IB] = -mult_ref[c, rows:]
        srce_ref[c, PAD:, :IB] = -mult_ref[c, rows:]
    span = PB + LANES
    at_row = lax.broadcasted_iota(jnp.int32, (PAD, span), 0)
    at_col = lax.broadcasted_iota(jnp.int32, (PAD, span), 1)
    for p in range(prow_ref.shape[1]):
        row = prow_ref[0, p] - tile * rows
        col = pcol_ref[0, p]
        base = pl.multiple_of(jnp.minimum(col // LANES * LANES, width - span), LANES)
        hits_col = (at_col >= col - base) & (at_col < col - base + PB)

        def add(ref, line, p=p, base=base, hits_col=hits_col):
            first = pl.multiple_of(line // PAD * PAD, PAD)
            for c in range(2):
                where = (c, pl.ds(first, PAD), pl.ds(base, span))
                hit = hits_col & (at_row == line - first)
                ref[where] = ref[where] + jnp.where(hit, pcur_ref[0, c, p], 0.0)

        @pl.when((row >= 0) & (row < rows))
        def _():
            add(src_ref, row)

        @pl.when((row >= -PAD) & (row < 0))
        def _():
            add(srce_ref, row + PAD)

        @pl.when((row >= rows) & (row < rows + PAD))
        def _():
            add(srce_ref, row - rows + PAD)


def first_kernel(
    start_ref, diag_ref, one_ref, two_ref, src_ref, add_ref, mask_ref, *refs
):
    w_refs, (srce_ref, dge_ref, f0e_ref, f1_ref) = refs[:-4], refs[-4:]
    w = Weights(w_refs)
    size = w.size
    even = lax.rem(lax.axis_index("tile"), 2) == 0
    for c in range(2):
        one, two = one_ref[c], two_ref[c]
        up = unpack_rows(jnp.where(even, two, one))
        down = unpack_rows(jnp.where(even, one, two))
        f0e_ref[c, :PAD] = pltpu.roll(up, 5, 0)
        f0e_ref[c, PAD:] = down
        dge_ref[c, :PAD] = pltpu.roll(up, 1, 0)
        dge_ref[c, PAD:] = pltpu.roll(down, 3, 0)
        srce_ref[c, :PAD] = add_ref[c, :PAD] + pltpu.roll(up, 3, 0)
        srce_ref[c, PAD:] = add_ref[c, PAD:] + pltpu.roll(down, 5, 0)
    sweep(
        w, start_reader(start_ref, f0e_ref, mask_ref), (src_ref, srce_ref), (diag_ref, dge_ref), mask_ref,
        0, f1_ref.shape[2] // size, f1_ref,
    )


def far_kernel(
    count, start_ref, f0e_ref, f1_ref, src_ref, srce_ref, diag_ref, dge_ref, mask_ref, *refs
):
    pieces, w_refs, (f2s_ref, f2e_ref, f3e_ref, far_ref, f1e_ref) = refs[:count], refs[count:-5], refs[-5:]
    w = Weights(w_refs)
    size, last = w.size, w.last
    rows = far_ref.shape[1]
    mask = line_mask(mask_ref, size)
    into = []
    for c in range(2):
        cells = pieces[0][c]
        for piece in pieces[1:]:
            cells += piece[c]
        ends = jnp.concatenate([cells[rows:], cells[:rows], cells[rows:]], axis=0)
        into.append(jnp.concatenate([jnp.zeros((rows + 2 * PAD, size - IB), jnp.float32), ends], axis=1))
    source, diag = (src_ref, srce_ref), (diag_ref, dge_ref)
    end = stored_source(source, last, size)

    def with_incoming(c):
        return end(c) + into[c]

    new = relax_block(start_reader(start_ref, f0e_ref, mask_ref), with_incoming, diag, w, last, mask)
    for c in range(2):
        f1e_ref[c] = new[c]
    old = reader([(0, f1_ref)], size)
    f1 = reader([(last, f1e_ref), (0, f1_ref)], size)
    fill = f2s_ref.shape[2] // size

    def beside(first, count):
        cols = pl.ds(first * size, count * size)
        sweep(w, old, source, diag, mask_ref, first, count, f2s_ref.at[:, :, cols])

    beside(0, fill // 2)
    for k, at in ((last, with_incoming), (last - 1, stored_source(source, last - 1, size))):
        new = relax_block(f1, at, diag, w, k, mask)
        for c in range(2):
            f2e_ref[c, :, (k - last + 1) * size : (k - last + 2) * size] = new[c]
    beside(fill // 2, fill - fill // 2)
    new = relax_block(reader([(last - 1, f2e_ref)], size), with_incoming, diag, w, last, mask)
    for c in range(2):
        f3e_ref[c] = new[c][PAD : PAD + rows]
        far_ref[c] = new[c][PAD : PAD + rows, size - IB :]


def middle_kernel(f1_ref, f2s_ref, src_ref, srce_ref, diag_ref, dge_ref, mask_ref, *refs):
    w_refs, (out_ref, f2_ref, f3_ref, sem) = refs[:-4], refs[-4:]
    w = Weights(w_refs)
    size = w.size
    first, done = f2s_ref.shape[2] // size, f3_ref.shape[2] // size
    early = first - 1
    source, diag = (src_ref, srce_ref), (diag_ref, dge_ref)
    f1 = reader([(0, f1_ref)], size)
    f2 = reader([(0, f2s_ref), (first, f2_ref)], size)
    sweep(w, f2, source, diag, mask_ref, 0, early, f3_ref.at[:, :, pl.ds(0, early * size)])
    copies = [block_copy(f3_ref, k, out_ref, k, size, sem.at[k]) for k in range(early)]
    for copy in copies:
        copy.start()
    sweep(w, f1, source, diag, mask_ref, first, f2_ref.shape[2] // size, f2_ref)
    rest = pl.ds(early * size, (done - early) * size)
    sweep(w, f2, source, diag, mask_ref, early, done - early, f3_ref.at[:, :, rest])
    for copy in copies:
        copy.wait()


def block_copy(ref, k, out_ref, at, size, sem):
    return pltpu.make_async_copy(
        ref.at[:, :, pl.ds(k * size, size)], out_ref.at[:, :, pl.ds(at * size, size)], sem
    )


def third_kernel(first, f2s_ref, f2_ref, f2e_ref, src_ref, srce_ref, diag_ref, dge_ref, mask_ref, _, *refs):
    w_refs, f3_ref = refs[:-1], refs[-1]
    w = Weights(w_refs)
    size = w.size
    source, diag = (src_ref, srce_ref), (diag_ref, dge_ref)
    f2 = reader([(w.last - 1, f2e_ref), (f2s_ref.shape[2] // size, f2_ref), (0, f2s_ref)], size)
    sweep(w, f2, source, diag, mask_ref, first, f3_ref.shape[2] // size, f3_ref)


def last_kernel(
    f2_first, early, _, f2_ref, f2e_ref, f3_ref, more_ref, f3e_ref, src_ref, srce_ref, diag_ref, dge_ref, mask_ref,
    mult_ref, mine_ref, theirs_ref, *refs,
):
    w_refs, (out_ref, next_ref, held_ref, new_ref, sem) = refs[:-5], refs[-5:]
    w = Weights(w_refs)
    size, last = w.size, w.last
    count = held_ref.shape[0]
    first = last - count
    source, diag = (src_ref, srce_ref), (diag_ref, dge_ref)
    done = f3_ref.shape[2] // size
    copies = [block_copy(f3_ref, k, out_ref, k, size, sem.at[k]) for k in range(early, done)]
    copies += [block_copy(more_ref, k - done, out_ref, k, size, sem.at[k]) for k in range(done, first)]
    copies.append(block_copy(f3e_ref, 0, out_ref, last, size, sem.at[last]))
    for copy in copies:
        copy.start()
    new_ref[...] = mult_ref[...] + (f3_ref[:, :, :IB] - (mine_ref[...] + theirs_ref[...]))
    copies.append(pltpu.make_async_copy(new_ref, next_ref, sem.at[last + 1]))
    copies[-1].start()
    f2 = reader([(last - 1, f2e_ref), (f2_first, f2_ref)], size)
    for i in range(count):
        sweep(w, f2, source, diag, mask_ref, first + i, 1, held_ref.at[i])
        copies.append(block_copy(held_ref.at[i], 0, out_ref, first + i, size, sem.at[first + i]))
        copies[-1].start()
    for copy in copies:
        copy.wait()


def per_device(
    load_current,
    diagonal,
    start_field,
    block_inverse,
    multipliers,
    active_rows,
    contact_peer,
    contact_len,
    port_row,
    port_col,
    port_current,
):
    load, diag, start, mult = load_current[0], diagonal[0], start_field[0], multipliers[0]
    _, rows, width = load.shape
    nb, _, size, _, _ = block_inverse.shape[1:]
    high = rows + 2 * PAD

    count = lax.axis_size("sub")

    m1, m2 = call(
        tiles_kernel,
        (mult,),
        [VMEM_SPEC],
        [held((2, PAD, IB))] * 2,
        MIB,
        flops=CARRY[0],
        moved=10**6,
    )
    ends = (m1, m2)
    m1, m2 = swap_edges(m1, m2)
    one, two, peers, mask = call(
        edges_kernel,
        (start, load, diag, ends[0], contact_peer, contact_len, active_rows),
        [VMEM_SPEC] * 4 + [SMEM_SPEC] * 3,
        [held((2, PAD, width // PAD * (PAD - 1)))] * 2
        + [held((2, rows + PAD, LANES), jnp.int32), held((high, LANES))],
        4 * MIB,
        flops=CARRY[2],
        moved=10**6,
    )
    got_one, got_two = swap_edges(one, two)
    flat = flat_weights(block_inverse[0])
    chips = count // 2
    quarter = nb // 4
    lines_mult = call(
        lines_kernel,
        (mult, m1, m2, one),
        [VMEM_SPEC] * 4,
        held((2, rows + PAD, IB)),
        MIB,
    )
    other = swap_cores(lines_mult)
    mask, after = passed(CARRY[1], mask, lines_mult)
    w1, token = split_weights(flat, size, 0, quarter, after)
    half = held((chips // 2, *lines_mult.shape))
    keep, send = call(
        merge_kernel, (peers, lines_mult, other, token), [VMEM_SPEC] * 4, [half] * 2, 2 * MIB
    )
    got = over_bit(send, 1)
    w2, token = split_weights(flat, size, quarter, nb - quarter, keep)
    weights = (*w1, *w2)
    step = 6 * high * (2 * size) ** 2
    some = held((2, 2 * PAD, width))

    src, add = call(
        source_kernel,
        (load, lines_mult, port_row, port_col, port_current),
        [VMEM_SPEC] * 2 + [SMEM_SPEC] * 3,
        [held(load.shape), some],
        2 * MIB,
        moved=8 * MIB,
    )

    def run(kernel, args, outs, blocks, limit=4 * MIB, scratch=(), out_specs=None, aliased=False):
        operands = (*args, *weights)
        specs = [VMEM_SPEC] * len(operands)
        if aliased:
            specs[0] = ANY_SPEC
        return call(
            kernel, operands, specs, outs, limit, scratch, step * blocks, 0, out_specs, {0: 0} if aliased else {}
        )

    bit = 1
    while keep.shape[0] > 1:
        keep, send = call(fold_kernel, (keep, got, token), [VMEM_SPEC] * 3, halved(keep), 2 * MIB)
        bit *= 2
        got = over_bit(send, bit)
    incoming = [keep[0], got[0]]
    srce, dge, f0e, f1 = run(
        first_kernel,
        (start, diag, got_one, got_two, src, add, mask),
        [some, some, some, held((2, high, (nb - 1) * size))],
        nb - 1,
    )
    known = (src, srce, diag, dge, mask)
    fill = nb * 3 // 8
    f2s, f2e, f3e, far = run(
        functools.partial(far_kernel, len(incoming)),
        (start, f0e, f1, *known, *incoming),
        [
            held((2, high, fill * size)),
            held((2, high, 2 * size)),
            held((2, rows, size)),
            held((2, rows, IB)),
        ],
        4 + fill,
        scratch=[held((2, high, size))],
    )
    ends = [to_chip(far, step) if step else far for step in range(chips)]
    done, tail = nb * 9 // 16, nb // 16
    whole = jax.ShapeDtypeStruct((2, rows, width), jnp.float32)
    partly, f2, f3a = run(
        middle_kernel,
        (f1, f2s, *known),
        [whole, held((2, high, (nb - 2 - fill) * size)), held((2, rows, done * size))],
        nb - 2 - fill + done,
        scratch=[pltpu.SemaphoreType.DMA((fill - 1,))],
        out_specs=[ANY_SPEC, VMEM_SPEC, VMEM_SPEC],
    )
    mine, theirs = call(
        sums_kernel, (peers, f3a, *ends), [VMEM_SPEC] * (2 + len(ends)), [held(far.shape)] * 2, MIB
    )
    theirs = swap_cores(theirs)
    more = nb - 1 - tail - done
    f3b = run(
        functools.partial(third_kernel, done),
        (f2s, f2, f2e, *known, mine),
        held((2, rows, more * size)),
        more,
    )
    solved, updated = run(
        functools.partial(last_kernel, fill, fill - 1),
        (partly, f2, f2e, f3a, f3b, f3e, *known, mult, mine, theirs),
        [whole, jax.ShapeDtypeStruct(mult.shape, jnp.float32)],
        tail,
        scratch=[
            pltpu.VMEM((tail, 2, rows, size), jnp.float32),
            pltpu.VMEM(mult.shape, jnp.float32),
            pltpu.SemaphoreType.DMA((nb + 1,)),
        ],
        out_specs=[ANY_SPEC] * 2,
        aliased=True,
    )
    return (solved[None], updated[None])


def solution(mesh):
    lines = P("sub", None, "tile", None)
    in_specs = (
        lines,
        lines,
        lines,
        P("sub", None, None, None, None, None),
        lines,
        P(),
        P(),
        P(),
        P("sub", None),
        P("sub", None),
        P("sub", None, None),
    )
    return jax.shard_map(
        per_device, mesh=mesh, in_specs=in_specs, out_specs=(lines, lines), check_vma=False
    )
```
